128 devices in a mesh: fsdp: 16 (over z, x_hi, core), context: 4 (over y), tensor: 2 (over x_lo).
Axes of the slice: x: 4 (x_hi: 2, x_lo: 2; x = x_hi * 2 + x_lo), y: 4, z: 4, core: 2. Of those that a mesh axis runs over, the one named last changes fastest.
Arguments:
- tokens: bfloat16 [16384, 1536], P(('fsdp', 'context')), may hold values from -6 to 6
- cotangent: bfloat16 [16384, 1536], P(('fsdp', 'context')), may hold values from -6 to 6
- lengths: int32 [16, 3], P('fsdp'), may hold values from 1 to 896, 1024 in all within a row
- gain_attn: bfloat16 [1536], P('fsdp'), may hold values from 0.5 to 1.5
- w_query: bfloat16 [1536, 1536], P('fsdp', 'tensor'), may hold values from -0.15625 to 0.15625
- b_query: bfloat16 [1536], P('tensor'), may hold values from -3 to 3
- w_key: bfloat16 [1536, 256], P('fsdp', 'tensor'), may hold values from -0.15625 to 0.15625
- b_key: bfloat16 [256], P('tensor'), may hold values from -3 to 3
- w_value: bfloat16 [1536, 256], P('fsdp', 'tensor'), may hold values from -0.15625 to 0.15625
- b_value: bfloat16 [256], P('tensor'), may hold values from -3 to 3
- w_out: bfloat16 [1536, 1536], P('tensor', 'fsdp'), may hold values from -1.25 to 1.25
- gain_mlp: bfloat16 [1536], P('fsdp'), may hold values from 0.5 to 1.5
- w_gate: bfloat16 [1536, 8960], P('fsdp', 'tensor'), may hold values from -0.15625 to 0.15625
- w_up: bfloat16 [1536, 8960], P('fsdp', 'tensor'), may hold values from -0.15625 to 0.15625
- w_down: bfloat16 [8960, 1536], P('tensor', 'fsdp'), may hold values from -0.0625 to 0.0625
Outputs:
- result: bfloat16 [16384, 1536], P(('fsdp', 'context'))
- grad_tokens: float32 [16384, 1536], P(('fsdp', 'context'))
- grad_gain_attn: float32 [1536], P('fsdp')
- grad_w_query: float32 [1536, 1536], P('fsdp', 'tensor')
- grad_b_query: float32 [1536], P('tensor')
- grad_w_key: float32 [1536, 256], P('fsdp', 'tensor')
- grad_b_key: float32 [256], P('tensor')
- grad_w_value: float32 [1536, 256], P('fsdp', 'tensor')
- grad_b_value: float32 [256], P('tensor')
- grad_w_out: float32 [1536, 1536], P('tensor', 'fsdp')
- grad_gain_mlp: float32 [1536], P('fsdp')
- grad_w_gate: float32 [1536, 8960], P('fsdp', 'tensor')
- grad_w_up: float32 [1536, 8960], P('fsdp', 'tensor')
- grad_w_down: float32 [8960, 1536], P('tensor', 'fsdp')
The draws below stay inside these ranges and needn't reach their ends.
Inputs may be any that keep to these rules, and one draw needn't show every extreme that they name: Each row holds the lengths of the 3 sequences packed in order into one group of 1024 tokens; they sum to 1024, and the longest is exactly 896.
All inputs are finite; a program needn't handle non-finite values.
Results may differ from the reference program's by a relative error of at most 0.024.
Values may be sent and summed in bfloat16 or wider, within the bound.
A program may use at most 320 MiB of HBM per device.

```python
import math
import jax
import jax.numpy as jnp
import numpy as np
from jax import lax

D = 1536
QH = 12
KVH = 2
HD = 128
FF = 8960
SEQS = 3
GROUPS = 16
GROUP = 1024
LONGEST = 896
TOKENS = 16384


def levels(rng, extent, shards, low, high):
    def one(dim, blocks):
        steps = jax.random.uniform(jax.random.fold_in(jax.random.fold_in(rng, 6), dim), (blocks,), jnp.float32, low / len(shards), high / len(shards))
        return jnp.repeat(jnp.exp(steps), extent[dim] // blocks).reshape((-1,) + (1,) * (len(extent) - dim - 1))

    gain = one(*shards[0])
    for cut in shards[1:]:
        gain = gain * one(*cut)
    return gain


def split_up(count, total, reach, skew):
    loads = [(1 << 20) // math.isqrt(standing ** skew) + 1 for standing in range(2, count + 1)]
    rest, holding = total - reach - (count - 1), [1] * (count - 1)
    while rest > 0:
        candidates = [i for i in range(count - 1) if holding[i] < reach]
        mass, remaining = sum([loads[i] for i in candidates]), rest
        for i in candidates:
            extra = min(reach - holding[i], max(1, remaining * loads[i] // mass), rest)
            holding[i] = holding[i] + extra
            rest = rest - extra
    return np.array([reach] + holding)


def uneven_parts(own_key, amount, total, most, lean):
    if amount == 2:
        one = jax.random.randint(own_key, (), max(1, total - most), min(most, total - 1) + 1)
        return jnp.stack([one, total - one])
    sizes = jnp.asarray(split_up(amount, total, most, lean), jnp.int32)
    pairs = (amount - 1) // 2
    donor, sink = sizes[1:1 + 2 * pairs:2], sizes[2:2 + 2 * pairs:2]
    room = jnp.minimum(donor - 1, most - sink)
    moved = jax.random.randint(jax.random.fold_in(own_key, 1), (pairs,), 0, 1 << 20) % (room + 1)
    sizes = sizes.at[1:1 + 2 * pairs:2].set(donor - moved).at[2:2 + 2 * pairs:2].set(sink + moved)
    return sizes[jax.random.permutation(jax.random.fold_in(own_key, 2), amount)]


def noise(key, extent, scale, most, pieces=(), held_as=jnp.bfloat16):
    result = scale * jax.random.normal(key, extent, jnp.float32)
    if pieces:
        result = result * levels(key, extent, pieces, -0.22, 0.18)
    return jnp.clip(result, -most, most).astype(held_as)


def setup_inputs(seed: int = 0) -> dict:
    key_list = jax.random.split(jax.random.key(seed), 16)
    tokens = noise(key_list[0], (TOKENS, D), 1.0, 6.0, ((0, 64),))
    cotangent = noise(key_list[1], (TOKENS, D), 1.0, 6.0, ((0, 64),))
    lengths = jax.vmap(lambda own: uneven_parts(own, SEQS, GROUP, LONGEST, 2))(jax.random.split(key_list[2], GROUPS)).reshape((GROUPS, SEQS)).astype(jnp.int32)
    gain_attn = jnp.clip(1.0 + 0.1 * jax.random.normal(key_list[3], (D,), jnp.float32), 0.5, 1.5).astype(jnp.bfloat16)
    w_query = noise(key_list[4], (D, QH * HD), D ** -0.5, 0.15625, ((0, 16), (1, 2)))
    b_query = noise(key_list[5], (QH * HD,), 0.5, 3.0, ((0, 2),))
    w_key = noise(key_list[6], (D, KVH * HD), D ** -0.5, 0.15625, ((0, 16), (1, 2)))
    b_key = noise(key_list[7], (KVH * HD,), 0.5, 3.0, ((0, 2),))
    w_value = noise(key_list[8], (D, KVH * HD), D ** -0.5, 0.15625, ((0, 16), (1, 2)))
    b_value = noise(key_list[9], (KVH * HD,), 0.5, 3.0, ((0, 2),))
    w_out = noise(key_list[10], (QH * HD, D), (QH * HD // 64) ** -0.5, 1.25, ((0, 2), (1, 16)))
    gain_mlp = jnp.clip(1.0 + 0.1 * jax.random.normal(key_list[11], (D,), jnp.float32), 0.5, 1.5).astype(jnp.bfloat16)
    w_gate = noise(key_list[12], (D, FF), D ** -0.5, 0.15625, ((0, 16), (1, 2)))
    w_up = noise(key_list[13], (D, FF), D ** -0.5, 0.15625, ((0, 16), (1, 2)))
    w_down = noise(key_list[14], (FF, D), FF ** -0.5, 0.0625, ((0, 2), (1, 16)))
    return {"tokens": tokens, "cotangent": cotangent, "lengths": lengths, "gain_attn": gain_attn, "w_query": w_query, "b_query": b_query, "w_key": w_key, "b_key": b_key, "w_value": w_value, "b_value": b_value, "w_out": w_out, "gain_mlp": gain_mlp, "w_gate": w_gate, "w_up": w_up, "w_down": w_down}


ROPE_BASE = 1000000.0
EPSILON = 1e-06

@jax.custom_vjp
def low(v):
    return lax.optimization_barrier(v.astype(jnp.bfloat16)).astype(jnp.float32)

@jax.custom_vjp
def low_back(v):
    return v

def low_keep(v):
    return (low(v), None)

def low_pass(kept, grad):
    return (grad,)

def back_keep(v):
    return (v, None)

def back_low(kept, grad):
    return (low(grad),)
low.defvjp(low_keep, low_pass)
low_back.defvjp(back_keep, back_low)

def precise(left, right):
    return jnp.dot(left, right, precision=lax.Precision.HIGHEST, preferred_element_type=jnp.float32)

def rms_norm(values, gain_vec):
    return values * lax.rsqrt(lax.optimization_barrier(jnp.mean(values * values, axis=-1, keepdims=True)) + EPSILON) * gain_vec

def rope_tables(positions, head_width):
    half_width = head_width // 2
    freq_index = jnp.arange(half_width).astype(jnp.float32)
    inverse = ROPE_BASE ** (-(freq_index * 2.0 / head_width))
    angles = positions.astype(jnp.float32)[:, None] * inverse[None, :]
    cosine = jnp.cos(angles)
    sine_table = jnp.sin(angles)
    return (jnp.concatenate([cosine, cosine], -1), jnp.concatenate([sine_table, sine_table], -1))

def rotate(values, cosine, sine_table):
    half_width = values.shape[-1] // 2
    turned = jnp.concatenate([-values[..., half_width:], values[..., :half_width]], -1)
    return values * cosine[:, None, :] + turned * sine_table[:, None, :]

def segment_info(seq_lengths, total_rows):
    ends_at = jnp.cumsum(seq_lengths).astype(jnp.int32)
    places = jnp.arange(total_rows, dtype=jnp.int32)
    passed = places[:, None] >= ends_at[None, :]
    segment = lax.optimization_barrier(jnp.sum(passed.astype(jnp.int32), axis=1)).astype(jnp.int32)
    starts = lax.optimization_barrier(jnp.sum(jnp.where(passed, seq_lengths[None, :], 0), axis=1)).astype(jnp.int32)
    return (segment, places - starts)

def layer(inputs, weights, segment, positions):
    gain_attn, w_query, b_query, w_key, b_key, w_value, b_value, w_out, gain_mlp, w_gate, w_up, w_down = weights
    length_rows = inputs.shape[0]
    head_groups = QH // KVH
    highest = lax.Precision.HIGHEST
    cosine, sine_table = rope_tables(positions, HD)
    normed_one = low(rms_norm(inputs, gain_attn))
    query_lin = low_back(precise(normed_one, w_query) + b_query)
    key_lin = low_back(precise(normed_one, w_key) + b_key)
    value_all = low(low_back(precise(normed_one, w_value) + b_value)).reshape(length_rows, KVH, HD)
    query_all = low(rotate(query_lin.reshape(length_rows, QH, HD), cosine, sine_table))
    query_all = query_all.reshape(length_rows, KVH, head_groups, HD)
    key_all = low(rotate(key_lin.reshape(length_rows, KVH, HD), cosine, sine_table))
    scores = low_back(jnp.einsum('qgjd,kgd->gjqk', query_all, key_all, precision=highest) * HD ** (-0.5))
    places = jnp.arange(length_rows, dtype=jnp.int32)
    allowed = (segment[:, None] == segment[None, :]) & (places[None, :] <= places[:, None])
    masked = jnp.where(allowed, scores, -1e+30)
    row_top = lax.optimization_barrier(jnp.max(masked, axis=-1, keepdims=True))
    expo = jnp.exp(masked - row_top)
    probs = expo / lax.optimization_barrier(jnp.sum(expo, axis=-1, keepdims=True))
    mixed = jnp.einsum('gjqk,kgd->qgjd', low(probs), value_all, precision=highest)
    mixed = low(low_back(mixed.reshape(length_rows, QH * HD)))
    middle = inputs + low_back(precise(mixed, w_out))
    normed_two = low(rms_norm(middle, gain_mlp))
    gate_lin = low_back(precise(normed_two, w_gate))
    up_lin = low_back(precise(normed_two, w_up))
    hidden = low(gate_lin * jax.nn.sigmoid(gate_lin) * up_lin)
    return middle + low_back(precise(hidden, w_down))

def reference(tokens, cotangent, lengths, gain_attn, w_query, b_query, w_key, b_key, w_value, b_value, w_out, gain_mlp, w_gate, w_up, w_down):
    params = tuple((item.astype(jnp.float32) for item in (gain_attn, w_query, b_query, w_key, b_key, w_value, b_value, w_out, gain_mlp, w_gate, w_up, w_down)))
    inputs = tokens.astype(jnp.float32).reshape(GROUPS, GROUP, D)

    def forward(input_groups, weights):

        def one_group(packed):
            group_rows, seq_lengths = packed
            segment, positions = segment_info(seq_lengths, GROUP)
            return jax.checkpoint(layer)(group_rows, weights, segment, positions)
        return lax.map(one_group, (input_groups, lengths))
    outputs, pull = jax.vjp(forward, inputs, params)
    d_inputs, d_params = pull(cotangent.astype(jnp.float32).reshape(GROUPS, GROUP, D))
    return (outputs.reshape(TOKENS, D).astype(jnp.bfloat16), d_inputs.reshape(TOKENS, D), d_params[0], d_params[1], d_params[2], d_params[3], d_params[4], d_params[5], d_params[6], d_params[7], d_params[8], d_params[9], d_params[10], d_params[11])
```

```python
import jax
import jax.numpy as jnp
from jax import lax
from jax.experimental import pallas as pl
from jax.sharding import PartitionSpec as P

HD = 128


ROPE_BASE = 1000000.0
EPSILON = 1e-06


def rms_norm(values, gain_vec):
    return (
        values * lax.rsqrt(jnp.mean(values * values, axis=-1, keepdims=True) + EPSILON) * gain_vec
    )


def rope_tables(positions, head_width):
    half_width = head_width // 2
    freq_index = jnp.arange(half_width).astype(jnp.float32)
    inverse = ROPE_BASE ** (-(freq_index * 2.0 / head_width))
    angles = positions.astype(jnp.float32)[:, None] * inverse[None, :]
    cosine = jnp.cos(angles)
    sine_table = jnp.sin(angles)
    return (jnp.concatenate([cosine, cosine], -1), jnp.concatenate([sine_table, sine_table], -1))


def rotate(values, cosine, sine_table):
    half_width = values.shape[-1] // 2
    turned = jnp.concatenate([-values[..., half_width:], values[..., :half_width]], -1)
    return values * cosine[:, None, :] + turned * sine_table[:, None, :]


def segment_info(seq_lengths, total_rows):
    ends_at = jnp.cumsum(seq_lengths)
    places = jnp.arange(total_rows, dtype=jnp.int32)
    passed = places[:, None] >= ends_at[None, :]
    segment = jnp.sum(passed.astype(jnp.int32), axis=1)
    starts = jnp.sum(jnp.where(passed, seq_lengths[None, :], 0), axis=1)
    return (segment, places - starts)


def lead_dot(left, right):
    return lax.dot_general(
        left, right, (((0,), (0,)), ((), ())), preferred_element_type=jnp.float32
    )


def tail_dot(left, right):
    return lax.dot_general(
        left, right, (((1,), (1,)), ((), ())), preferred_element_type=jnp.float32
    )


def swap_sum(x, axis):
    low = x.astype(jnp.bfloat16)
    other = lax.ppermute(low, axis, [(0, 1), (1, 0)])
    return low.astype(jnp.float32) + other.astype(jnp.float32)


def hidden_range(width, parts, rank):
    tiles = width // 128
    span = -(-tiles // parts) * 128
    start = jnp.minimum(rank * span, width - span)
    return span, pl.multiple_of(start, 128), parts * span - width


def on_device(
    tokens,
    cotangent,
    lengths,
    gain_attn,
    w_query,
    b_query,
    w_key,
    b_key,
    w_value,
    b_value,
    w_out,
    gain_mlp,
    w_gate,
    w_up,
    w_down,
):
    bf16, f32 = jnp.bfloat16, jnp.float32
    row_count, width = tokens.shape
    context_size = lax.axis_size("context")
    context_rank = lax.axis_index("context")
    fsdp_rank = lax.axis_index("fsdp")
    shard = w_query.shape[0]
    query_cols, kv_cols, hidden_cols = w_query.shape[1], w_key.shape[1], w_gate.shape[1]
    heads_kv = kv_cols // HD
    heads_query = query_cols // HD
    per_group = heads_query // heads_kv
    score_scale = HD ** (-0.5)
    group_rows = row_count * context_size
    segment_all, position_all = segment_info(lengths[0], group_rows)
    first_row = context_rank * row_count
    segment_mine = lax.dynamic_slice_in_dim(segment_all, first_row, row_count)
    position_mine = lax.dynamic_slice_in_dim(position_all, first_row, row_count)
    query_at = first_row + jnp.arange(row_count, dtype=jnp.int32)
    key_at = jnp.arange(group_rows, dtype=jnp.int32)
    allowed = (segment_mine[:, None] == segment_all[None, :]) & (
        key_at[None, :] <= query_at[:, None]
    )
    cosine, sine_table = rope_tables(position_mine, HD)

    span, start, overlap = hidden_range(hidden_cols, context_size, context_rank)
    gains = jnp.pad(jnp.stack([gain_attn, gain_mlp], axis=1), ((0, 0), (0, 126)))
    attn_pack = jnp.concatenate([w_query, w_key, w_value, w_out.T, gains], axis=1)
    mlp_pack = jnp.concatenate(
        [lax.dynamic_slice_in_dim(w, start, span, axis=1) for w in (w_gate, w_up, w_down.T)], axis=1
    )
    attn_full = lax.all_gather(attn_pack, "fsdp", axis=0, tiled=True)
    mlp_full = lax.all_gather(mlp_pack, "fsdp", axis=0, tiled=True)
    lin_cols = query_cols + 2 * kv_cols
    lin_full = attn_full[:, :lin_cols]
    out_turned = attn_full[:, lin_cols : lin_cols + query_cols]
    gain_one = attn_full[:, lin_cols + query_cols].astype(f32)
    gain_two = attn_full[:, lin_cols + query_cols + 1].astype(f32)
    gate_full, lift_full, down_turned = (mlp_full[:, k * span : (k + 1) * span] for k in range(3))
    keep = (
        jnp.arange(span) >= jnp.where(context_rank == context_size - 1, overlap, 0)
    )[None, :]
    dy_group = lax.all_gather(cotangent, "context", axis=0, tiled=True)

    inputs = tokens.astype(f32)
    normed_one = rms_norm(inputs, gain_one).astype(bf16)
    bias = jnp.concatenate([b_query, b_key, b_value]).astype(f32)
    lin = jnp.dot(normed_one, lin_full, preferred_element_type=f32) + bias
    query_lin = lin[:, :query_cols]
    key_lin = lin[:, query_cols : query_cols + kv_cols]
    value_lin = lin[:, query_cols + kv_cols :]
    query_heads = rotate(query_lin.reshape(row_count, heads_query, HD), cosine, sine_table).astype(bf16)
    query_heads = query_heads.reshape(row_count, heads_kv, per_group, HD)
    key_heads = rotate(key_lin.reshape(row_count, heads_kv, HD), cosine, sine_table).astype(bf16)
    value_heads = value_lin.astype(bf16).reshape(row_count, heads_kv, HD)
    kv_group = lax.all_gather(
        jnp.concatenate([key_heads, value_heads], axis=1), "context", axis=0, tiled=True
    )
    key_group, value_group = kv_group[:, :heads_kv], kv_group[:, heads_kv:]
    scores = (
        jnp.einsum("qgjd,kgd->gjqk", query_heads, key_group, preferred_element_type=f32)
        * score_scale
    )
    scores = jnp.where(allowed, scores, -1e30)
    row_top = jnp.max(scores, axis=-1, keepdims=True)
    expo = jnp.exp(scores - row_top)
    probs = expo / jnp.sum(expo, axis=-1, keepdims=True)
    probs_low = probs.astype(bf16)
    mixed = jnp.einsum("gjqk,kgd->qgjd", probs_low, value_group, preferred_element_type=f32)
    mixed = mixed.reshape(row_count, heads_query * HD).astype(bf16)
    middle = inputs + swap_sum(tail_dot(mixed, out_turned), "tensor")
    normed_two = rms_norm(middle, gain_two).astype(bf16)

    normed_group = lax.all_gather(normed_two, "context", axis=0, tiled=True)
    d_hidden = jnp.dot(dy_group, down_turned, preferred_element_type=f32)
    gate_lin = jnp.dot(normed_group, gate_full, preferred_element_type=f32)
    lift_lin = jnp.dot(normed_group, lift_full, preferred_element_type=f32)
    sigmoid_gate = jax.nn.sigmoid(gate_lin)
    swish = gate_lin * sigmoid_gate
    hidden = jnp.where(keep, swish * lift_lin, 0.0).astype(bf16)
    d_gate = jnp.where(
        keep, d_hidden * lift_lin * sigmoid_gate * (1.0 + gate_lin * (1.0 - sigmoid_gate)), 0.0
    ).astype(bf16)
    d_lift = jnp.where(keep, d_hidden * swish, 0.0).astype(bf16)
    d_normed_part = tail_dot(d_gate, gate_full) + tail_dot(d_lift, lift_full)
    d_normed_two = swap_sum(
        lax.psum_scatter(d_normed_part.astype(bf16), "context", scatter_dimension=0, tiled=True),
        "tensor",
    )
    mlp_part = tail_dot(hidden, down_turned)
    mlp_branch = swap_sum(
        lax.psum_scatter(mlp_part.astype(bf16), "context", scatter_dimension=0, tiled=True),
        "tensor",
    )
    result = (middle + mlp_branch).astype(bf16)
    mlp_grads = jnp.concatenate(
        [
            lead_dot(normed_group, d_gate).astype(bf16),
            lead_dot(normed_group, d_lift).astype(bf16),
            lead_dot(dy_group, hidden).astype(bf16),
        ],
        axis=1,
    )
    mlp_shard = lax.psum_scatter(mlp_grads, "fsdp", scatter_dimension=0, tiled=True)
    mlp_all = lax.all_gather(mlp_shard, "context", axis=0)

    def whole(k):
        parts = [mlp_all[i, :, k * span : (k + 1) * span] for i in range(context_size)]
        parts[-1] = parts[-1][:, overlap:]
        return jnp.concatenate(parts, axis=1).astype(f32)

    _, pull_two = jax.vjp(rms_norm, middle, gain_two)
    d_middle_norm, grad_gain_mlp = pull_two(d_normed_two)
    d_middle = cotangent.astype(f32) + d_middle_norm
    d_branch = d_middle.astype(bf16)
    grad_w_out = lead_dot(d_branch, mixed)
    d_mixed = (
        jnp.dot(d_branch, out_turned, preferred_element_type=f32)
        .astype(bf16)
        .reshape(row_count, heads_kv, per_group, HD)
    )
    d_probs = jnp.einsum("qgjd,kgd->gjqk", d_mixed, value_group, preferred_element_type=f32)
    inner = jnp.sum(probs * d_probs, axis=-1, keepdims=True)
    d_scores = (probs * (d_probs - inner)).astype(bf16)
    d_query = (
        jnp.einsum("gjqk,kgd->qgjd", d_scores, key_group, preferred_element_type=f32) * score_scale
    )
    d_key_part = (
        jnp.einsum("gjqk,qgjd->kgd", d_scores, query_heads, preferred_element_type=f32)
        * score_scale
    )
    d_value_part = jnp.einsum("gjqk,qgjd->kgd", probs_low, d_mixed, preferred_element_type=f32)
    d_kv = lax.psum_scatter(
        jnp.concatenate([d_key_part, d_value_part], axis=1), "context", scatter_dimension=0, tiled=True
    )
    d_key, d_value = d_kv[:, :heads_kv], d_kv[:, heads_kv:]

    def turn_query(values):
        return rotate(values, cosine, sine_table)

    _, pull_query = jax.vjp(turn_query, query_lin.reshape(row_count, heads_query, HD))
    _, pull_key = jax.vjp(turn_query, key_lin.reshape(row_count, heads_kv, HD))
    d_query_lin = pull_query(d_query.reshape(row_count, heads_query, HD))[0]
    d_key_lin = pull_key(d_key)[0]
    d_lin = jnp.concatenate(
        [
            d_query_lin.reshape(row_count, query_cols),
            d_key_lin.reshape(row_count, kv_cols),
            d_value.reshape(row_count, kv_cols),
        ],
        axis=1,
    ).astype(bf16)
    bias_part = jnp.sum(d_lin.astype(f32), axis=0)
    attn_grads = jnp.concatenate(
        [lead_dot(normed_one, d_lin).astype(bf16), grad_w_out.astype(bf16)], axis=1
    )
    attn_shard = lax.psum(
        lax.psum_scatter(attn_grads, "fsdp", scatter_dimension=0, tiled=True), "context"
    ).astype(f32)
    d_normed_one = swap_sum(tail_dot(d_lin, lin_full), "tensor")
    _, pull_one = jax.vjp(rms_norm, inputs, gain_one)
    d_input_norm, grad_gain_attn = pull_one(d_normed_one)
    grad_tokens = d_middle + d_input_norm
    small = lax.psum(
        jnp.concatenate([grad_gain_attn, grad_gain_mlp, bias_part]), ("fsdp", "context")
    )
    own = lambda at: lax.dynamic_slice_in_dim(small, at + fsdp_rank * shard, shard)
    bias_total = small[2 * width :]
    return (
        result,
        grad_tokens,
        own(0),
        attn_shard[:, :query_cols],
        bias_total[:query_cols],
        attn_shard[:, query_cols : query_cols + kv_cols],
        bias_total[query_cols : query_cols + kv_cols],
        attn_shard[:, query_cols + kv_cols : lin_cols],
        bias_total[query_cols + kv_cols :],
        attn_shard[:, lin_cols:].T,
        own(width),
        whole(0),
        whole(1),
        whole(2).T,
    )


def solution(mesh):
    return jax.shard_map(
        on_device,
        mesh=mesh,
        in_specs=(
            P(("fsdp", "context"), None),
            P(("fsdp", "context"), None),
            P("fsdp", None),
            P("fsdp"),
            P("fsdp", "tensor"),
            P("tensor"),
            P("fsdp", "tensor"),
            P("tensor"),
            P("fsdp", "tensor"),
            P("tensor"),
            P("tensor", "fsdp"),
            P("fsdp"),
            P("fsdp", "tensor"),
            P("fsdp", "tensor"),
            P("tensor", "fsdp"),
        ),
        out_specs=(
            P(("fsdp", "context"), None),
            P(("fsdp", "context"), None),
            P("fsdp"),
            P("fsdp", "tensor"),
            P("tensor"),
            P("fsdp", "tensor"),
            P("tensor"),
            P("fsdp", "tensor"),
            P("tensor"),
            P("tensor", "fsdp"),
            P("fsdp"),
            P("fsdp", "tensor"),
            P("fsdp", "tensor"),
            P("tensor", "fsdp"),
        ),
        check_vma=False,
    )
```

```python
import jax
import jax.numpy as jnp
from jax import lax
from jax.experimental import pallas as pl
from jax.experimental.pallas import tpu as pltpu
from jax.sharding import PartitionSpec as P

HD = 128
MESH = pl.DeviceIdType.MESH
ANY = pl.BlockSpec(memory_space=pl.ANY)
VM = pl.BlockSpec(memory_space=pltpu.VMEM)
f32, bf16 = jnp.float32, jnp.bfloat16

ROPE_BASE = 1000000.0
EPSILON = 1e-06

def meet(targets):
    barrier = pltpu.get_barrier_semaphore()
    for t in targets:
        pl.semaphore_signal(barrier, inc=1, device_id=t, device_id_type=MESH)
    pl.semaphore_wait(barrier, len(targets))

def gather_kernel(x_ref, y_ref, w_ref, g_ref, send, recv, local):
    shard = x_ref.shape[0]
    rows = y_ref.shape[0]
    f = lax.axis_index("fsdp"); c = lax.axis_index("context")
    n, m = lax.axis_size("fsdp"), lax.axis_size("context")
    core = lambda i: i + 1 - 2 * lax.rem(i, 2)
    far = lambda i: i + 2 - 4 * lax.rem(lax.div(i, 2), 2)
    up = lambda i: lax.rem(i + 4, n)
    down = lambda i: lax.rem(i + n - 4, n)
    nxt, prv = lax.rem(c + 1, m), lax.rem(c + m - 1, m)
    F = lambda i: {"fsdp": i}
    C = lambda i: {"context": i}
    meet([F(core(f)), F(far(f)), F(up(f)), F(down(f)), C(nxt), C(prv)])
    own = pltpu.make_async_copy(x_ref, w_ref.at[pl.ds(f * shard, shard)], local.at[0])
    own.start()
    own2 = pltpu.make_async_copy(y_ref, g_ref.at[pl.ds(c * rows, rows)], local.at[1])
    own2.start()
    half = shard // 2
    started = []
    def push(k, ref, at, size, to, src=None):
        win = ref.at[pl.ds(pl.multiple_of(at, 16), size)]
        cp = pltpu.make_async_remote_copy(win if src is None else src, win, send.at[k], recv.at[k],
                                          device_id=to, device_id_type=MESH)
        cp.start(); started.append(cp)
    def land(k, ref, at, size, like):
        win = ref.at[pl.ds(pl.multiple_of(at, 16), size)]
        pltpu.make_async_remote_copy(win, win, send.at[k], recv.at[k], device_id=like, device_id_type=MESH).wait_recv()
    push(0, w_ref, f * shard, shard, F(far(f)), x_ref)
    push(1, w_ref, f * shard, shard, F(up(f)), x_ref)
    push(2, w_ref, f * shard, shard, F(down(f)), x_ref)
    push(20, g_ref, c * rows, rows, C(nxt), y_ref)
    push(21, g_ref, c * rows, rows, C(prv), y_ref)
    push(3, w_ref, f * shard, shard, F(core(f)), x_ref)
    p = far(f)
    land(0, w_ref, p * shard, shard, F(p))
    push(4, w_ref, p * shard, shard, F(up(f)))
    push(5, w_ref, p * shard, shard, F(down(f)))
    push(6, w_ref, p * shard, shard, F(core(f)))
    a, b = down(f), up(f)
    land(1, w_ref, a * shard, shard, F(a))
    push(7, w_ref, a * shard, half, F(up(f)))
    push(8, w_ref, a * shard, shard, F(core(f)))
    land(2, w_ref, b * shard, shard, F(b))
    push(9, w_ref, b * shard + half, half, F(down(f)))
    push(10, w_ref, b * shard, shard, F(core(f)))
    hr = rows // 2
    land(20, g_ref, prv * rows, rows, C(prv))
    push(22, g_ref, prv * rows, hr, C(nxt))
    land(21, g_ref, nxt * rows, rows, C(nxt))
    push(23, g_ref, nxt * rows + hr, hr, C(prv))
    a2, b2 = far(a), far(b)
    land(4, w_ref, a2 * shard, shard, F(a))
    push(11, w_ref, a2 * shard, half, F(up(f)))
    push(12, w_ref, a2 * shard, shard, F(core(f)))
    land(5, w_ref, b2 * shard, shard, F(b))
    push(13, w_ref, b2 * shard + half, half, F(down(f)))
    push(14, w_ref, b2 * shard, shard, F(core(f)))
    o = lax.rem(f + 8, n); o2 = far(o)
    land(7, w_ref, o * shard, half, F(a))
    push(15, w_ref, o * shard, half, F(core(f)))
    land(9, w_ref, o * shard + half, half, F(b))
    push(16, w_ref, o * shard + half, half, F(core(f)))
    land(11, w_ref, o2 * shard, half, F(a))
    push(17, w_ref, o2 * shard, half, F(core(f)))
    land(13, w_ref, o2 * shard + half, half, F(b))
    push(18, w_ref, o2 * shard + half, half, F(core(f)))
    s = core(f)
    sib = F(s)
    land(3, w_ref, s * shard, shard, sib)
    land(6, w_ref, far(s) * shard, shard, sib)
    land(8, w_ref, down(s) * shard, shard, sib)
    land(10, w_ref, up(s) * shard, shard, sib)
    land(12, w_ref, far(down(s)) * shard, shard, sib)
    land(14, w_ref, far(up(s)) * shard, shard, sib)
    so = lax.rem(s + 8, n)
    land(15, w_ref, so * shard, half, sib)
    land(16, w_ref, so * shard + half, half, sib)
    land(17, w_ref, far(so) * shard, half, sib)
    land(18, w_ref, far(so) * shard + half, half, sib)
    cf = lax.rem(c + 2, m)
    land(22, g_ref, cf * rows, hr, C(prv))
    land(23, g_ref, cf * rows + hr, hr, C(nxt))
    for cp in started: cp.wait_send()
    own.wait(); own2.wait()

def gather(x, y, cid=1):
    shard, cols = x.shape; rows, width = y.shape
    return pl.pallas_call(gather_kernel,
        out_shape=(jax.ShapeDtypeStruct((16*shard, cols), x.dtype), jax.ShapeDtypeStruct((4*rows, width), y.dtype)),
        in_specs=[ANY]*2, out_specs=(ANY, ANY),
        scratch_shapes=[pltpu.SemaphoreType.DMA((24,)), pltpu.SemaphoreType.DMA((24,)), pltpu.SemaphoreType.DMA((2,))],
        compiler_params=pltpu.CompilerParams(collective_id=cid, has_side_effects=True), name="gather_rows")(x, y)

def norm_kernel(part_ref, x_ref, gain_ref, mid_ref, out_ref, other, normed, send, recv, local):
    rows = part_ref.shape[0]
    chunks = 4
    size = rows // chunks
    half = size // 2
    c = lax.axis_index("context"); m = lax.axis_size("context")
    nxt, prv, cf = lax.rem(c + 1, m), lax.rem(c + m - 1, m), lax.rem(c + 2, m)
    T = {"tensor": 1 - lax.axis_index("tensor")}
    C = lambda i: {"context": i}
    meet([T, C(nxt), C(prv)])
    def copy(src, dst, k, to):
        return pltpu.make_async_remote_copy(src, dst, send.at[k], recv.at[k], device_id=to, device_id_type=MESH)
    def rows_of(owner, at, n):
        return out_ref.at[pl.ds(pl.multiple_of(owner * rows + at, 16), n)]
    started = []
    for k in range(chunks):
        at = pl.ds(k * size, size)
        cp = copy(part_ref.at[at], other.at[at], k, T); cp.start(); started.append(cp)
    locals_ = []
    def forward(k):
        a = rows_of(prv, k * size, size)
        copy(a, a, chunks + k, C(prv)).wait_recv()
        w = rows_of(prv, k * size, half)
        cp = copy(w, w, 3 * chunks + k, C(nxt)); cp.start(); started.append(cp)
        a = rows_of(nxt, k * size, size)
        copy(a, a, 2 * chunks + k, C(nxt)).wait_recv()
        w = rows_of(nxt, k * size + half, half)
        cp = copy(w, w, 4 * chunks + k, C(prv)); cp.start(); started.append(cp)
    for k in range(chunks):
        at = pl.ds(k * size, size)
        started[k].wait_recv()
        mid = x_ref[at].astype(f32) + (part_ref[at].astype(f32) + other[at].astype(f32))
        mid_ref[at] = mid
        r = lax.rsqrt(jnp.mean(mid * mid, axis=-1, keepdims=True) + EPSILON)
        normed[at] = (mid * r * gain_ref[...]).astype(bf16)
        lc = pltpu.make_async_copy(normed.at[at], rows_of(c, k * size, size), local.at[k]); lc.start(); locals_.append(lc)
        for d, to in ((0, nxt), (1, prv)):
            cp = copy(normed.at[at], rows_of(c, k * size, size), (1 + d) * chunks + k, C(to)); cp.start(); started.append(cp)
        if k:
            forward(k - 1)
    forward(chunks - 1)
    for k in range(chunks):
        w = rows_of(cf, k * size, half); copy(w, w, 3 * chunks + k, C(prv)).wait_recv()
        w = rows_of(cf, k * size + half, half); copy(w, w, 4 * chunks + k, C(nxt)).wait_recv()
    for cp in started: cp.wait_send()
    for lc in locals_: lc.wait()

def norm_gather(part, x, gain, cid=2):
    rows, width = x.shape
    return pl.pallas_call(norm_kernel,
        out_shape=(jax.ShapeDtypeStruct((rows, width), f32), jax.ShapeDtypeStruct((4 * rows, width), bf16)),
        in_specs=[VM] * 3, out_specs=(VM, ANY),
        scratch_shapes=[pltpu.VMEM((rows, width), bf16), pltpu.VMEM((rows, width), bf16),
                        pltpu.SemaphoreType.DMA((20,)), pltpu.SemaphoreType.DMA((20,)), pltpu.SemaphoreType.DMA((4,))],
        compiler_params=pltpu.CompilerParams(collective_id=cid, has_side_effects=True), name="norm_gather")(part, x, gain[None])

class Wire:
    def __init__(self, send, recv):
        self.send, self.recv, self.used, self.started = send, recv, 0, []

    def push(self, src, dst, to):
        k = self.used
        self.used += 1
        copy = pltpu.make_async_remote_copy(
            src, dst, self.send.at[k], self.recv.at[k], device_id=to, device_id_type=MESH
        )
        copy.start()
        self.started.append(copy)
        return copy

    def drain(self):
        for copy in self.started:
            copy.wait_send()


def along_context():
    c, m = lax.axis_index("context"), lax.axis_size("context")
    return c, lax.rem(c + 1, m), lax.rem(c + m - 1, m), lax.rem(c + 2, m)


def along_fsdp():
    f, n = lax.axis_index("fsdp"), lax.axis_size("fsdp")
    core = f + 1 - 2 * lax.rem(f, 2)
    far = f + 2 - 4 * lax.rem(lax.div(f, 2), 2)
    return f, core, far, lax.rem(f + 4, n), lax.rem(f + n - 4, n)


class RowSum:
    def __init__(self, wire, part, out, from_prv, from_nxt, mine, other, chunks):
        self.wire, self.part, self.out, self.chunks = wire, part, out, chunks
        self.from_prv, self.from_nxt, self.mine, self.other = from_prv, from_nxt, mine, other
        self.rows, self.width = out.shape
        self.half = self.rows // 2
        self.c, self.nxt, self.prv, self.cf = along_context()
        self.relay_p, self.relay_n, self.plain_p, self.plain_n = {}, {}, {}, {}
        self.more_p, self.more_n, self.swap = {}, {}, {}

    def cols(self, k):
        size = self.width // self.chunks
        return pl.ds(k * size, size)

    def win(self, owner, second, k):
        at = pl.multiple_of(owner * self.rows + second * self.half, 16)
        return pl.ds(at, self.half), self.cols(k)

    def start(self, k):
        up, down = {"context": self.nxt}, {"context": self.prv}
        part, cols = self.part, self.cols(k)
        push = self.wire.push
        self.relay_p[k] = push(part.at[self.win(self.cf, 0, k)], self.from_prv.at[0, :, cols], up)
        self.relay_n[k] = push(part.at[self.win(self.cf, 1, k)], self.from_nxt.at[0, :, cols], down)
        self.plain_p[k] = push(part.at[self.win(self.nxt, 1, k)], self.from_prv.at[1, :, cols], up)
        self.plain_n[k] = push(part.at[self.win(self.prv, 0, k)], self.from_nxt.at[1, :, cols], down)

    def relay(self, k):
        cols, push = self.cols(k), self.wire.push
        self.relay_p[k].wait_recv()
        self.from_prv[0, :, cols] = (
            self.from_prv[0, :, cols].astype(f32) + self.part[self.win(self.nxt, 0, k)].astype(f32)
        ).astype(bf16)
        self.more_p[k] = push(self.from_prv.at[0, :, cols], self.from_prv.at[2, :, cols], {"context": self.nxt})
        self.relay_n[k].wait_recv()
        self.from_nxt[0, :, cols] = (
            self.from_nxt[0, :, cols].astype(f32) + self.part[self.win(self.prv, 1, k)].astype(f32)
        ).astype(bf16)
        self.more_n[k] = push(self.from_nxt.at[0, :, cols], self.from_nxt.at[2, :, cols], {"context": self.prv})

    def exchange(self, k):
        cols, half = self.cols(k), self.half
        self.plain_n[k].wait_recv()
        self.more_p[k].wait_recv()
        first = (
            self.part[self.win(self.c, 0, k)].astype(f32)
            + self.from_nxt[1, :, cols].astype(f32)
            + self.from_prv[2, :, cols].astype(f32)
        )
        self.mine[pl.ds(0, half), cols] = first.astype(bf16)
        self.plain_p[k].wait_recv()
        self.more_n[k].wait_recv()
        second = (
            self.part[self.win(self.c, 1, k)].astype(f32)
            + self.from_prv[1, :, cols].astype(f32)
            + self.from_nxt[2, :, cols].astype(f32)
        )
        self.mine[pl.ds(half, half), cols] = second.astype(bf16)
        to = {"tensor": 1 - lax.axis_index("tensor")}
        self.swap[k] = self.wire.push(self.mine.at[:, cols], self.other.at[:, cols], to)

    def finish(self, k):
        cols = self.cols(k)
        self.swap[k].wait_recv()
        total = self.mine[:, cols].astype(f32) + self.other[:, cols].astype(f32)
        self.out[:, cols] = total.astype(self.out.dtype)


class ShardSum:
    def __init__(self, wire, got, from_down, from_up, pair, last, chunks):
        self.wire, self.got, self.from_down, self.from_up = wire, got, from_down, from_up
        self.pair, self.last, self.chunks = pair, last, chunks
        self.shard, width = got.shape[1:]
        self.half, self.size = self.shard // 2, width // chunks
        self.f, self.core, self.far, self.up, self.down = along_fsdp()
        self.side = lax.rem(lax.div(self.f, 2), 2)
        self.mine = lax.rem(self.f, 2)
        self.cores, self.plain, self.relay, self.more, self.cross = {}, {}, {}, {}, {}

    def cols(self, k):
        return pl.ds(k * self.size, self.size)

    def send_core(self, k, rel, src):
        self.cores[k, rel] = self.wire.push(
            src, self.got.at[pl.ds(2 * rel, 2), :, self.cols(k)], {"fsdp": self.core}
        )

    def add_core(self, k, rel, own):
        self.cores[k, rel].wait_recv()
        at = pl.ds(2 * rel, 2), slice(None), self.cols(k)
        self.got[at] = (self.got[at].astype(f32) + own.astype(f32)).astype(bf16)

    def block(self, rel, second, k):
        return pl.ds(2 * rel, 2), pl.ds(second * self.half, self.half), self.cols(k)

    def start(self, k):
        got, cols, push = self.got, self.cols(k), self.wire.push
        up, down = {"fsdp": self.up}, {"fsdp": self.down}
        self.relay[k] = (
            push(got.at[self.block(2, 0, k)], self.from_down.at[0, :, :, cols], up),
            push(got.at[self.block(2, 1, k)], self.from_up.at[0, :, :, cols], down),
        )
        self.plain[k] = (
            push(got.at[self.block(1, 1, k)], self.from_down.at[1, :, :, cols], up),
            push(got.at[self.block(3, 0, k)], self.from_up.at[1, :, :, cols], down),
        )

    def relays(self, k):
        cols, push = self.cols(k), self.wire.push
        self.relay[k][0].wait_recv()
        at = (0, slice(None), slice(None), cols)
        self.from_down[at] = (
            self.from_down[at].astype(f32) + self.got[self.block(1, 0, k)].astype(f32)
        ).astype(bf16)
        one = push(self.from_down.at[at], self.from_down.at[2, :, :, cols], {"fsdp": self.up})
        self.relay[k][1].wait_recv()
        self.from_up[at] = (
            self.from_up[at].astype(f32) + self.got[self.block(3, 1, k)].astype(f32)
        ).astype(bf16)
        two = push(self.from_up.at[at], self.from_up.at[2, :, :, cols], {"fsdp": self.down})
        self.more[k] = (one, two)

    def across(self, k):
        cols, half = self.cols(k), self.half
        self.more[k][0].wait_recv()
        self.plain[k][1].wait_recv()
        self.pair[:, pl.ds(0, half), cols] = (
            self.got[self.block(0, 0, k)].astype(f32)
            + self.from_down[2, :, :, cols].astype(f32)
            + self.from_up[1, :, :, cols].astype(f32)
        ).astype(bf16)
        self.more[k][1].wait_recv()
        self.plain[k][0].wait_recv()
        self.pair[:, pl.ds(half, half), cols] = (
            self.got[self.block(0, 1, k)].astype(f32)
            + self.from_down[1, :, :, cols].astype(f32)
            + self.from_up[2, :, :, cols].astype(f32)
        ).astype(bf16)
        self.cross[k] = self.wire.push(
            self.pair.at[1 - self.side, :, cols], self.last.at[:, cols], {"fsdp": self.far}
        )

    def total(self, k):
        cols = self.cols(k)
        self.cross[k].wait_recv()
        return self.pair[self.side, :, cols].astype(f32) + self.last[:, cols].astype(f32)


def shard_scratch(shard, width, blocks=8):
    return [
        pltpu.VMEM((blocks, shard, width), bf16),
        pltpu.VMEM((3, 2, shard // 2, width), bf16),
        pltpu.VMEM((3, 2, shard // 2, width), bf16),
        pltpu.VMEM((2, shard, width), bf16),
        pltpu.VMEM((shard, width), bf16),
    ]


def row_scratch(rows, width):
    return [pltpu.VMEM((3, rows // 2, width), bf16)] * 2 + [pltpu.VMEM((rows, width), bf16)] * 2


def everyone_near():
    _, core, far, up, down = along_fsdp()
    _, nxt, prv, _ = along_context()
    return [{"fsdp": i} for i in (core, far, up, down)] + [
        {"context": nxt}, {"context": prv}, {"tensor": 1 - lax.axis_index("tensor")}
    ]


ORDER = (2, 1, 3, 0)


def mlp_back_kernel(
    normed_ref, dy_ref, gate_ref, lift_ref, hidden_ref, first_ref, second_ref,
    first_out, second_out, shard_out,
    grads, got, from_down, from_up, pair, last,
    prv1, nxt1, mine1, other1, prv2, nxt2, mine2, other2, send, recv,
):
    wire = Wire(send, recv)
    meet(everyone_near())
    chunks = 3
    sums = ShardSum(wire, got, from_down, from_up, pair, last, chunks)
    rows1 = RowSum(wire, first_ref, first_out, prv1, nxt1, mine1, other1, chunks)
    rows2 = RowSum(wire, second_ref, second_out, prv2, nxt2, mine2, other2, chunks)
    shard, span = sums.shard, sums.size
    z = lax.div(sums.f, 4)
    for k in range(chunks):
        rows1.start(k)
    pairs = ((normed_ref, gate_ref), (normed_ref, lift_ref), (dy_ref, hidden_ref))
    for k, (left, right) in enumerate(pairs):
        for rel in ORDER:
            at = pl.multiple_of(lax.rem(z + rel, 4) * (4 * shard), 4 * shard)
            tile = jnp.dot(left[pl.ds(at, 4 * shard), :], right[...], preferred_element_type=f32).astype(bf16)
            for side in range(2):
                for core in range(2):
                    lo = (2 * side + core) * shard
                    grads[core, 2 * rel + side, :, sums.cols(k)] = tile[lo : lo + shard]
            sums.send_core(k, rel, grads.at[1 - sums.mine, pl.ds(2 * rel, 2), :, sums.cols(k)])
        if k == 1:
            for j in range(chunks):
                rows1.relay(j)
            for j in range(chunks):
                rows2.start(j)
        if k >= 1:
            for rel in ORDER:
                sums.add_core(k - 1, rel, grads[sums.mine, pl.ds(2 * rel, 2), :, sums.cols(k - 1)])
            sums.start(k - 1)
    for rel in ORDER:
        sums.add_core(2, rel, grads[sums.mine, pl.ds(2 * rel, 2), :, sums.cols(2)])
    sums.start(2)
    for k in range(chunks):
        rows1.exchange(k)
        sums.relays(k)
    for k in range(chunks):
        rows2.relay(k)
    for k in range(chunks):
        rows1.finish(k)
        sums.across(k)
    for k in range(chunks):
        rows2.exchange(k)
    for k in range(chunks):
        shard_out[:, sums.cols(k)] = sums.total(k).astype(bf16)
        rows2.finish(k)
    wire.drain()


def mlp_back(normed_turned, dy_turned, d_gate, d_lift, hidden, first, second, cid=3):
    width = normed_turned.shape[0]
    rows, span = first.shape[0] // 4, d_gate.shape[1]
    shard = width // 16
    sems = 3 * (4 + 4 + 2 + 1) + 2 * 3 * 7
    return pl.pallas_call(
        mlp_back_kernel,
        out_shape=(
            jax.ShapeDtypeStruct((rows, width), f32),
            jax.ShapeDtypeStruct((rows, width), bf16),
            jax.ShapeDtypeStruct((shard, 3 * span), bf16),
        ),
        in_specs=[VM] * 7,
        out_specs=(VM,) * 3,
        scratch_shapes=[pltpu.VMEM((2, 8, shard, 3 * span), bf16)]
        + shard_scratch(shard, 3 * span)
        + row_scratch(rows, width) * 2
        + [pltpu.SemaphoreType.DMA((sems,)), pltpu.SemaphoreType.DMA((sems,))],
        compiler_params=pltpu.CompilerParams(
            collective_id=cid, has_side_effects=True, vmem_limit_bytes=62 << 20
        ),
        name="mlp_back",
    )(normed_turned, dy_turned, d_gate, d_lift, hidden, first, second)


def rms_norm(values, gain_vec):
    return (
        values * lax.rsqrt(jnp.mean(values * values, axis=-1, keepdims=True) + EPSILON) * gain_vec
    )


def rope_tables(positions, head_width):
    half_width = head_width // 2
    freq_index = jnp.arange(half_width).astype(jnp.float32)
    inverse = ROPE_BASE ** (-(freq_index * 2.0 / head_width))
    angles = positions.astype(jnp.float32)[:, None] * inverse[None, :]
    cosine = jnp.cos(angles)
    sine_table = jnp.sin(angles)
    return (jnp.concatenate([cosine, cosine], -1), jnp.concatenate([sine_table, sine_table], -1))


def rotate(values, cosine, sine_table):
    half_width = values.shape[-1] // 2
    turned = jnp.concatenate([-values[..., half_width:], values[..., :half_width]], -1)
    return values * cosine[:, None, :] + turned * sine_table[:, None, :]


def segment_info(seq_lengths, total_rows):
    ends_at = jnp.cumsum(seq_lengths)
    places = jnp.arange(total_rows, dtype=jnp.int32)
    passed = places[:, None] >= ends_at[None, :]
    segment = jnp.sum(passed.astype(jnp.int32), axis=1)
    starts = jnp.sum(jnp.where(passed, seq_lengths[None, :], 0), axis=1)
    return (segment, places - starts)


def lead_dot(left, right):
    return lax.dot_general(
        left, right, (((0,), (0,)), ((), ())), preferred_element_type=jnp.float32
    )


def tail_dot(left, right):
    return lax.dot_general(
        left, right, (((1,), (1,)), ((), ())), preferred_element_type=jnp.float32
    )


def swap_sum(x, axis):
    low = x.astype(jnp.bfloat16)
    other = lax.ppermute(low, axis, [(0, 1), (1, 0)])
    return low.astype(jnp.float32) + other.astype(jnp.float32)


def around(x):
    size, rank = lax.axis_size("context"), lax.axis_index("context")
    parts = [x] + [
        lax.ppermute(x, "context", [(i, (i - k) % size) for i in range(size)]) for k in range(1, size)
    ]
    twice = jnp.concatenate(parts + parts, axis=0)
    rows = x.shape[0]
    return lax.dynamic_slice_in_dim(twice, (size - rank) % size * rows, size * rows)


def back_around(x):
    size, rank = lax.axis_size("context"), lax.axis_index("context")
    rows = x.shape[0] // size
    total = lax.dynamic_slice_in_dim(x, rank * rows, rows)
    for k in range(1, size):
        block = lax.dynamic_slice_in_dim(x, (rank + k) % size * rows, rows)
        total = total + lax.ppermute(block, "context", [(i, (i + k) % size) for i in range(size)])
    return total


def hidden_range(width, parts, rank):
    tiles = width // 128
    span = -(-tiles // parts) * 128
    start = jnp.minimum(rank * span, width - span)
    return span, pl.multiple_of(start, 128), parts * span - width


def on_device(
    tokens,
    cotangent,
    lengths,
    gain_attn,
    w_query,
    b_query,
    w_key,
    b_key,
    w_value,
    b_value,
    w_out,
    gain_mlp,
    w_gate,
    w_up,
    w_down,
):
    row_count, width = tokens.shape
    context_size = lax.axis_size("context")
    context_rank = lax.axis_index("context")
    fsdp_rank = lax.axis_index("fsdp")
    shard = w_query.shape[0]
    query_cols, kv_cols, hidden_cols = w_query.shape[1], w_key.shape[1], w_gate.shape[1]
    heads_kv = kv_cols // HD
    heads_query = query_cols // HD
    per_group = heads_query // heads_kv
    score_scale = HD ** (-0.5)
    group_rows = row_count * context_size
    segment_all, position_all = segment_info(lengths[0], group_rows)
    first_row = context_rank * row_count
    segment_mine = lax.dynamic_slice_in_dim(segment_all, first_row, row_count)
    position_mine = lax.dynamic_slice_in_dim(position_all, first_row, row_count)
    query_at = first_row + jnp.arange(row_count, dtype=jnp.int32)
    key_at = jnp.arange(group_rows, dtype=jnp.int32)
    allowed = (segment_mine[:, None] == segment_all[None, :]) & (
        key_at[None, :] <= query_at[:, None]
    )
    cosine, sine_table = rope_tables(position_mine, HD)

    span, start, overlap = hidden_range(hidden_cols, context_size, context_rank)
    gains = jnp.pad(jnp.stack([gain_attn, gain_mlp], axis=1), ((0, 0), (0, 126)))
    attn_pack = jnp.concatenate([w_query, w_key, w_value, w_out.T, gains], axis=1)
    mlp_pack = jnp.concatenate(
        [lax.dynamic_slice_in_dim(w, start, span, axis=1) for w in (w_gate, w_up, w_down.T)], axis=1
    )
    attn_full, dy_group = gather(attn_pack, cotangent)
    mlp_pack, attn_full = lax.optimization_barrier((mlp_pack, attn_full))
    mlp_full = lax.all_gather(mlp_pack, "fsdp", axis=0, tiled=True)
    lin_cols = query_cols + 2 * kv_cols
    lin_full = attn_full[:, :lin_cols]
    out_turned = attn_full[:, lin_cols : lin_cols + query_cols]
    gain_one = attn_full[:, lin_cols + query_cols].astype(f32)
    gain_two = attn_full[:, lin_cols + query_cols + 1].astype(f32)
    gate_full, lift_full, down_turned = (mlp_full[:, k * span : (k + 1) * span] for k in range(3))
    keep = (
        jnp.arange(span) >= jnp.where(context_rank == context_size - 1, overlap, 0)
    )[None, :]

    inputs = tokens.astype(f32)
    normed_one = rms_norm(inputs, gain_one).astype(bf16)
    bias = jnp.concatenate([b_query, b_key, b_value]).astype(f32)
    lin = jnp.dot(normed_one, lin_full, preferred_element_type=f32) + bias
    query_lin = lin[:, :query_cols]
    key_lin = lin[:, query_cols : query_cols + kv_cols]
    value_lin = lin[:, query_cols + kv_cols :]
    query_heads = rotate(query_lin.reshape(row_count, heads_query, HD), cosine, sine_table).astype(bf16)
    query_heads = query_heads.reshape(row_count, heads_kv, per_group, HD)
    key_heads = rotate(key_lin.reshape(row_count, heads_kv, HD), cosine, sine_table).astype(bf16)
    value_heads = value_lin.astype(bf16).reshape(row_count, heads_kv, HD)
    kv_group = around(jnp.concatenate([key_heads, value_heads], axis=1))
    key_group, value_group = kv_group[:, :heads_kv], kv_group[:, heads_kv:]
    scores = (
        jnp.einsum("qgjd,kgd->gjqk", query_heads, key_group, preferred_element_type=f32)
        * score_scale
    )
    scores = jnp.where(allowed, scores, -1e30)
    row_top = jnp.max(scores, axis=-1, keepdims=True)
    expo = jnp.exp(scores - row_top)
    probs = expo / jnp.sum(expo, axis=-1, keepdims=True)
    probs_low = probs.astype(bf16)
    mixed = jnp.einsum("gjqk,kgd->qgjd", probs_low, value_group, preferred_element_type=f32)
    mixed = mixed.reshape(row_count, heads_query * HD).astype(bf16)

    middle, normed_group = norm_gather(tail_dot(mixed, out_turned).astype(bf16), tokens, gain_two)
    d_hidden = jnp.dot(dy_group, down_turned, preferred_element_type=f32)
    gate_lin = jnp.dot(normed_group, gate_full, preferred_element_type=f32)
    lift_lin = jnp.dot(normed_group, lift_full, preferred_element_type=f32)
    sigmoid_gate = jax.nn.sigmoid(gate_lin)
    swish = gate_lin * sigmoid_gate
    hidden = jnp.where(keep, swish * lift_lin, 0.0).astype(bf16)
    d_gate = jnp.where(
        keep, d_hidden * lift_lin * sigmoid_gate * (1.0 + gate_lin * (1.0 - sigmoid_gate)), 0.0
    ).astype(bf16)
    d_lift = jnp.where(keep, d_hidden * swish, 0.0).astype(bf16)
    d_normed_part = tail_dot(d_gate, gate_full) + tail_dot(d_lift, lift_full)
    mlp_part = tail_dot(hidden, down_turned).astype(bf16)
    d_normed_two, mlp_branch, mlp_shard = mlp_back(
        normed_group.T, dy_group.T, d_gate, d_lift, hidden, d_normed_part.astype(bf16), mlp_part
    )
    result = (middle + mlp_branch.astype(f32)).astype(bf16)
    mlp_all = lax.all_gather(mlp_shard, "context", axis=0)

    def whole(k):
        parts = [mlp_all[i, :, k * span : (k + 1) * span] for i in range(context_size)]
        parts[-1] = parts[-1][:, overlap:]
        return jnp.concatenate(parts, axis=1).astype(f32)

    _, pull_two = jax.vjp(rms_norm, middle, gain_two)
    d_middle_norm, grad_gain_mlp = pull_two(d_normed_two)
    d_middle = cotangent.astype(f32) + d_middle_norm
    d_branch = d_middle.astype(bf16)
    grad_w_out = lead_dot(d_branch, mixed)
    d_mixed = (
        jnp.dot(d_branch, out_turned, preferred_element_type=f32)
        .astype(bf16)
        .reshape(row_count, heads_kv, per_group, HD)
    )
    d_probs = jnp.einsum("qgjd,kgd->gjqk", d_mixed, value_group, preferred_element_type=f32)
    inner = jnp.sum(probs * d_probs, axis=-1, keepdims=True)
    d_scores = (probs * (d_probs - inner)).astype(bf16)
    d_query = (
        jnp.einsum("gjqk,kgd->qgjd", d_scores, key_group, preferred_element_type=f32) * score_scale
    )
    d_key_part = (
        jnp.einsum("gjqk,qgjd->kgd", d_scores, query_heads, preferred_element_type=f32)
        * score_scale
    )
    d_value_part = jnp.einsum("gjqk,qgjd->kgd", probs_low, d_mixed, preferred_element_type=f32)
    d_kv = back_around(jnp.concatenate([d_key_part, d_value_part], axis=1))
    d_key, d_value = d_kv[:, :heads_kv], d_kv[:, heads_kv:]

    def turn_query(values):
        return rotate(values, cosine, sine_table)

    _, pull_query = jax.vjp(turn_query, query_lin.reshape(row_count, heads_query, HD))
    _, pull_key = jax.vjp(turn_query, key_lin.reshape(row_count, heads_kv, HD))
    d_query_lin = pull_query(d_query.reshape(row_count, heads_query, HD))[0]
    d_key_lin = pull_key(d_key)[0]
    d_lin = jnp.concatenate(
        [
            d_query_lin.reshape(row_count, query_cols),
            d_key_lin.reshape(row_count, kv_cols),
            d_value.reshape(row_count, kv_cols),
        ],
        axis=1,
    ).astype(bf16)
    bias_part = jnp.sum(d_lin.astype(f32), axis=0)
    attn_grads = jnp.concatenate(
        [lead_dot(normed_one, d_lin).astype(bf16), grad_w_out.astype(bf16)], axis=1
    )
    attn_shard = lax.psum(
        lax.psum_scatter(attn_grads, "fsdp", scatter_dimension=0, tiled=True), "context"
    ).astype(f32)
    d_normed_one = swap_sum(tail_dot(d_lin, lin_full), "tensor")
    _, pull_one = jax.vjp(rms_norm, inputs, gain_one)
    d_input_norm, grad_gain_attn = pull_one(d_normed_one)
    grad_tokens = d_middle + d_input_norm
    small = jnp.sum(
        lax.all_gather(
            jnp.concatenate([grad_gain_attn, grad_gain_mlp, bias_part])[None], ("fsdp", "context"), axis=0, tiled=True
        ),
        axis=0,
    )
    own = lambda at: lax.dynamic_slice_in_dim(small, at + fsdp_rank * shard, shard)
    bias_total = small[2 * width :]
    return (
        result,
        grad_tokens,
        own(0),
        attn_shard[:, :query_cols],
        bias_total[:query_cols],
        attn_shard[:, query_cols : query_cols + kv_cols],
        bias_total[query_cols : query_cols + kv_cols],
        attn_shard[:, query_cols + kv_cols : lin_cols],
        bias_total[query_cols + kv_cols :],
        attn_shard[:, lin_cols:].T,
        own(width),
        whole(0),
        whole(1),
        whole(2).T,
    )


def solution(mesh):
    return jax.shard_map(
        on_device,
        mesh=mesh,
        in_specs=(
            P(("fsdp", "context"), None),
            P(("fsdp", "context"), None),
            P("fsdp", None),
            P("fsdp"),
            P("fsdp", "tensor"),
            P("tensor"),
            P("fsdp", "tensor"),
            P("tensor"),
            P("fsdp", "tensor"),
            P("tensor"),
            P("tensor", "fsdp"),
            P("fsdp"),
            P("fsdp", "tensor"),
            P("fsdp", "tensor"),
            P("tensor", "fsdp"),
        ),
        out_specs=(
            P(("fsdp", "context"), None),
            P(("fsdp", "context"), None),
            P("fsdp"),
            P("fsdp", "tensor"),
            P("tensor"),
            P("fsdp", "tensor"),
            P("tensor"),
            P("fsdp", "tensor"),
            P("tensor"),
            P("tensor", "fsdp"),
            P("fsdp"),
            P("fsdp", "tensor"),
            P("fsdp", "tensor"),
            P("tensor", "fsdp"),
        ),
        check_vma=False,
    )
```

```python
import jax
import jax.numpy as jnp
from jax import lax
from jax.experimental import pallas as pl
from jax.experimental.pallas import tpu as pltpu
from jax.sharding import PartitionSpec as P

HD = 128
MESH = pl.DeviceIdType.MESH
ANY = pl.BlockSpec(memory_space=pl.ANY)
VM = pl.BlockSpec(memory_space=pltpu.VMEM)
f32, bf16 = jnp.float32, jnp.bfloat16

ROPE_BASE = 1000000.0
EPSILON = 1e-06

def meet(targets):
    barrier = pltpu.get_barrier_semaphore()
    for t in targets:
        pl.semaphore_signal(barrier, inc=1, device_id=t, device_id_type=MESH)
    pl.semaphore_wait(barrier, len(targets))

def gather_kernel(x_ref, y_ref, w_ref, g_ref, send, recv, local):
    shard = x_ref.shape[0]
    rows = y_ref.shape[0]
    f = lax.axis_index("fsdp"); c = lax.axis_index("context")
    n, m = lax.axis_size("fsdp"), lax.axis_size("context")
    core = lambda i: i + 1 - 2 * lax.rem(i, 2)
    far = lambda i: i + 2 - 4 * lax.rem(lax.div(i, 2), 2)
    up = lambda i: lax.rem(i + 4, n)
    down = lambda i: lax.rem(i + n - 4, n)
    nxt, prv = lax.rem(c + 1, m), lax.rem(c + m - 1, m)
    F = lambda i: {"fsdp": i}
    C = lambda i: {"context": i}
    meet([F(core(f)), F(far(f)), F(up(f)), F(down(f)), C(nxt), C(prv)])
    own = pltpu.make_async_copy(x_ref, w_ref.at[pl.ds(f * shard, shard)], local.at[0])
    own.start()
    own2 = pltpu.make_async_copy(y_ref, g_ref.at[pl.ds(c * rows, rows)], local.at[1])
    own2.start()
    half = shard // 2
    started = []
    def push(k, ref, at, size, to, src=None):
        win = ref.at[pl.ds(pl.multiple_of(at, 16), size)]
        cp = pltpu.make_async_remote_copy(win if src is None else src, win, send.at[k], recv.at[k],
                                          device_id=to, device_id_type=MESH)
        cp.start(); started.append(cp)
    def land(k, ref, at, size, like):
        win = ref.at[pl.ds(pl.multiple_of(at, 16), size)]
        pltpu.make_async_remote_copy(win, win, send.at[k], recv.at[k], device_id=like, device_id_type=MESH).wait_recv()
    push(0, w_ref, f * shard, shard, F(far(f)), x_ref)
    push(1, w_ref, f * shard, shard, F(up(f)), x_ref)
    push(2, w_ref, f * shard, shard, F(down(f)), x_ref)
    push(20, g_ref, c * rows, rows, C(nxt), y_ref)
    push(21, g_ref, c * rows, rows, C(prv), y_ref)
    push(3, w_ref, f * shard, shard, F(core(f)), x_ref)
    p = far(f)
    land(0, w_ref, p * shard, shard, F(p))
    push(4, w_ref, p * shard, shard, F(up(f)))
    push(5, w_ref, p * shard, shard, F(down(f)))
    push(6, w_ref, p * shard, shard, F(core(f)))
    a, b = down(f), up(f)
    land(1, w_ref, a * shard, shard, F(a))
    push(7, w_ref, a * shard, half, F(up(f)))
    push(8, w_ref, a * shard, shard, F(core(f)))
    land(2, w_ref, b * shard, shard, F(b))
    push(9, w_ref, b * shard + half, half, F(down(f)))
    push(10, w_ref, b * shard, shard, F(core(f)))
    hr = rows // 2
    land(20, g_ref, prv * rows, rows, C(prv))
    push(22, g_ref, prv * rows, hr, C(nxt))
    land(21, g_ref, nxt * rows, rows, C(nxt))
    push(23, g_ref, nxt * rows + hr, hr, C(prv))
    a2, b2 = far(a), far(b)
    land(4, w_ref, a2 * shard, shard, F(a))
    push(11, w_ref, a2 * shard, half, F(up(f)))
    push(12, w_ref, a2 * shard, shard, F(core(f)))
    land(5, w_ref, b2 * shard, shard, F(b))
    push(13, w_ref, b2 * shard + half, half, F(down(f)))
    push(14, w_ref, b2 * shard, shard, F(core(f)))
    o = lax.rem(f + 8, n); o2 = far(o)
    land(7, w_ref, o * shard, half, F(a))
    push(15, w_ref, o * shard, half, F(core(f)))
    land(9, w_ref, o * shard + half, half, F(b))
    push(16, w_ref, o * shard + half, half, F(core(f)))
    land(11, w_ref, o2 * shard, half, F(a))
    push(17, w_ref, o2 * shard, half, F(core(f)))
    land(13, w_ref, o2 * shard + half, half, F(b))
    push(18, w_ref, o2 * shard + half, half, F(core(f)))
    s = core(f)
    sib = F(s)
    land(3, w_ref, s * shard, shard, sib)
    land(6, w_ref, far(s) * shard, shard, sib)
    land(8, w_ref, down(s) * shard, shard, sib)
    land(10, w_ref, up(s) * shard, shard, sib)
    land(12, w_ref, far(down(s)) * shard, shard, sib)
    land(14, w_ref, far(up(s)) * shard, shard, sib)
    so = lax.rem(s + 8, n)
    land(15, w_ref, so * shard, half, sib)
    land(16, w_ref, so * shard + half, half, sib)
    land(17, w_ref, far(so) * shard, half, sib)
    land(18, w_ref, far(so) * shard + half, half, sib)
    cf = lax.rem(c + 2, m)
    land(22, g_ref, cf * rows, hr, C(prv))
    land(23, g_ref, cf * rows + hr, hr, C(nxt))
    for cp in started: cp.wait_send()
    own.wait(); own2.wait()

def gather(x, y, cid=1):
    shard, cols = x.shape; rows, width = y.shape
    return pl.pallas_call(gather_kernel,
        out_shape=(jax.ShapeDtypeStruct((16*shard, cols), x.dtype), jax.ShapeDtypeStruct((4*rows, width), y.dtype)),
        in_specs=[ANY]*2, out_specs=(ANY, ANY),
        scratch_shapes=[pltpu.SemaphoreType.DMA((24,)), pltpu.SemaphoreType.DMA((24,)), pltpu.SemaphoreType.DMA((2,))],
        compiler_params=pltpu.CompilerParams(collective_id=cid, has_side_effects=True), name="gather_rows")(x, y)

def norm_kernel(part_ref, x_ref, gain_ref, mid_ref, out_ref, other, normed, send, recv, local):
    rows = part_ref.shape[0]
    chunks = 4
    size = rows // chunks
    half = size // 2
    c = lax.axis_index("context"); m = lax.axis_size("context")
    nxt, prv, cf = lax.rem(c + 1, m), lax.rem(c + m - 1, m), lax.rem(c + 2, m)
    T = {"tensor": 1 - lax.axis_index("tensor")}
    C = lambda i: {"context": i}
    meet([T, C(nxt), C(prv)])
    def copy(src, dst, k, to):
        return pltpu.make_async_remote_copy(src, dst, send.at[k], recv.at[k], device_id=to, device_id_type=MESH)
    def rows_of(owner, at, n):
        return out_ref.at[pl.ds(pl.multiple_of(owner * rows + at, 16), n)]
    started = []
    for k in range(chunks):
        at = pl.ds(k * size, size)
        cp = copy(part_ref.at[at], other.at[at], k, T); cp.start(); started.append(cp)
    locals_ = []
    def forward(k):
        a = rows_of(prv, k * size, size)
        copy(a, a, chunks + k, C(prv)).wait_recv()
        w = rows_of(prv, k * size, half)
        cp = copy(w, w, 3 * chunks + k, C(nxt)); cp.start(); started.append(cp)
        a = rows_of(nxt, k * size, size)
        copy(a, a, 2 * chunks + k, C(nxt)).wait_recv()
        w = rows_of(nxt, k * size + half, half)
        cp = copy(w, w, 4 * chunks + k, C(prv)); cp.start(); started.append(cp)
    for k in range(chunks):
        at = pl.ds(k * size, size)
        started[k].wait_recv()
        mid = x_ref[at].astype(f32) + (part_ref[at].astype(f32) + other[at].astype(f32))
        mid_ref[at] = mid
        r = lax.rsqrt(jnp.mean(mid * mid, axis=-1, keepdims=True) + EPSILON)
        normed[at] = (mid * r * gain_ref[...]).astype(bf16)
        lc = pltpu.make_async_copy(normed.at[at], rows_of(c, k * size, size), local.at[k]); lc.start(); locals_.append(lc)
        for d, to in ((0, nxt), (1, prv)):
            cp = copy(normed.at[at], rows_of(c, k * size, size), (1 + d) * chunks + k, C(to)); cp.start(); started.append(cp)
        if k:
            forward(k - 1)
    forward(chunks - 1)
    for k in range(chunks):
        w = rows_of(cf, k * size, half); copy(w, w, 3 * chunks + k, C(prv)).wait_recv()
        w = rows_of(cf, k * size + half, half); copy(w, w, 4 * chunks + k, C(nxt)).wait_recv()
    for cp in started: cp.wait_send()
    for lc in locals_: lc.wait()

def norm_gather(part, x, gain, cid=2):
    rows, width = x.shape
    return pl.pallas_call(norm_kernel,
        out_shape=(jax.ShapeDtypeStruct((rows, width), f32), jax.ShapeDtypeStruct((4 * rows, width), bf16)),
        in_specs=[VM] * 3, out_specs=(VM, ANY),
        scratch_shapes=[pltpu.VMEM((rows, width), bf16), pltpu.VMEM((rows, width), bf16),
                        pltpu.SemaphoreType.DMA((20,)), pltpu.SemaphoreType.DMA((20,)), pltpu.SemaphoreType.DMA((4,))],
        compiler_params=pltpu.CompilerParams(collective_id=cid, has_side_effects=True), name="norm_gather")(part, x, gain[None])

class Wire:
    def __init__(self, send, recv):
        self.send, self.recv, self.used, self.started = send, recv, 0, []

    def push(self, src, dst, to):
        k = self.used
        self.used += 1
        copy = pltpu.make_async_remote_copy(
            src, dst, self.send.at[k], self.recv.at[k], device_id=to, device_id_type=MESH
        )
        copy.start()
        self.started.append(copy)
        return copy

    def sent(self, *copies):
        for copy in copies:
            copy.wait_send()
            self.started = [other for other in self.started if other is not copy]

    def drain(self):
        self.sent(*list(self.started))


class Loads:
    def __init__(self, sems):
        self.sems, self.used = sems, 0

    def start(self, src, dst):
        copy = pltpu.make_async_copy(src, dst, self.sems.at[self.used])
        self.used += 1
        copy.start()
        return copy


def along_context():
    c, m = lax.axis_index("context"), lax.axis_size("context")
    return c, lax.rem(c + 1, m), lax.rem(c + m - 1, m), lax.rem(c + 2, m)


def along_fsdp():
    f, n = lax.axis_index("fsdp"), lax.axis_size("fsdp")
    core = f + 1 - 2 * lax.rem(f, 2)
    far = f + 2 - 4 * lax.rem(lax.div(f, 2), 2)
    return f, core, far, lax.rem(f + 4, n), lax.rem(f + n - 4, n)


class RowSum:
    def __init__(self, wire, part, from_prv, from_nxt, mine, other, chunks):
        self.wire, self.part, self.chunks = wire, part, chunks
        self.from_prv, self.from_nxt, self.mine, self.other = from_prv, from_nxt, mine, other
        self.rows, self.width = mine.shape
        self.half = self.rows // 2
        self.c, self.nxt, self.prv, self.cf = along_context()
        self.relays, self.plains, self.mores, self.swaps = {}, {}, {}, {}

    def cols(self, k):
        size = self.width // self.chunks
        return pl.ds(k * size, size)

    def win(self, owner, second, k):
        at = pl.multiple_of(owner * self.rows + second * self.half, 16)
        return pl.ds(at, self.half), self.cols(k)

    def start(self):
        up, down = {"context": self.nxt}, {"context": self.prv}
        part, push = self.part, self.wire.push
        for k in range(self.chunks):
            cols = self.cols(k)
            self.relays[k] = (
                push(part.at[self.win(self.cf, 0, k)], self.from_prv.at[0, :, cols], up),
                push(part.at[self.win(self.cf, 1, k)], self.from_nxt.at[0, :, cols], down),
            )
        for k in range(self.chunks):
            cols = self.cols(k)
            self.plains[k] = (
                push(part.at[self.win(self.nxt, 1, k)], self.from_prv.at[1, :, cols], up),
                push(part.at[self.win(self.prv, 0, k)], self.from_nxt.at[1, :, cols], down),
            )

    def relay(self, k):
        cols, push = self.cols(k), self.wire.push
        self.relays[k][0].wait_recv()
        self.from_prv[0, :, cols] = (
            self.from_prv[0, :, cols].astype(f32) + self.part[self.win(self.nxt, 0, k)].astype(f32)
        ).astype(bf16)
        one = push(self.from_prv.at[0, :, cols], self.from_prv.at[2, :, cols], {"context": self.nxt})
        self.relays[k][1].wait_recv()
        self.from_nxt[0, :, cols] = (
            self.from_nxt[0, :, cols].astype(f32) + self.part[self.win(self.prv, 1, k)].astype(f32)
        ).astype(bf16)
        two = push(self.from_nxt.at[0, :, cols], self.from_nxt.at[2, :, cols], {"context": self.prv})
        self.mores[k] = (one, two)

    def exchange(self, k):
        cols, half = self.cols(k), self.half
        self.plains[k][1].wait_recv()
        self.mores[k][0].wait_recv()
        first = (
            self.part[self.win(self.c, 0, k)].astype(f32)
            + self.from_nxt[1, :, cols].astype(f32)
            + self.from_prv[2, :, cols].astype(f32)
        )
        self.mine[pl.ds(0, half), cols] = first.astype(bf16)
        self.plains[k][0].wait_recv()
        self.mores[k][1].wait_recv()
        second = (
            self.part[self.win(self.c, 1, k)].astype(f32)
            + self.from_prv[1, :, cols].astype(f32)
            + self.from_nxt[2, :, cols].astype(f32)
        )
        self.mine[pl.ds(half, half), cols] = second.astype(bf16)
        to = {"tensor": 1 - lax.axis_index("tensor")}
        self.swaps[k] = self.wire.push(self.mine.at[:, cols], self.other.at[:, cols], to)

    def landed(self):
        for k in range(self.chunks):
            self.swaps[k].wait_recv()

    def total(self, rows):
        return self.mine[rows, :].astype(f32) + self.other[rows, :].astype(f32)


class ShardSum:
    def __init__(self, wire, both, came, from_down, from_up, pair, last, ranges):
        self.wire, self.both, self.came = wire, both, came
        self.from_down, self.from_up = from_down, from_up
        self.pair, self.last, self.ranges = pair, last, ranges
        self.shard = both.shape[2]
        self.half = self.shard // 2
        self.f, self.core, self.far, self.up, self.down = along_fsdp()
        self.side = lax.rem(lax.div(self.f, 2), 2)
        self.mine = lax.rem(self.f, 2)
        self.z = lax.div(self.f, 4)
        self.cores, self.plain, self.relay, self.more, self.cross = {}, {}, {}, {}, {}

    def cols(self, k):
        return pl.ds(*self.ranges[k])

    def block_cols(self, rel):
        size = 4 * self.shard
        return pl.ds(pl.multiple_of(lax.rem(self.z + rel, 4) * size, 128), size)

    def multiply(self, k, rel, left, right):
        tile = lax.dot_general(
            left, right, (((0,), (0,)), ((), ())), preferred_element_type=f32
        ).astype(bf16)
        cols = self.cols(k)
        for side in range(2):
            for core in range(2):
                lo = (2 * side + core) * self.shard
                place = lax.rem(core + self.mine, 2)
                self.both[place, 2 * rel + side, :, cols] = tile[lo : lo + self.shard]
        self.cores[k, rel] = self.wire.push(
            self.both.at[1, pl.ds(2 * rel, 2), :, cols],
            self.came.at[pl.ds(2 * rel, 2), :, cols],
            {"fsdp": self.core},
        )

    def block(self, rel, second, k):
        return pl.ds(2 * rel, 2), pl.ds(second * self.half, self.half), self.cols(k)

    def add_core(self, k, rel):
        self.cores[k, rel].wait_recv()
        at = pl.ds(2 * rel, 2), slice(None), self.cols(k)
        mine = (0,) + at
        self.both[mine] = (self.both[mine].astype(f32) + self.came[at].astype(f32)).astype(bf16)

    def start(self, k):
        got, cols, push = self.both.at[0], self.cols(k), self.wire.push
        up, down = {"fsdp": self.up}, {"fsdp": self.down}
        self.add_core(k, 2)
        self.relay[k] = (
            push(got.at[self.block(2, 0, k)], self.from_down.at[0, :, :, cols], up),
            push(got.at[self.block(2, 1, k)], self.from_up.at[0, :, :, cols], down),
        )
        self.add_core(k, 1)
        self.add_core(k, 3)
        self.plain[k] = (
            push(got.at[self.block(1, 1, k)], self.from_down.at[1, :, :, cols], up),
            push(got.at[self.block(3, 0, k)], self.from_up.at[1, :, :, cols], down),
        )
        self.add_core(k, 0)

    def relays(self, k):
        got, cols, push = self.both.at[0], self.cols(k), self.wire.push
        self.relay[k][0].wait_recv()
        at = (0, slice(None), slice(None), cols)
        self.from_down[at] = (
            self.from_down[at].astype(f32) + got[self.block(1, 0, k)].astype(f32)
        ).astype(bf16)
        one = push(self.from_down.at[at], self.from_down.at[2, :, :, cols], {"fsdp": self.up})
        self.relay[k][1].wait_recv()
        self.from_up[at] = (
            self.from_up[at].astype(f32) + got[self.block(3, 1, k)].astype(f32)
        ).astype(bf16)
        two = push(self.from_up.at[at], self.from_up.at[2, :, :, cols], {"fsdp": self.down})
        self.more[k] = (one, two)

    def across(self, k):
        got, cols, half = self.both.at[0], self.cols(k), self.half
        self.more[k][0].wait_recv()
        self.plain[k][1].wait_recv()
        self.pair[:, pl.ds(0, half), cols] = (
            got[self.block(0, 0, k)].astype(f32)
            + self.from_down[2, :, :, cols].astype(f32)
            + self.from_up[1, :, :, cols].astype(f32)
        ).astype(bf16)
        self.more[k][1].wait_recv()
        self.plain[k][0].wait_recv()
        self.pair[:, pl.ds(half, half), cols] = (
            got[self.block(0, 1, k)].astype(f32)
            + self.from_down[1, :, :, cols].astype(f32)
            + self.from_up[2, :, :, cols].astype(f32)
        ).astype(bf16)
        self.cross[k] = self.wire.push(
            self.pair.at[1 - self.side, :, cols], self.last.at[:, cols], {"fsdp": self.far}
        )

    def total(self, k):
        cols = self.cols(k)
        self.cross[k].wait_recv()
        return self.pair[self.side, :, cols].astype(f32) + self.last[:, cols].astype(f32)


def row_scratch(rows, width):
    return [pltpu.VMEM((3, rows // 2, width), bf16)] * 2 + [pltpu.VMEM((rows, width), bf16)] * 2


def everyone_near():
    _, core, far, up, down = along_fsdp()
    _, nxt, prv, _ = along_context()
    return [{"fsdp": i} for i in (core, far, up, down)] + [
        {"context": nxt}, {"context": prv}, {"tensor": 1 - lax.axis_index("tensor")}
    ]


def half_turn(x):
    return pltpu.roll(x, HD // 2, 1)


def signal(sem, to):
    pl.semaphore_signal(sem, inc=1, device_id=to, device_id_type=MESH)


ORDER = (2, 1, 3, 0)
SMALL = (8, 512)


def layer_back_kernel(
    normed_hbm, dy_hbm, gate_hbm, lift_hbm, hidden_hbm, first_hbm, second_hbm,
    out_hbm, lin_hbm, probs_hbm,
    middle_ref, dy_ref, gain_two_ref, mixed_ref, query_ref, key_ref, value_ref,
    normed_one_ref, tokens_ref, gain_one_ref, cos_ref, sin_ref,
    result_ref, gt_ref, small_ref, attn_ref, mlp_hbm,
    part, from_prv, from_nxt, mine, other,
    left, right, both, came, from_down, from_up, pair, last, shard_out,
    probs, d_middle, d_branch, d_mixed, acc_k, acc_v, kv_send, kv_came,
    d_lin, swap_mine, swap_other, attn_own, attn_came, small_own, small_came,
    send, recv, local, free,
):
    wire, loads = Wire(send, recv), Loads(local)
    rows, width = middle_ref.shape
    group = part.shape[0]
    q_cols, kv_cols = mixed_ref.shape[1], key_ref.shape[1]
    heads = q_cols // HD
    span = hidden_hbm.shape[1]
    scale = HD ** (-0.5)
    c, nxt, prv, cf = along_context()
    f, core, far, up, down = along_fsdp()
    C = lambda i: {"context": i}
    F = lambda i: {"fsdp": i}
    T = {"tensor": 1 - lax.axis_index("tensor")}

    def keep_small(at, values):
        for k in range(values.shape[1] // SMALL[1]):
            small_own[pl.ds(at + k, 1), :] = values[:, k * SMALL[1] : (k + 1) * SMALL[1]]

    load_part = loads.start(first_hbm, part)
    load_left = loads.start(normed_hbm, left)
    load_r0 = loads.start(gate_hbm, right.at[0])
    load_r1 = loads.start(lift_hbm, right.at[1])
    opposite = lax.rem(f + 8, lax.axis_size("fsdp"))
    meet(everyone_near() + [C(cf), F(opposite)])

    one = RowSum(wire, part, from_prv, from_nxt, mine, other, 3)
    two = RowSum(wire, part, from_prv, from_nxt, mine, other, 3)
    mlp = ShardSum(wire, both, came, from_down, from_up, pair, last, [(k * span, span) for k in range(3)])
    attn = ShardSum(
        wire, both, came, from_down, from_up, pair, last,
        [(0, q_cols), (q_cols, q_cols), (2 * q_cols, 2 * kv_cols)],
    )
    load_part.wait()
    one.start()

    load_left.wait()
    load_r0.wait()
    for rel in ORDER:
        mlp.multiply(0, rel, left[:, mlp.block_cols(rel)], right[0])
    load_r0 = loads.start(hidden_hbm, right.at[0])
    load_r1.wait()
    for rel in ORDER:
        mlp.multiply(1, rel, left[:, mlp.block_cols(rel)], right[1])
    load_left = loads.start(dy_hbm, left)
    for k in range(3):
        one.relay(k)
    mlp.start(0)
    load_r0.wait()
    load_left.wait()
    for rel in ORDER:
        mlp.multiply(2, rel, left[:, mlp.block_cols(rel)], right[0])
    deep = left.shape[0]
    rest = width - deep
    load_out = (
        loads.start(out_hbm.at[pl.ds(0, deep)], left.at[:, pl.ds(0, q_cols)]),
        loads.start(out_hbm.at[pl.ds(deep, rest)], left.at[pl.ds(0, rest), pl.ds(q_cols, q_cols)]),
    )
    lin_cols = lin_hbm.shape[1]
    load_lin = (
        loads.start(lin_hbm.at[pl.ds(0, deep)], right.at[0, :, pl.ds(0, lin_cols)]),
        loads.start(lin_hbm.at[pl.ds(deep, rest)], right.at[1, pl.ds(0, rest), pl.ds(0, lin_cols)]),
    )
    load_probs = {h: loads.start(probs_hbm.at[h], probs.at[h % 2]) for h in range(2)}
    mlp.start(1)
    one.exchange(0)
    one.exchange(1)
    mlp.start(2)
    one.exchange(2)
    signal(free.at[0], F(core))
    for k in range(3):
        wire.sent(*one.relays[k], *one.plains[k], *one.mores[k])
    signal(free.at[1], C(nxt))
    signal(free.at[2], C(prv))
    load_part = loads.start(second_hbm, part)
    mlp.relays(0)
    mlp.relays(1)
    one.landed()

    sizes = 64
    gain_grad = jnp.zeros((1, width), f32)
    for at in range(0, rows, sizes):
        at = pl.ds(at, sizes)
        grad, mid = one.total(at), middle_ref[at, :]
        r = lax.rsqrt(jnp.mean(mid * mid, axis=-1, keepdims=True) + EPSILON)
        gain_grad += jnp.sum(grad * mid * r, axis=0, keepdims=True)
        scaled = grad * gain_two_ref[...]
        back = jnp.mean(scaled * mid, axis=-1, keepdims=True)
        value = dy_ref[at, :].astype(f32) + r * scaled - mid * (r * r * r * back)
        d_middle[at, :] = value
        d_branch[at, :] = value.astype(bf16)
    keep_small(3, gain_grad)
    wire.sent(*one.swaps.values())
    signal(free.at[3], T)
    load_part.wait()
    pl.semaphore_wait(free.at[1], 1)
    pl.semaphore_wait(free.at[2], 1)
    two.start()
    mlp.relays(2)

    for copy in load_out:
        copy.wait()
    d_mixed[...] = (
        jnp.dot(d_branch[:, pl.ds(0, deep)], left[:, pl.ds(0, q_cols)], preferred_element_type=f32)
        + jnp.dot(
            d_branch[:, pl.ds(deep, rest)], left[pl.ds(0, rest), pl.ds(q_cols, q_cols)],
            preferred_element_type=f32,
        )
    ).astype(bf16)
    lane = lax.broadcasted_iota(jnp.int32, (1, HD), 1)
    sign = jnp.where(lane < HD // 2, 1.0, -1.0).astype(f32)

    def turn_back(w):
        return w * cos_ref[...] + half_turn(w * sin_ref[...]) * sign

    nt = (((1,), (1,)), ((), ()))
    tn = (((0,), (0,)), ((), ()))

    def head(h):
        cols = pl.ds(h * HD, HD)
        load_probs[h].wait()
        p = probs[h % 2]
        dm = d_mixed[:, cols]
        dp = lax.dot_general(dm, value_ref[...], nt, preferred_element_type=f32)
        inner = jnp.sum(p * dp, axis=-1, keepdims=True)
        ds = (p * (dp - inner)).astype(bf16)
        dq = jnp.dot(ds, key_ref[...], preferred_element_type=f32) * scale
        d_lin[:, cols] = turn_back(dq).astype(bf16)
        dk = lax.dot_general(ds, query_ref[:, cols], tn, preferred_element_type=f32)
        dv = lax.dot_general(p.astype(bf16), dm, tn, preferred_element_type=f32)
        if h == 0:
            acc_k[...] = dk
            acc_v[...] = dv
        else:
            acc_k[...] += dk
            acc_v[...] += dv
        if h + 2 < heads:
            load_probs[h + 2] = loads.start(probs_hbm.at[h + 2], probs.at[h % 2])

    head(0)
    mlp.across(0)
    head(1)
    mlp.across(1)
    for k in range(3):
        two.relay(k)
    head(2)
    mlp.across(2)
    for k in range(3):
        wire.sent(*mlp.more[k])
    signal(free.at[4], F(up))
    signal(free.at[5], F(down))
    head(3)
    for k in range(3):
        shard_out[:, mlp.cols(k)] = mlp.total(k).astype(bf16)
    signal(free.at[6], F(far))
    spread = [
        wire.push(shard_out, mlp_hbm.at[c], C(nxt)),
        wire.push(shard_out, mlp_hbm.at[c], C(prv)),
    ]
    keep = loads.start(shard_out, mlp_hbm.at[c])
    head(4)
    pl.semaphore_wait(free.at[3], 1)
    for k in range(3):
        two.exchange(k)
    head(5)

    for k in range(4):
        kv_send[k, 0] = acc_k[pl.ds(k * rows, rows), :].astype(bf16)
        kv_send[k, 1] = acc_v[pl.ds(k * rows, rows), :].astype(bf16)
    kv = [
        wire.push(kv_send.at[nxt], kv_came.at[0], C(nxt)),
        wire.push(kv_send.at[prv], kv_came.at[1], C(prv)),
        wire.push(kv_send.at[cf], kv_came.at[2], C(cf)),
    ]
    for k in range(3):
        wire.sent(*[mlp.cores[k, rel] for rel in ORDER], *mlp.relay[k], *mlp.plain[k], mlp.cross[k])
    pl.semaphore_wait(free.at[0], 1)
    for rel in ORDER:
        attn.multiply(0, rel, d_branch[:, attn.block_cols(rel)], mixed_ref[...])
    for rel in ORDER:
        attn.multiply(1, rel, normed_one_ref[:, attn.block_cols(rel)], d_lin[:, pl.ds(0, q_cols)])
    for copy in kv:
        copy.wait_recv()
    d_key = acc_k[pl.ds(pl.multiple_of(c * rows, 8), rows), :]
    d_value = acc_v[pl.ds(pl.multiple_of(c * rows, 8), rows), :]
    for k in range(3):
        d_key += kv_came[k, 0].astype(f32)
        d_value += kv_came[k, 1].astype(f32)
    d_lin[:, pl.ds(q_cols, kv_cols)] = turn_back(d_key * scale).astype(bf16)
    d_lin[:, pl.ds(q_cols + kv_cols, kv_cols)] = d_value.astype(bf16)
    for copy in load_lin:
        copy.wait()
    swap_mine[:, pl.ds(0, deep)] = lax.dot_general(
        d_lin[...], right[0, :, pl.ds(0, lin_cols)], nt, preferred_element_type=f32
    ).astype(bf16)
    swap_mine[:, pl.ds(deep, rest)] = lax.dot_general(
        d_lin[...], right[1, pl.ds(0, rest), pl.ds(0, lin_cols)], nt, preferred_element_type=f32
    ).astype(bf16)
    swap = wire.push(swap_mine, swap_other, T)
    for rel in ORDER:
        attn.multiply(
            2, rel, normed_one_ref[:, attn.block_cols(rel)], d_lin[:, pl.ds(q_cols, 2 * kv_cols)]
        )
    pl.semaphore_wait(free.at[4], 1)
    pl.semaphore_wait(free.at[5], 1)
    for k in range(3):
        attn.start(k)
    keep_small(6, jnp.sum(d_lin[...].astype(f32), axis=0, keepdims=True))
    half = shard_out.shape[0] // 2
    spread[0].wait_recv()
    w = mlp_hbm.at[prv, pl.ds(0, half)]
    spread.append(wire.push(w, w, C(nxt)))
    spread[1].wait_recv()
    w = mlp_hbm.at[nxt, pl.ds(half, half)]
    spread.append(wire.push(w, w, C(prv)))
    two.landed()
    for at in range(0, rows, sizes):
        at = pl.ds(at, sizes)
        result_ref[at, :] = (middle_ref[at, :] + two.total(at)).astype(bf16)
    for k in range(3):
        attn.relays(k)
    pl.semaphore_wait(free.at[6], 1)
    for k in range(3):
        attn.across(k)

    swap.wait_recv()
    gain_grad = jnp.zeros((1, width), f32)
    for at in range(0, rows, sizes):
        at = pl.ds(at, sizes)
        grad = swap_mine[at, :].astype(f32) + swap_other[at, :].astype(f32)
        mid = tokens_ref[at, :].astype(f32)
        r = lax.rsqrt(jnp.mean(mid * mid, axis=-1, keepdims=True) + EPSILON)
        gain_grad += jnp.sum(grad * mid * r, axis=0, keepdims=True)
        scaled = grad * gain_one_ref[...]
        back = jnp.mean(scaled * mid, axis=-1, keepdims=True)
        gt_ref[at, :] = d_middle[at, :] + r * scaled - mid * (r * r * r * back)
    keep_small(0, gain_grad)

    for k in range(3):
        attn_own[:, attn.cols(k)] = attn.total(k).astype(bf16)
    both_ways = [
        wire.push(attn_own, attn_came.at[0], C(nxt)),
        wire.push(attn_own, attn_came.at[1], C(prv)),
    ]
    steps = [F(core), F(far), F(f + 4 - 8 * lax.rem(lax.div(f, 4), 2)), F(opposite),
             C(c + 1 - 2 * lax.rem(c, 2)), C(cf)]
    for k, to in enumerate(steps):
        copy = wire.push(small_own if k == 0 else small_came.at[2 * k - 1], small_came.at[2 * k], to)
        copy.wait_recv()
        have = small_own[...] if k == 0 else small_came[2 * k - 1]
        total = have + small_came[2 * k]
        if k == len(steps) - 1:
            small_ref[...] = total
        else:
            small_came[2 * k + 1] = total
        if k == 1:
            both_ways[0].wait_recv()
            both_ways[1].wait_recv()
            both_ways.append(
                wire.push(attn_came.at[0, pl.ds(0, half)], attn_came.at[2, pl.ds(0, half)], C(nxt))
            )
            both_ways.append(
                wire.push(attn_came.at[1, pl.ds(half, half)], attn_came.at[2, pl.ds(half, half)], C(prv))
            )
    both_ways[2].wait_recv()
    both_ways[3].wait_recv()
    own_pair = attn_own[...].astype(f32) + attn_came[2].astype(f32)
    next_pair = attn_came[0].astype(f32) + attn_came[1].astype(f32)
    attn_ref[...] = own_pair + next_pair
    spread[2].wait_recv()
    spread[3].wait_recv()
    keep.wait()
    wire.drain()


def layer_back(hbm, near, cid=4):
    normed, dy, gate, lift, hidden, first, second, out, lin, probs = hbm
    group, width = normed.shape
    rows = group // 4
    shard, span = width // 16, gate.shape[1]
    lin_cols = lin.shape[1]
    q_cols = out.shape[1]
    sems = 2 * 21 + 2 * (12 + 3 * 7) + 3 + 1 + 4 + 4 + 6
    return pl.pallas_call(
        layer_back_kernel,
        out_shape=(
            jax.ShapeDtypeStruct((rows, width), bf16),
            jax.ShapeDtypeStruct((rows, width), f32),
            jax.ShapeDtypeStruct(SMALL, f32),
            jax.ShapeDtypeStruct((shard, lin_cols + q_cols), f32),
            jax.ShapeDtypeStruct((4, shard, 3 * span), bf16),
        ),
        in_specs=[ANY] * len(hbm) + [VM] * len(near),
        out_specs=(VM, VM, VM, VM, ANY),
        scratch_shapes=[pltpu.VMEM((group, width), bf16)]
        + row_scratch(rows, width)
        + [
            pltpu.VMEM((group, width), bf16),
            pltpu.VMEM((2, group, span), bf16),
            pltpu.VMEM((2, 8, shard, 3 * span), bf16),
            pltpu.VMEM((8, shard, 3 * span), bf16),
            pltpu.VMEM((3, 2, shard // 2, 3 * span), bf16),
            pltpu.VMEM((3, 2, shard // 2, 3 * span), bf16),
            pltpu.VMEM((2, shard, 3 * span), bf16),
            pltpu.VMEM((shard, 3 * span), bf16),
            pltpu.VMEM((shard, 3 * span), bf16),
            pltpu.VMEM((2, rows, group), f32),
            pltpu.VMEM((rows, width), f32),
            pltpu.VMEM((rows, width), bf16),
            pltpu.VMEM((rows, q_cols), bf16),
            pltpu.VMEM((group, HD), f32),
            pltpu.VMEM((group, HD), f32),
            pltpu.VMEM((4, 2, rows, HD), bf16),
            pltpu.VMEM((3, 2, rows, HD), bf16),
            pltpu.VMEM((rows, lin_cols), bf16),
            pltpu.VMEM((rows, width), bf16),
            pltpu.VMEM((rows, width), bf16),
            pltpu.VMEM((shard, lin_cols + q_cols), bf16),
            pltpu.VMEM((3, shard, lin_cols + q_cols), bf16),
            pltpu.VMEM(SMALL, f32),
            pltpu.VMEM((11,) + SMALL, f32),
            pltpu.SemaphoreType.DMA((sems,)),
            pltpu.SemaphoreType.DMA((sems,)),
            pltpu.SemaphoreType.DMA((18,)),
            pltpu.SemaphoreType.REGULAR((7,)),
        ],
        compiler_params=pltpu.CompilerParams(
            collective_id=cid, has_side_effects=True, vmem_limit_bytes=63 << 20
        ),
        name="layer_back",
    )(*hbm, *near)


def rms_norm(values, gain_vec):
    return (
        values * lax.rsqrt(jnp.mean(values * values, axis=-1, keepdims=True) + EPSILON) * gain_vec
    )


def rope_tables(positions, head_width):
    half_width = head_width // 2
    freq_index = jnp.arange(half_width).astype(jnp.float32)
    inverse = ROPE_BASE ** (-(freq_index * 2.0 / head_width))
    angles = positions.astype(jnp.float32)[:, None] * inverse[None, :]
    cosine = jnp.cos(angles)
    sine_table = jnp.sin(angles)
    return (jnp.concatenate([cosine, cosine], -1), jnp.concatenate([sine_table, sine_table], -1))


def rotate(values, cosine, sine_table):
    half_width = values.shape[-1] // 2
    turned = jnp.concatenate([-values[..., half_width:], values[..., :half_width]], -1)
    return values * cosine[:, None, :] + turned * sine_table[:, None, :]


def segment_info(seq_lengths, total_rows):
    ends_at = jnp.cumsum(seq_lengths)
    places = jnp.arange(total_rows, dtype=jnp.int32)
    passed = places[:, None] >= ends_at[None, :]
    segment = jnp.sum(passed.astype(jnp.int32), axis=1)
    starts = jnp.sum(jnp.where(passed, seq_lengths[None, :], 0), axis=1)
    return (segment, places - starts)


def lead_dot(left, right):
    return lax.dot_general(
        left, right, (((0,), (0,)), ((), ())), preferred_element_type=jnp.float32
    )


def tail_dot(left, right):
    return lax.dot_general(
        left, right, (((1,), (1,)), ((), ())), preferred_element_type=jnp.float32
    )


def around(x):
    size, rank = lax.axis_size("context"), lax.axis_index("context")
    parts = [x] + [
        lax.ppermute(x, "context", [(i, (i - k) % size) for i in range(size)]) for k in range(1, size)
    ]
    twice = jnp.concatenate(parts + parts, axis=0)
    rows = x.shape[0]
    return lax.dynamic_slice_in_dim(twice, (size - rank) % size * rows, size * rows)


def hidden_range(width, parts, rank):
    tiles = width // 128
    span = -(-tiles // parts) * 128
    start = jnp.minimum(rank * span, width - span)
    return span, pl.multiple_of(start, 128), parts * span - width


def on_device(
    tokens,
    cotangent,
    lengths,
    gain_attn,
    w_query,
    b_query,
    w_key,
    b_key,
    w_value,
    b_value,
    w_out,
    gain_mlp,
    w_gate,
    w_up,
    w_down,
):
    row_count, width = tokens.shape
    context_size = lax.axis_size("context")
    context_rank = lax.axis_index("context")
    fsdp_rank = lax.axis_index("fsdp")
    shard = w_query.shape[0]
    query_cols, kv_cols, hidden_cols = w_query.shape[1], w_key.shape[1], w_gate.shape[1]
    heads_kv = kv_cols // HD
    heads_query = query_cols // HD
    per_group = heads_query // heads_kv
    score_scale = HD ** (-0.5)
    group_rows = row_count * context_size
    segment_all, position_all = segment_info(lengths[0], group_rows)
    first_row = context_rank * row_count
    segment_mine = lax.dynamic_slice_in_dim(segment_all, first_row, row_count)
    position_mine = lax.dynamic_slice_in_dim(position_all, first_row, row_count)
    query_at = first_row + jnp.arange(row_count, dtype=jnp.int32)
    key_at = jnp.arange(group_rows, dtype=jnp.int32)
    allowed = (segment_mine[:, None] == segment_all[None, :]) & (
        key_at[None, :] <= query_at[:, None]
    )
    cosine, sine_table = rope_tables(position_mine, HD)

    span, start, overlap = hidden_range(hidden_cols, context_size, context_rank)
    gains = jnp.pad(jnp.stack([gain_attn, gain_mlp], axis=1), ((0, 0), (0, 126)))
    attn_pack = jnp.concatenate([w_query, w_key, w_value, w_out.T, gains], axis=1)
    mlp_pack = jnp.concatenate(
        [lax.dynamic_slice_in_dim(w, start, span, axis=1) for w in (w_gate, w_up, w_down.T)], axis=1
    )
    attn_full, dy_group = gather(attn_pack, cotangent)
    mlp_pack, attn_full = lax.optimization_barrier((mlp_pack, attn_full))
    mlp_full = lax.all_gather(mlp_pack, "fsdp", axis=0, tiled=True)
    lin_cols = query_cols + 2 * kv_cols
    lin_full = attn_full[:, :lin_cols]
    out_turned = attn_full[:, lin_cols : lin_cols + query_cols]
    gain_one = attn_full[:, lin_cols + query_cols].astype(f32)
    gain_two = attn_full[:, lin_cols + query_cols + 1].astype(f32)
    gate_full, lift_full, down_turned = (mlp_full[:, k * span : (k + 1) * span] for k in range(3))
    keep = (
        jnp.arange(span) >= jnp.where(context_rank == context_size - 1, overlap, 0)
    )[None, :]

    inputs = tokens.astype(f32)
    normed_one = rms_norm(inputs, gain_one).astype(bf16)
    bias = jnp.concatenate([b_query, b_key, b_value]).astype(f32)
    lin = jnp.dot(normed_one, lin_full, preferred_element_type=f32) + bias
    query_lin = lin[:, :query_cols]
    key_lin = lin[:, query_cols : query_cols + kv_cols]
    value_lin = lin[:, query_cols + kv_cols :]
    query_heads = rotate(query_lin.reshape(row_count, heads_query, HD), cosine, sine_table).astype(bf16)
    query_heads = query_heads.reshape(row_count, heads_kv, per_group, HD)
    key_heads = rotate(key_lin.reshape(row_count, heads_kv, HD), cosine, sine_table).astype(bf16)
    value_heads = value_lin.astype(bf16).reshape(row_count, heads_kv, HD)
    kv_group = around(jnp.concatenate([key_heads, value_heads], axis=1))
    key_group, value_group = kv_group[:, :heads_kv], kv_group[:, heads_kv:]
    scores = (
        jnp.einsum("qgjd,kgd->gjqk", query_heads, key_group, preferred_element_type=f32)
        * score_scale
    )
    scores = jnp.where(allowed, scores, -1e30)
    row_top = jnp.max(scores, axis=-1, keepdims=True)
    expo = jnp.exp(scores - row_top)
    probs = expo / jnp.sum(expo, axis=-1, keepdims=True)
    probs_low = probs.astype(bf16)
    mixed = jnp.einsum("gjqk,kgd->qgjd", probs_low, value_group, preferred_element_type=f32)
    mixed = mixed.reshape(row_count, heads_query * HD).astype(bf16)

    middle, normed_group = norm_gather(tail_dot(mixed, out_turned).astype(bf16), tokens, gain_two)
    d_hidden = jnp.dot(dy_group, down_turned, preferred_element_type=f32)
    gate_lin = jnp.dot(normed_group, gate_full, preferred_element_type=f32)
    lift_lin = jnp.dot(normed_group, lift_full, preferred_element_type=f32)
    sigmoid_gate = jax.nn.sigmoid(gate_lin)
    swish = gate_lin * sigmoid_gate
    hidden = jnp.where(keep, swish * lift_lin, 0.0).astype(bf16)
    d_gate = jnp.where(
        keep, d_hidden * lift_lin * sigmoid_gate * (1.0 + gate_lin * (1.0 - sigmoid_gate)), 0.0
    ).astype(bf16)
    d_lift = jnp.where(keep, d_hidden * swish, 0.0).astype(bf16)
    d_normed_part = tail_dot(d_gate, gate_full) + tail_dot(d_lift, lift_full)
    mlp_part = tail_dot(hidden, down_turned).astype(bf16)
    result, grad_tokens, small, attn_shard, mlp_all = layer_back(
        (
            normed_group, dy_group, d_gate, d_lift, hidden, d_normed_part.astype(bf16), mlp_part,
            out_turned, lin_full, probs.reshape(heads_query, row_count, group_rows),
        ),
        (
            middle, cotangent, gain_two[None], mixed, query_heads.reshape(row_count, query_cols),
            key_group.reshape(group_rows, kv_cols), value_group.reshape(group_rows, kv_cols),
            normed_one, tokens, gain_one[None], cosine, sine_table,
        ),
    )

    def whole(k):
        parts = [mlp_all[i, :, k * span : (k + 1) * span] for i in range(context_size)]
        parts[-1] = parts[-1][:, overlap:]
        return jnp.concatenate(parts, axis=1).astype(f32)

    small = small.reshape(-1)
    own = lambda at: lax.dynamic_slice_in_dim(small, at + fsdp_rank * shard, shard)
    bias_total = small[2 * width :]
    at_query = query_cols
    at_key = at_query + query_cols
    at_value = at_key + kv_cols
    return (
        result,
        grad_tokens,
        own(0),
        attn_shard[:, at_query:at_key],
        bias_total[:query_cols],
        attn_shard[:, at_key:at_value],
        bias_total[query_cols : query_cols + kv_cols],
        attn_shard[:, at_value:],
        bias_total[query_cols + kv_cols :],
        attn_shard[:, :query_cols].T,
        own(width),
        whole(0),
        whole(1),
        whole(2).T,
    )


def solution(mesh):
    return jax.shard_map(
        on_device,
        mesh=mesh,
        in_specs=(
            P(("fsdp", "context"), None),
            P(("fsdp", "context"), None),
            P("fsdp", None),
            P("fsdp"),
            P("fsdp", "tensor"),
            P("tensor"),
            P("fsdp", "tensor"),
            P("tensor"),
            P("fsdp", "tensor"),
            P("tensor"),
            P("tensor", "fsdp"),
            P("fsdp"),
            P("fsdp", "tensor"),
            P("fsdp", "tensor"),
            P("tensor", "fsdp"),
        ),
        out_specs=(
            P(("fsdp", "context"), None),
            P(("fsdp", "context"), None),
            P("fsdp"),
            P("fsdp", "tensor"),
            P("tensor"),
            P("fsdp", "tensor"),
            P("tensor"),
            P("fsdp", "tensor"),
            P("tensor"),
            P("tensor", "fsdp"),
            P("fsdp"),
            P("fsdp", "tensor"),
            P("fsdp", "tensor"),
            P("tensor", "fsdp"),
        ),
        check_vma=False,
    )
```

```python
import jax
import jax.numpy as jnp
from jax import lax
from jax.experimental import pallas as pl
from jax.experimental.pallas import tpu as pltpu
from jax.sharding import PartitionSpec as P

HD = 128
MESH = pl.DeviceIdType.MESH
ANY = pl.BlockSpec(memory_space=pl.ANY)
VM = pl.BlockSpec(memory_space=pltpu.VMEM)
f32, bf16 = jnp.float32, jnp.bfloat16

ROPE_BASE = 1000000.0
EPSILON = 1e-06

def meet(targets):
    barrier = pltpu.get_barrier_semaphore()
    for t in targets:
        pl.semaphore_signal(barrier, inc=1, device_id=t, device_id_type=MESH)
    pl.semaphore_wait(barrier, len(targets))

class Wire:
    def __init__(self, send, recv):
        self.send, self.recv, self.used, self.started = send, recv, 0, []

    def push(self, src, dst, to):
        k = self.used
        self.used += 1
        copy = pltpu.make_async_remote_copy(
            src, dst, self.send.at[k], self.recv.at[k], device_id=to, device_id_type=MESH
        )
        copy.start()
        self.started.append(copy)
        return copy

    def sent(self, *copies):
        for copy in copies:
            copy.wait_send()
            self.started = [other for other in self.started if other is not copy]

    def drain(self):
        self.sent(*list(self.started))


class Loads:
    def __init__(self, sems):
        self.sems, self.used = sems, 0

    def start(self, src, dst):
        copy = pltpu.make_async_copy(src, dst, self.sems.at[self.used])
        self.used += 1
        copy.start()
        return copy


def along_context():
    c, m = lax.axis_index("context"), lax.axis_size("context")
    return c, lax.rem(c + 1, m), lax.rem(c + m - 1, m), lax.rem(c + 2, m)


def along_fsdp():
    f, n = lax.axis_index("fsdp"), lax.axis_size("fsdp")
    core = f + 1 - 2 * lax.rem(f, 2)
    far = f + 2 - 4 * lax.rem(lax.div(f, 2), 2)
    return f, core, far, lax.rem(f + 4, n), lax.rem(f + n - 4, n)


class RowSum:
    def __init__(self, wire, part, from_prv, from_nxt, mine, other, chunks):
        self.wire, self.part, self.chunks = wire, part, chunks
        self.from_prv, self.from_nxt, self.mine, self.other = from_prv, from_nxt, mine, other
        self.rows, self.width = mine.shape
        self.half = self.rows // 2
        self.c, self.nxt, self.prv, self.cf = along_context()
        self.relays, self.plains, self.mores, self.swaps = {}, {}, {}, {}

    def cols(self, k):
        size = self.width // self.chunks
        return pl.ds(k * size, size)

    def win(self, owner, second, k):
        at = pl.multiple_of(owner * self.rows + second * self.half, 16)
        return pl.ds(at, self.half), self.cols(k)

    def start(self):
        up, down = {"context": self.nxt}, {"context": self.prv}
        part, push = self.part, self.wire.push
        for k in range(self.chunks):
            cols = self.cols(k)
            self.relays[k] = (
                push(part.at[self.win(self.cf, 0, k)], self.from_prv.at[0, :, cols], up),
                push(part.at[self.win(self.cf, 1, k)], self.from_nxt.at[0, :, cols], down),
            )
        for k in range(self.chunks):
            cols = self.cols(k)
            self.plains[k] = (
                push(part.at[self.win(self.nxt, 1, k)], self.from_prv.at[1, :, cols], up),
                push(part.at[self.win(self.prv, 0, k)], self.from_nxt.at[1, :, cols], down),
            )

    def relay(self, k):
        cols, push = self.cols(k), self.wire.push
        self.relays[k][0].wait_recv()
        self.from_prv[0, :, cols] = (
            self.from_prv[0, :, cols].astype(f32) + self.part[self.win(self.nxt, 0, k)].astype(f32)
        ).astype(bf16)
        one = push(self.from_prv.at[0, :, cols], self.from_prv.at[2, :, cols], {"context": self.nxt})
        self.relays[k][1].wait_recv()
        self.from_nxt[0, :, cols] = (
            self.from_nxt[0, :, cols].astype(f32) + self.part[self.win(self.prv, 1, k)].astype(f32)
        ).astype(bf16)
        two = push(self.from_nxt.at[0, :, cols], self.from_nxt.at[2, :, cols], {"context": self.prv})
        self.mores[k] = (one, two)

    def exchange(self, k):
        cols, half = self.cols(k), self.half
        self.plains[k][1].wait_recv()
        self.mores[k][0].wait_recv()
        first = (
            self.part[self.win(self.c, 0, k)].astype(f32)
            + self.from_nxt[1, :, cols].astype(f32)
            + self.from_prv[2, :, cols].astype(f32)
        )
        self.mine[pl.ds(0, half), cols] = first.astype(bf16)
        self.plains[k][0].wait_recv()
        self.mores[k][1].wait_recv()
        second = (
            self.part[self.win(self.c, 1, k)].astype(f32)
            + self.from_prv[1, :, cols].astype(f32)
            + self.from_nxt[2, :, cols].astype(f32)
        )
        self.mine[pl.ds(half, half), cols] = second.astype(bf16)
        to = {"tensor": 1 - lax.axis_index("tensor")}
        self.swaps[k] = self.wire.push(self.mine.at[:, cols], self.other.at[:, cols], to)

    def landed(self):
        for k in range(self.chunks):
            self.swaps[k].wait_recv()

    def total(self, rows):
        return self.mine[rows, :].astype(f32) + self.other[rows, :].astype(f32)


class ShardSum:
    def __init__(self, wire, both, came, from_down, from_up, pair, last, ranges):
        self.wire, self.both, self.came = wire, both, came
        self.from_down, self.from_up = from_down, from_up
        self.pair, self.last, self.ranges = pair, last, ranges
        self.shard = both.shape[2]
        self.half = self.shard // 2
        self.f, self.core, self.far, self.up, self.down = along_fsdp()
        self.side = lax.rem(lax.div(self.f, 2), 2)
        self.mine = lax.rem(self.f, 2)
        self.z = lax.div(self.f, 4)
        self.cores, self.plain, self.relay, self.more, self.cross = {}, {}, {}, {}, {}

    def cols(self, k):
        return pl.ds(*self.ranges[k])

    def block_cols(self, rel):
        size = 4 * self.shard
        return pl.ds(pl.multiple_of(lax.rem(self.z + rel, 4) * size, 128), size)

    def multiply(self, k, rel, left, right):
        tile = lax.dot_general(
            left, right, (((0,), (0,)), ((), ())), preferred_element_type=f32
        ).astype(bf16)
        cols = self.cols(k)
        for side in range(2):
            for core in range(2):
                lo = (2 * side + core) * self.shard
                place = lax.rem(core + self.mine, 2)
                self.both[place, 2 * rel + side, :, cols] = tile[lo : lo + self.shard]
        self.cores[k, rel] = self.wire.push(
            self.both.at[1, pl.ds(2 * rel, 2), :, cols],
            self.came.at[pl.ds(2 * rel, 2), :, cols],
            {"fsdp": self.core},
        )

    def block(self, rel, second, k):
        return pl.ds(2 * rel, 2), pl.ds(second * self.half, self.half), self.cols(k)

    def add_core(self, k, rel):
        self.cores[k, rel].wait_recv()
        at = pl.ds(2 * rel, 2), slice(None), self.cols(k)
        mine = (0,) + at
        self.both[mine] = (self.both[mine].astype(f32) + self.came[at].astype(f32)).astype(bf16)

    def start(self, k):
        got, cols, push = self.both.at[0], self.cols(k), self.wire.push
        up, down = {"fsdp": self.up}, {"fsdp": self.down}
        self.add_core(k, 2)
        self.relay[k] = (
            push(got.at[self.block(2, 0, k)], self.from_down.at[0, :, :, cols], up),
            push(got.at[self.block(2, 1, k)], self.from_up.at[0, :, :, cols], down),
        )
        self.add_core(k, 1)
        self.add_core(k, 3)
        self.plain[k] = (
            push(got.at[self.block(1, 1, k)], self.from_down.at[1, :, :, cols], up),
            push(got.at[self.block(3, 0, k)], self.from_up.at[1, :, :, cols], down),
        )
        self.add_core(k, 0)

    def relays(self, k):
        got, cols, push = self.both.at[0], self.cols(k), self.wire.push
        self.relay[k][0].wait_recv()
        at = (0, slice(None), slice(None), cols)
        self.from_down[at] = (
            self.from_down[at].astype(f32) + got[self.block(1, 0, k)].astype(f32)
        ).astype(bf16)
        one = push(self.from_down.at[at], self.from_down.at[2, :, :, cols], {"fsdp": self.up})
        self.relay[k][1].wait_recv()
        self.from_up[at] = (
            self.from_up[at].astype(f32) + got[self.block(3, 1, k)].astype(f32)
        ).astype(bf16)
        two = push(self.from_up.at[at], self.from_up.at[2, :, :, cols], {"fsdp": self.down})
        self.more[k] = (one, two)

    def across(self, k):
        got, cols, half = self.both.at[0], self.cols(k), self.half
        self.more[k][0].wait_recv()
        self.plain[k][1].wait_recv()
        self.pair[:, pl.ds(0, half), cols] = (
            got[self.block(0, 0, k)].astype(f32)
            + self.from_down[2, :, :, cols].astype(f32)
            + self.from_up[1, :, :, cols].astype(f32)
        ).astype(bf16)
        self.more[k][1].wait_recv()
        self.plain[k][0].wait_recv()
        self.pair[:, pl.ds(half, half), cols] = (
            got[self.block(0, 1, k)].astype(f32)
            + self.from_down[1, :, :, cols].astype(f32)
            + self.from_up[2, :, :, cols].astype(f32)
        ).astype(bf16)
        self.cross[k] = self.wire.push(
            self.pair.at[1 - self.side, :, cols], self.last.at[:, cols], {"fsdp": self.far}
        )

    def total(self, k):
        cols = self.cols(k)
        self.cross[k].wait_recv()
        return self.pair[self.side, :, cols].astype(f32) + self.last[:, cols].astype(f32)


def row_scratch(rows, width):
    return [pltpu.VMEM((3, rows // 2, width), bf16)] * 2 + [pltpu.VMEM((rows, width), bf16)] * 2


def everyone_near():
    _, core, far, up, down = along_fsdp()
    _, nxt, prv, _ = along_context()
    return [{"fsdp": i} for i in (core, far, up, down)] + [
        {"context": nxt}, {"context": prv}, {"tensor": 1 - lax.axis_index("tensor")}
    ]


def half_turn(x):
    return pltpu.roll(x, HD // 2, 1)


def signal(sem, to):
    pl.semaphore_signal(sem, inc=1, device_id=to, device_id_type=MESH)


ORDER = (2, 1, 3, 0)
SMALL = (8, 512)


def layer_back_kernel(
    normed_hbm, dy_hbm, gate_hbm, lift_hbm, hidden_hbm, first_hbm, second_hbm,
    out_hbm, lin_hbm, probs_hbm,
    middle_ref, dy_ref, gain_two_ref, mixed_ref, query_ref, key_ref, value_ref,
    normed_one_ref, tokens_ref, gain_one_ref, cos_ref, sin_ref,
    result_ref, gt_ref, small_ref, attn_ref, mlp_hbm,
    part, from_prv, from_nxt, mine, other,
    left, right, both, came, from_down, from_up, pair, last, shard_out,
    probs, d_middle, d_branch, d_mixed, acc_k, acc_v, kv_send, kv_came,
    d_lin, swap_mine, swap_other, attn_own, attn_came, small_own, small_came,
    send, recv, local, free,
):
    wire, loads = Wire(send, recv), Loads(local)
    rows, width = middle_ref.shape
    group = part.shape[0]
    q_cols, kv_cols = mixed_ref.shape[1], key_ref.shape[1]
    heads = q_cols // HD
    span = hidden_hbm.shape[1]
    scale = HD ** (-0.5)
    c, nxt, prv, cf = along_context()
    f, core, far, up, down = along_fsdp()
    C = lambda i: {"context": i}
    F = lambda i: {"fsdp": i}
    T = {"tensor": 1 - lax.axis_index("tensor")}

    def keep_small(at, values):
        for k in range(values.shape[1] // SMALL[1]):
            small_own[pl.ds(at + k, 1), :] = values[:, k * SMALL[1] : (k + 1) * SMALL[1]]

    load_part = loads.start(first_hbm, part)
    load_left = loads.start(normed_hbm, left)
    load_r0 = loads.start(gate_hbm, right.at[0])
    load_r1 = loads.start(lift_hbm, right.at[1])
    opposite = lax.rem(f + 8, lax.axis_size("fsdp"))
    meet(everyone_near() + [C(cf), F(opposite)])

    one = RowSum(wire, part, from_prv, from_nxt, mine, other, 3)
    two = RowSum(wire, part, from_prv, from_nxt, mine, other, 3)
    mlp = ShardSum(wire, both, came, from_down, from_up, pair, last, [(k * span, span) for k in range(3)])
    attn = ShardSum(
        wire, both, came, from_down, from_up, pair, last,
        [(0, q_cols), (q_cols, q_cols), (2 * q_cols, 2 * kv_cols)],
    )
    load_part.wait()
    one.start()

    load_left.wait()
    load_r0.wait()
    for rel in ORDER:
        mlp.multiply(0, rel, left[:, mlp.block_cols(rel)], right[0])
    load_r0 = loads.start(hidden_hbm, right.at[0])
    load_r1.wait()
    for rel in ORDER:
        mlp.multiply(1, rel, left[:, mlp.block_cols(rel)], right[1])
    load_left = loads.start(dy_hbm, left)
    for k in range(3):
        one.relay(k)
    mlp.start(0)
    load_r0.wait()
    load_left.wait()
    for rel in ORDER:
        mlp.multiply(2, rel, left[:, mlp.block_cols(rel)], right[0])
    deep = left.shape[0]
    rest = width - deep
    load_out = (
        loads.start(out_hbm.at[pl.ds(0, deep)], left.at[:, pl.ds(0, q_cols)]),
        loads.start(out_hbm.at[pl.ds(deep, rest)], left.at[pl.ds(0, rest), pl.ds(q_cols, q_cols)]),
    )
    lin_cols = lin_hbm.shape[1]
    load_lin = (
        loads.start(lin_hbm.at[pl.ds(0, deep)], right.at[0, :, pl.ds(0, lin_cols)]),
        loads.start(lin_hbm.at[pl.ds(deep, rest)], right.at[1, pl.ds(0, rest), pl.ds(0, lin_cols)]),
    )
    load_probs = {h: loads.start(probs_hbm.at[h], probs.at[h % 2]) for h in range(2)}
    mlp.start(1)
    one.exchange(0)
    one.exchange(1)
    mlp.start(2)
    one.exchange(2)
    signal(free.at[0], F(core))
    for k in range(3):
        wire.sent(*one.relays[k], *one.plains[k], *one.mores[k])
    signal(free.at[1], C(nxt))
    signal(free.at[2], C(prv))
    load_part = loads.start(second_hbm, part)
    mlp.relays(0)
    mlp.relays(1)
    one.landed()

    sizes = 64
    gain_grad = jnp.zeros((1, width), f32)
    for at in range(0, rows, sizes):
        at = pl.ds(at, sizes)
        grad, mid = one.total(at), middle_ref[at, :]
        r = lax.rsqrt(jnp.mean(mid * mid, axis=-1, keepdims=True) + EPSILON)
        gain_grad += jnp.sum(grad * mid * r, axis=0, keepdims=True)
        scaled = grad * gain_two_ref[...]
        back = jnp.mean(scaled * mid, axis=-1, keepdims=True)
        value = dy_ref[at, :].astype(f32) + r * scaled - mid * (r * r * r * back)
        d_middle[at, :] = value
        d_branch[at, :] = value.astype(bf16)
    keep_small(3, gain_grad)
    wire.sent(*one.swaps.values())
    signal(free.at[3], T)
    load_part.wait()
    pl.semaphore_wait(free.at[1], 1)
    pl.semaphore_wait(free.at[2], 1)
    two.start()
    mlp.relays(2)

    for copy in load_out:
        copy.wait()
    d_mixed[...] = (
        jnp.dot(d_branch[:, pl.ds(0, deep)], left[:, pl.ds(0, q_cols)], preferred_element_type=f32)
        + jnp.dot(
            d_branch[:, pl.ds(deep, rest)], left[pl.ds(0, rest), pl.ds(q_cols, q_cols)],
            preferred_element_type=f32,
        )
    ).astype(bf16)
    lane = lax.broadcasted_iota(jnp.int32, (1, HD), 1)
    sign = jnp.where(lane < HD // 2, 1.0, -1.0).astype(f32)

    def turn_back(w):
        return w * cos_ref[...] + half_turn(w * sin_ref[...]) * sign

    nt = (((1,), (1,)), ((), ()))
    tn = (((0,), (0,)), ((), ()))

    def head(h):
        cols = pl.ds(h * HD, HD)
        load_probs[h].wait()
        p = probs[h % 2]
        dm = d_mixed[:, cols]
        dp = lax.dot_general(dm, value_ref[...], nt, preferred_element_type=f32)
        inner = jnp.sum(p * dp, axis=-1, keepdims=True)
        ds = (p * (dp - inner)).astype(bf16)
        dq = jnp.dot(ds, key_ref[...], preferred_element_type=f32) * scale
        d_lin[:, cols] = turn_back(dq).astype(bf16)
        dk = lax.dot_general(ds, query_ref[:, cols], tn, preferred_element_type=f32)
        dv = lax.dot_general(p.astype(bf16), dm, tn, preferred_element_type=f32)
        if h == 0:
            acc_k[...] = dk
            acc_v[...] = dv
        else:
            acc_k[...] += dk
            acc_v[...] += dv
        if h + 2 < heads:
            load_probs[h + 2] = loads.start(probs_hbm.at[h + 2], probs.at[h % 2])

    head(0)
    mlp.across(0)
    head(1)
    mlp.across(1)
    for k in range(3):
        two.relay(k)
    head(2)
    mlp.across(2)
    for k in range(3):
        wire.sent(*mlp.more[k])
    signal(free.at[4], F(up))
    signal(free.at[5], F(down))
    head(3)
    for k in range(3):
        shard_out[:, mlp.cols(k)] = mlp.total(k).astype(bf16)
    signal(free.at[6], F(far))
    spread = [
        wire.push(shard_out, mlp_hbm.at[c], C(nxt)),
        wire.push(shard_out, mlp_hbm.at[c], C(prv)),
    ]
    keep = loads.start(shard_out, mlp_hbm.at[c])
    head(4)
    pl.semaphore_wait(free.at[3], 1)
    for k in range(3):
        two.exchange(k)
    head(5)

    for k in range(4):
        kv_send[k, 0] = acc_k[pl.ds(k * rows, rows), :].astype(bf16)
        kv_send[k, 1] = acc_v[pl.ds(k * rows, rows), :].astype(bf16)
    kv = [
        wire.push(kv_send.at[nxt], kv_came.at[0], C(nxt)),
        wire.push(kv_send.at[prv], kv_came.at[1], C(prv)),
        wire.push(kv_send.at[cf], kv_came.at[2], C(cf)),
    ]
    for k in range(3):
        wire.sent(*[mlp.cores[k, rel] for rel in ORDER], *mlp.relay[k], *mlp.plain[k], mlp.cross[k])
    pl.semaphore_wait(free.at[0], 1)
    for rel in ORDER:
        attn.multiply(0, rel, d_branch[:, attn.block_cols(rel)], mixed_ref[...])
    for rel in ORDER:
        attn.multiply(1, rel, normed_one_ref[:, attn.block_cols(rel)], d_lin[:, pl.ds(0, q_cols)])
    for copy in kv:
        copy.wait_recv()
    d_key = acc_k[pl.ds(pl.multiple_of(c * rows, 8), rows), :]
    d_value = acc_v[pl.ds(pl.multiple_of(c * rows, 8), rows), :]
    for k in range(3):
        d_key += kv_came[k, 0].astype(f32)
        d_value += kv_came[k, 1].astype(f32)
    d_lin[:, pl.ds(q_cols, kv_cols)] = turn_back(d_key * scale).astype(bf16)
    d_lin[:, pl.ds(q_cols + kv_cols, kv_cols)] = d_value.astype(bf16)
    for copy in load_lin:
        copy.wait()
    swap_mine[:, pl.ds(0, deep)] = lax.dot_general(
        d_lin[...], right[0, :, pl.ds(0, lin_cols)], nt, preferred_element_type=f32
    ).astype(bf16)
    swap_mine[:, pl.ds(deep, rest)] = lax.dot_general(
        d_lin[...], right[1, pl.ds(0, rest), pl.ds(0, lin_cols)], nt, preferred_element_type=f32
    ).astype(bf16)
    swap = wire.push(swap_mine, swap_other, T)
    for rel in ORDER:
        attn.multiply(
            2, rel, normed_one_ref[:, attn.block_cols(rel)], d_lin[:, pl.ds(q_cols, 2 * kv_cols)]
        )
    pl.semaphore_wait(free.at[4], 1)
    pl.semaphore_wait(free.at[5], 1)
    for k in range(3):
        attn.start(k)
    keep_small(6, jnp.sum(d_lin[...].astype(f32), axis=0, keepdims=True))
    half = shard_out.shape[0] // 2
    spread[0].wait_recv()
    w = mlp_hbm.at[prv, pl.ds(0, half)]
    spread.append(wire.push(w, w, C(nxt)))
    spread[1].wait_recv()
    w = mlp_hbm.at[nxt, pl.ds(half, half)]
    spread.append(wire.push(w, w, C(prv)))
    two.landed()
    for at in range(0, rows, sizes):
        at = pl.ds(at, sizes)
        result_ref[at, :] = (middle_ref[at, :] + two.total(at)).astype(bf16)
    for k in range(3):
        attn.relays(k)
    pl.semaphore_wait(free.at[6], 1)
    for k in range(3):
        attn.across(k)

    swap.wait_recv()
    gain_grad = jnp.zeros((1, width), f32)
    for at in range(0, rows, sizes):
        at = pl.ds(at, sizes)
        grad = swap_mine[at, :].astype(f32) + swap_other[at, :].astype(f32)
        mid = tokens_ref[at, :].astype(f32)
        r = lax.rsqrt(jnp.mean(mid * mid, axis=-1, keepdims=True) + EPSILON)
        gain_grad += jnp.sum(grad * mid * r, axis=0, keepdims=True)
        scaled = grad * gain_one_ref[...]
        back = jnp.mean(scaled * mid, axis=-1, keepdims=True)
        gt_ref[at, :] = d_middle[at, :] + r * scaled - mid * (r * r * r * back)
    keep_small(0, gain_grad)

    for k in range(3):
        attn_own[:, attn.cols(k)] = attn.total(k).astype(bf16)
    both_ways = [
        wire.push(attn_own, attn_came.at[0], C(nxt)),
        wire.push(attn_own, attn_came.at[1], C(prv)),
    ]
    steps = [F(core), F(far), F(f + 4 - 8 * lax.rem(lax.div(f, 4), 2)), F(opposite),
             C(c + 1 - 2 * lax.rem(c, 2)), C(cf)]
    for k, to in enumerate(steps):
        copy = wire.push(small_own if k == 0 else small_came.at[2 * k - 1], small_came.at[2 * k], to)
        copy.wait_recv()
        have = small_own[...] if k == 0 else small_came[2 * k - 1]
        total = have + small_came[2 * k]
        if k == len(steps) - 1:
            small_ref[...] = total
        else:
            small_came[2 * k + 1] = total
        if k == 1:
            both_ways[0].wait_recv()
            both_ways[1].wait_recv()
            both_ways.append(
                wire.push(attn_came.at[0, pl.ds(0, half)], attn_came.at[2, pl.ds(0, half)], C(nxt))
            )
            both_ways.append(
                wire.push(attn_came.at[1, pl.ds(half, half)], attn_came.at[2, pl.ds(half, half)], C(prv))
            )
    both_ways[2].wait_recv()
    both_ways[3].wait_recv()
    own_pair = attn_own[...].astype(f32) + attn_came[2].astype(f32)
    next_pair = attn_came[0].astype(f32) + attn_came[1].astype(f32)
    attn_ref[...] = own_pair + next_pair
    spread[2].wait_recv()
    spread[3].wait_recv()
    keep.wait()
    wire.drain()


def layer_back(hbm, near, cid=4):
    normed, dy, gate, lift, hidden, first, second, out, lin, probs = hbm
    group, width = normed.shape
    rows = group // 4
    shard, span = width // 16, gate.shape[1]
    lin_cols = lin.shape[1]
    q_cols = out.shape[1]
    sems = 2 * 21 + 2 * (12 + 3 * 7) + 3 + 1 + 4 + 4 + 6
    return pl.pallas_call(
        layer_back_kernel,
        out_shape=(
            jax.ShapeDtypeStruct((rows, width), bf16),
            jax.ShapeDtypeStruct((rows, width), f32),
            jax.ShapeDtypeStruct(SMALL, f32),
            jax.ShapeDtypeStruct((shard, lin_cols + q_cols), f32),
            jax.ShapeDtypeStruct((4, shard, 3 * span), bf16),
        ),
        in_specs=[ANY] * len(hbm) + [VM] * len(near),
        out_specs=(VM, VM, VM, VM, ANY),
        scratch_shapes=[pltpu.VMEM((group, width), bf16)]
        + row_scratch(rows, width)
        + [
            pltpu.VMEM((group, width), bf16),
            pltpu.VMEM((2, group, span), bf16),
            pltpu.VMEM((2, 8, shard, 3 * span), bf16),
            pltpu.VMEM((8, shard, 3 * span), bf16),
            pltpu.VMEM((3, 2, shard // 2, 3 * span), bf16),
            pltpu.VMEM((3, 2, shard // 2, 3 * span), bf16),
            pltpu.VMEM((2, shard, 3 * span), bf16),
            pltpu.VMEM((shard, 3 * span), bf16),
            pltpu.VMEM((shard, 3 * span), bf16),
            pltpu.VMEM((2, rows, group), f32),
            pltpu.VMEM((rows, width), f32),
            pltpu.VMEM((rows, width), bf16),
            pltpu.VMEM((rows, q_cols), bf16),
            pltpu.VMEM((group, HD), f32),
            pltpu.VMEM((group, HD), f32),
            pltpu.VMEM((4, 2, rows, HD), bf16),
            pltpu.VMEM((3, 2, rows, HD), bf16),
            pltpu.VMEM((rows, lin_cols), bf16),
            pltpu.VMEM((rows, width), bf16),
            pltpu.VMEM((rows, width), bf16),
            pltpu.VMEM((shard, lin_cols + q_cols), bf16),
            pltpu.VMEM((3, shard, lin_cols + q_cols), bf16),
            pltpu.VMEM(SMALL, f32),
            pltpu.VMEM((11,) + SMALL, f32),
            pltpu.SemaphoreType.DMA((sems,)),
            pltpu.SemaphoreType.DMA((sems,)),
            pltpu.SemaphoreType.DMA((18,)),
            pltpu.SemaphoreType.REGULAR((7,)),
        ],
        compiler_params=pltpu.CompilerParams(
            collective_id=cid, has_side_effects=True, vmem_limit_bytes=63 << 20
        ),
        name="layer_back",
    )(*hbm, *near)


class Blocks:
    def __init__(self, wire, ref, shard, cols=None):
        self.wire, self.ref, self.shard, self.half = wire, ref, shard, shard // 2
        self.cols = slice(None) if cols is None else cols
        self.f, self.core, self.far, self.up, self.down = along_fsdp()
        n = lax.axis_size("fsdp")
        self.opposite = lax.rem(self.f + 8, n)
        self.sibling = []

    def pair(self, i):
        return i + 2 - 4 * lax.rem(lax.div(i, 2), 2)

    def win(self, owner, lo=0, size=None):
        at = pl.multiple_of(owner * self.shard + lo, 16)
        return self.ref.at[pl.ds(at, size or self.shard), self.cols]

    def push(self, w, to):
        return self.wire.push(w, w, {"fsdp": to})

    def to_core(self, w):
        self.sibling.append(self.push(w, self.core))

    def e0(self):
        w = self.win(self.f)
        self.from_far = self.push(w, self.far)
        self.from_down = self.push(w, self.up)
        self.from_up = self.push(w, self.down)
        self.to_core(w)

    def e1(self):
        self.from_far.wait_recv()
        w = self.win(self.far)
        self.far_down = self.push(w, self.up)
        self.far_up = self.push(w, self.down)
        self.to_core(w)

    def relay(self, below, above, one, two):
        one.wait_recv()
        first = self.push(self.win(below, 0, self.half), self.up)
        self.to_core(self.win(below))
        two.wait_recv()
        second = self.push(self.win(above, self.half, self.half), self.down)
        self.to_core(self.win(above))
        return first, second

    def e2(self):
        self.last = self.relay(self.down, self.up, self.from_down, self.from_up)

    def e3(self):
        self.last += self.relay(self.pair(self.down), self.pair(self.up), self.far_down, self.far_up)

    def e4(self):
        for k, copy in enumerate(self.last):
            copy.wait_recv()
            owner = self.opposite if k < 2 else self.pair(self.opposite)
            self.to_core(self.win(owner, self.half * (k % 2), self.half))

    def end(self):
        for copy in self.sibling:
            copy.wait_recv()


def layer_front_kernel(
    query_hbm, key_hbm, value_hbm, out_hbm, gate_hbm, lift_hbm, down_hbm, dy_hbm,
    gains_ref, tokens_ref, cos_ref, sin_ref, seg_q_ref, seg_k_ref, bias_ref,
    middle_ref, normed_one_ref, mixed_ref, q_ref, kv_ref, gain_ref,
    normed_hbm, dyg_hbm, lin_hbm, outf_hbm, probs_hbm,
    d_gate_hbm, d_lift_hbm, hidden_hbm, first_hbm, second_hbm,
    gains, wl, wo, wm, dyg, normed, mask, probs, part, other, d_hidden,
    d_gate, d_lift, hidden, first, second,
    send, recv, local,
):
    wire, loads = Wire(send, recv), Loads(local)
    rows, width = tokens_ref.shape
    group = dyg.shape[0]
    shard, q_cols = query_hbm.shape
    kv_cols = key_hbm.shape[1]
    heads = q_cols // HD
    hidden_cols = gate_hbm.shape[1]
    span = d_hidden.shape[1]
    overlap = 4 * span - hidden_cols
    scale = HD ** (-0.5)
    c, nxt, prv, cf = along_context()
    f, core, far, up, down = along_fsdp()
    C = lambda i: {"context": i}
    T = {"tensor": 1 - lax.axis_index("tensor")}
    mine = pl.ds(pl.multiple_of(f * shard, 16), shard)
    group_rows = lambda owner, lo=0, size=rows: pl.ds(pl.multiple_of(owner * rows + lo, 16), size)
    start = pl.multiple_of(c * span - lax.div(c, 3) * overlap, 128)

    own = [
        loads.start(query_hbm, wl.at[mine, pl.ds(0, q_cols)]),
        loads.start(key_hbm, wl.at[mine, pl.ds(q_cols, kv_cols)]),
        loads.start(value_hbm, wl.at[mine, pl.ds(q_cols + kv_cols, kv_cols)]),
        loads.start(out_hbm, wo.at[mine, :]),
        loads.start(dy_hbm, dyg.at[group_rows(c), :]),
    ]
    big = [
        loads.start(w.at[:, pl.ds(start, span)], wm.at[mine, pl.ds(k * span, span)])
        for k, w in enumerate((down_hbm, gate_hbm, lift_hbm))
    ]
    tile = gains_ref.shape[0]
    gains[pl.ds(pl.multiple_of(f * tile, 16), tile), :] = gains_ref[...]
    meet(everyone_near() + [C(cf)])
    G = Blocks(wire, gains, tile)
    Q = Blocks(wire, wl, shard)
    O = Blocks(wire, wo, shard)
    Md, Mg, Mu = (Blocks(wire, wm, shard, pl.ds(k * span, span)) for k in range(3))

    G.e0()
    for copy in own:
        copy.wait()
    Q.e0()
    w = dyg.at[group_rows(c), :]
    dy_copies = [wire.push(w, w, C(nxt)), wire.push(w, w, C(prv))]
    G.e1()
    O.e0()
    here = c * rows + lax.broadcasted_iota(jnp.int32, (rows, group), 0)
    there = lax.broadcasted_iota(jnp.int32, (rows, group), 1)
    allowed = (seg_q_ref[...] == seg_k_ref[...]) & (there <= here)
    mask[...] = jnp.where(allowed, 0.0, -1e30).astype(f32)
    G.e2()
    G.e3()
    Q.e1()
    G.e4()
    G.end()
    for k in range(2):
        gain_ref[pl.ds(k, 1), :] = jnp.concatenate(
            [gains[pl.ds(i * tile + k, 1), :].astype(f32)[:, :shard] for i in range(width // shard)], axis=1
        )
    sizes = 64
    for at in range(0, rows, sizes):
        at = pl.ds(at, sizes)
        x = tokens_ref[at, :].astype(f32)
        r = lax.rsqrt(jnp.mean(x * x, axis=-1, keepdims=True) + EPSILON)
        normed_one_ref[at, :] = (x * r * gain_ref[pl.ds(0, 1), :]).astype(bf16)
    Q.e2()
    Q.e3()
    O.e1()
    Q.e4()
    for copy in big:
        copy.wait()
    Md.e0()
    Q.end()

    sign = jnp.where(lax.broadcasted_iota(jnp.int32, (1, HD), 1) < HD // 2, -1.0, 1.0).astype(f32)

    def turned(v):
        return v * cos_ref[...] + half_turn(v) * sign * sin_ref[...]

    def linear(at, size):
        cols = pl.ds(at, size)
        return jnp.dot(normed_one_ref[...], wl[:, cols], preferred_element_type=f32) + bias_ref[:, cols]

    lin = linear(q_cols, 2 * kv_cols)
    kv_ref[0, group_rows(c), :] = turned(lin[:, :kv_cols]).astype(bf16)
    kv_ref[1, group_rows(c), :] = lin[:, kv_cols:].astype(bf16)
    w = kv_ref.at[:, group_rows(c), :]
    kv = [wire.push(w, w, C(i)) for i in (nxt, prv, cf)]
    for h in range(0, heads, 2):
        lin = linear(h * HD, 2 * HD)
        q_ref[:, pl.ds(h * HD, HD)] = turned(lin[:, :HD]).astype(bf16)
        q_ref[:, pl.ds((h + 1) * HD, HD)] = turned(lin[:, HD:]).astype(bf16)
    O.e2()
    O.e3()
    Md.e1()
    Mg.e0()
    keep = [loads.start(wl, lin_hbm)]
    half = rows // 2
    dy_copies[0].wait_recv()
    w = dyg.at[group_rows(prv, 0, half), :]
    dy_copies.append(wire.push(w, w, C(nxt)))
    dy_copies[1].wait_recv()
    w = dyg.at[group_rows(nxt, half, half), :]
    dy_copies.append(wire.push(w, w, C(prv)))
    O.e4()
    for copy in kv:
        copy.wait_recv()

    nt = (((1,), (1,)), ((), ()))
    probs_out = {}

    def head(h):
        cols = pl.ds(h * HD, HD)
        s = lax.dot_general(q_ref[:, cols], kv_ref[0], nt, preferred_element_type=f32)
        s = s * scale + mask[...]
        e = jnp.exp(s - jnp.max(s, axis=-1, keepdims=True))
        p = e / jnp.sum(e, axis=-1, keepdims=True)
        if h >= 2:
            probs_out[h - 2].wait()
        probs[h % 2] = p
        probs_out[h] = loads.start(probs.at[h % 2], probs_hbm.at[h])
        mixed_ref[:, cols] = jnp.dot(p.astype(bf16), kv_ref[1], preferred_element_type=f32).astype(bf16)

    head(0)
    Md.e2()
    head(1)
    Md.e3()
    Mg.e1()
    head(2)
    Mu.e0()
    Md.e4()
    head(3)
    head(4)
    Mg.e2()
    head(5)
    probs_out[heads - 2].wait()
    probs_out[heads - 1].wait()
    O.end()
    chunks = rows // sizes
    swaps = []
    for k in range(chunks):
        at = pl.ds(k * sizes, sizes)
        part[at, :] = lax.dot_general(mixed_ref[at, :], wo[...], nt, preferred_element_type=f32).astype(bf16)
        swaps.append(wire.push(part.at[at, :], other.at[at, :], T))
    keep.append(loads.start(wo, outf_hbm))
    Mg.e3()
    Mu.e1()
    Mg.e4()
    for copy in dy_copies[2:]:
        copy.wait_recv()
    keep.append(loads.start(dyg, dyg_hbm))
    Md.end()

    from_prv, from_nxt, last = {}, {}, []
    cut = sizes // 2

    def forward(k):
        from_prv[k].wait_recv()
        w = normed.at[group_rows(prv, k * sizes, cut), :]
        last.append(wire.push(w, w, C(nxt)))
        from_nxt[k].wait_recv()
        w = normed.at[group_rows(nxt, k * sizes + cut, cut), :]
        last.append(wire.push(w, w, C(prv)))

    def hidden_back(owner):
        at = group_rows(owner)
        d_hidden[at, :] = jnp.dot(dyg[at, :], wm[:, pl.ds(0, span)], preferred_element_type=f32)

    for k in range(chunks):
        at = pl.ds(k * sizes, sizes)
        swaps[k].wait_recv()
        mid = tokens_ref[at, :].astype(f32) + (part[at, :].astype(f32) + other[at, :].astype(f32))
        middle_ref[at, :] = mid
        r = lax.rsqrt(jnp.mean(mid * mid, axis=-1, keepdims=True) + EPSILON)
        normed[group_rows(c, k * sizes, sizes), :] = (mid * r * gain_ref[pl.ds(1, 1), :]).astype(bf16)
        w = normed.at[group_rows(c, k * sizes, sizes), :]
        from_prv[k] = wire.push(w, w, C(nxt))
        from_nxt[k] = wire.push(w, w, C(prv))
        if k == 0:
            Mu.e2()
        hidden_back((c, prv, nxt, cf)[k])
    Mu.e3()
    Mg.end()
    forward(0)
    Mu.e4()
    forward(1)

    def feed(owner, waits=()):
        at = group_rows(owner)
        n = normed[at, :]
        gate = jnp.dot(n, wm[:, pl.ds(span, span)], preferred_element_type=f32)
        lift = jnp.dot(n, wm[:, pl.ds(2 * span, span)], preferred_element_type=f32)
        dh = d_hidden[at, :]
        skip = lax.div(c, 3) * overlap
        live = lax.broadcasted_iota(jnp.int32, dh.shape, 1) >= skip
        dh = jnp.where(live, dh, 0.0)
        sig = 1.0 / (1.0 + jnp.exp(-gate))
        swish = gate * sig
        hidden[at, :] = jnp.where(live, swish * lift, 0.0).astype(bf16)
        d_gate[at, :] = (dh * lift * sig * (1.0 + gate * (1.0 - sig))).astype(bf16)
        d_lift[at, :] = (dh * swish).astype(bf16)
        first[at, :] = (
            lax.dot_general(d_gate[at, :], wm[:, pl.ds(span, span)], nt, preferred_element_type=f32)
            + lax.dot_general(d_lift[at, :], wm[:, pl.ds(2 * span, span)], nt, preferred_element_type=f32)
        ).astype(bf16)
        second[at, :] = lax.dot_general(
            hidden[at, :], wm[:, pl.ds(0, span)], nt, preferred_element_type=f32
        ).astype(bf16)
        for src, dst in (
            (d_gate, d_gate_hbm), (d_lift, d_lift_hbm), (hidden, hidden_hbm), (first, first_hbm), (second, second_hbm),
        ):
            keep.append(loads.start(src.at[at, :], dst.at[at, :]))

    Mu.end()
    feed(c)
    forward(2)
    forward(3)
    feed(prv)
    feed(nxt)
    for copy in last:
        copy.wait_recv()
    keep.append(loads.start(normed, normed_hbm))
    feed(cf)
    for copy in keep:
        copy.wait()
    wire.drain()


def layer_front(hbm, near, span, cid=1):
    query, key, value, out, gate, lift, down, dy = hbm
    rows, width = dy.shape
    group = 4 * rows
    shard, q_cols = query.shape
    lin_cols = q_cols + 2 * key.shape[1]
    heads = q_cols // HD
    sems = 6 * 19 + 4 + 3 + 4 + 16
    S = jax.ShapeDtypeStruct
    return pl.pallas_call(
        layer_front_kernel,
        out_shape=(
            S((rows, width), f32),
            S((rows, width), bf16),
            S((rows, q_cols), bf16),
            S((rows, q_cols), bf16),
            S((2, group, HD), bf16),
            S((2, width), f32),
            S((group, width), bf16),
            S((group, width), bf16),
            S((width, lin_cols), bf16),
            S((width, q_cols), bf16),
            S((heads, rows, group), f32),
        )
        + (S((group, span), bf16),) * 3
        + (S((group, width), bf16),) * 2,
        in_specs=[ANY] * len(hbm) + [VM] * len(near),
        out_specs=(VM,) * 6 + (ANY,) * 10,
        scratch_shapes=[
            pltpu.VMEM((width // shard * near[0].shape[0], 128), bf16),
            pltpu.VMEM((width, lin_cols), bf16),
            pltpu.VMEM((width, q_cols), bf16),
            pltpu.VMEM((width, 3 * span), bf16),
            pltpu.VMEM((group, width), bf16),
            pltpu.VMEM((group, width), bf16),
            pltpu.VMEM((rows, group), f32),
            pltpu.VMEM((2, rows, group), f32),
            pltpu.VMEM((rows, width), bf16),
            pltpu.VMEM((rows, width), bf16),
            pltpu.VMEM((group, span), f32),
            pltpu.VMEM((group, span), bf16),
            pltpu.VMEM((group, span), bf16),
            pltpu.VMEM((group, span), bf16),
            pltpu.VMEM((group, width), bf16),
            pltpu.VMEM((group, width), bf16),
            pltpu.SemaphoreType.DMA((sems,)),
            pltpu.SemaphoreType.DMA((sems,)),
            pltpu.SemaphoreType.DMA((8 + heads + 4 + 20,)),
        ],
        compiler_params=pltpu.CompilerParams(
            collective_id=cid, has_side_effects=True, vmem_limit_bytes=63 << 20
        ),
        name="layer_front",
    )(*hbm, *near)


def rope_tables(positions, head_width):
    half_width = head_width // 2
    freq_index = jnp.arange(half_width).astype(jnp.float32)
    inverse = ROPE_BASE ** (-(freq_index * 2.0 / head_width))
    angles = positions.astype(jnp.float32)[:, None] * inverse[None, :]
    cosine = jnp.cos(angles)
    sine_table = jnp.sin(angles)
    return (jnp.concatenate([cosine, cosine], -1), jnp.concatenate([sine_table, sine_table], -1))


def segment_info(seq_lengths, total_rows):
    ends_at = jnp.cumsum(seq_lengths)
    places = jnp.arange(total_rows, dtype=jnp.int32)
    passed = places[:, None] >= ends_at[None, :]
    segment = jnp.sum(passed.astype(jnp.int32), axis=1)
    starts = jnp.sum(jnp.where(passed, seq_lengths[None, :], 0), axis=1)
    return (segment, places - starts)


def on_device(
    tokens,
    cotangent,
    lengths,
    gain_attn,
    w_query,
    b_query,
    w_key,
    b_key,
    w_value,
    b_value,
    w_out,
    gain_mlp,
    w_gate,
    w_up,
    w_down,
):
    row_count, width = tokens.shape
    context_size = lax.axis_size("context")
    context_rank = lax.axis_index("context")
    fsdp_rank = lax.axis_index("fsdp")
    shard = w_query.shape[0]
    query_cols, kv_cols, hidden_cols = w_query.shape[1], w_key.shape[1], w_gate.shape[1]
    group_rows = row_count * context_size
    segment_all, position_all = segment_info(lengths[0], group_rows)
    first_row = context_rank * row_count
    segment_mine = lax.dynamic_slice_in_dim(segment_all, first_row, row_count)
    position_mine = lax.dynamic_slice_in_dim(position_all, first_row, row_count)
    cosine, sine_table = rope_tables(position_mine, HD)

    span = -(-(hidden_cols // 128) // context_size) * 128
    overlap = context_size * span - hidden_cols
    gains = jnp.pad(jnp.stack([gain_attn, gain_mlp]), ((0, 30), (0, 128 - shard)))
    bias = jnp.concatenate([b_query, b_key, b_value]).astype(f32)[None]
    (
        middle, normed_one, mixed, query_heads, kv_group, gain_full,
        normed_group, dy_group, lin_full, out_turned, probs,
        d_gate, d_lift, hidden, d_normed_part, mlp_part,
    ) = layer_front(
        (w_query, w_key, w_value, w_out.T, w_gate, w_up, w_down.T, cotangent),
        (
            gains, tokens, cosine, sine_table, segment_mine[:, None], segment_all[None], bias,
        ),
        span,
    )
    result, grad_tokens, small, attn_shard, mlp_all = layer_back(
        (
            normed_group, dy_group, d_gate, d_lift, hidden, d_normed_part, mlp_part,
            out_turned, lin_full, probs,
        ),
        (
            middle, cotangent, gain_full[1:], mixed, query_heads, kv_group[0], kv_group[1],
            normed_one, tokens, gain_full[:1], cosine, sine_table,
        ),
    )

    def whole(k):
        parts = [mlp_all[i, :, k * span : (k + 1) * span] for i in range(context_size)]
        parts[-1] = parts[-1][:, overlap:]
        return jnp.concatenate(parts, axis=1).astype(f32)

    small = small.reshape(-1)
    own = lambda at: lax.dynamic_slice_in_dim(small, at + fsdp_rank * shard, shard)
    bias_total = small[2 * width :]
    at_query = query_cols
    at_key = at_query + query_cols
    at_value = at_key + kv_cols
    return (
        result,
        grad_tokens,
        own(0),
        attn_shard[:, at_query:at_key],
        bias_total[:query_cols],
        attn_shard[:, at_key:at_value],
        bias_total[query_cols : query_cols + kv_cols],
        attn_shard[:, at_value:],
        bias_total[query_cols + kv_cols :],
        attn_shard[:, :query_cols].T,
        own(width),
        whole(0),
        whole(1),
        whole(2).T,
    )


def solution(mesh):
    return jax.shard_map(
        on_device,
        mesh=mesh,
        in_specs=(
            P(("fsdp", "context"), None),
            P(("fsdp", "context"), None),
            P("fsdp", None),
            P("fsdp"),
            P("fsdp", "tensor"),
            P("tensor"),
            P("fsdp", "tensor"),
            P("tensor"),
            P("fsdp", "tensor"),
            P("tensor"),
            P("tensor", "fsdp"),
            P("fsdp"),
            P("fsdp", "tensor"),
            P("fsdp", "tensor"),
            P("tensor", "fsdp"),
        ),
        out_specs=(
            P(("fsdp", "context"), None),
            P(("fsdp", "context"), None),
            P("fsdp"),
            P("fsdp", "tensor"),
            P("tensor"),
            P("fsdp", "tensor"),
            P("tensor"),
            P("fsdp", "tensor"),
            P("tensor"),
            P("tensor", "fsdp"),
            P("fsdp"),
            P("fsdp", "tensor"),
            P("fsdp", "tensor"),
            P("tensor", "fsdp"),
        ),
        check_vma=False,
    )
```

```python
import jax
import jax.numpy as jnp
from jax import lax
from jax.experimental import pallas as pl
from jax.experimental.pallas import tpu as pltpu
from jax.sharding import PartitionSpec as P

HD = 128
MESH = pl.DeviceIdType.MESH
ANY = pl.BlockSpec(memory_space=pl.ANY)
VM = pl.BlockSpec(memory_space=pltpu.VMEM)
f32, bf16 = jnp.float32, jnp.bfloat16

ROPE_BASE = 1000000.0
EPSILON = 1e-06

def meet(targets):
    barrier = pltpu.get_barrier_semaphore()
    for t in targets:
        pl.semaphore_signal(barrier, inc=1, device_id=t, device_id_type=MESH)
    pl.semaphore_wait(barrier, len(targets))


class Wire:
    def __init__(self, send, recv):
        self.send, self.recv, self.used, self.started = send, recv, 0, []

    def push(self, src, dst, to):
        k = self.used
        self.used += 1
        copy = pltpu.make_async_remote_copy(
            src, dst, self.send.at[k], self.recv.at[k], device_id=to, device_id_type=MESH
        )
        copy.start()
        self.started.append(copy)
        return copy

    def sent(self, *copies):
        for copy in copies:
            copy.wait_send()
            self.started = [other for other in self.started if other is not copy]

    def drain(self):
        self.sent(*list(self.started))


class Loads:
    def __init__(self, sems):
        self.sems, self.used = sems, 0

    def start(self, src, dst):
        copy = pltpu.make_async_copy(src, dst, self.sems.at[self.used])
        self.used += 1
        copy.start()
        return copy


def along_context():
    c, m = lax.axis_index("context"), lax.axis_size("context")
    return c, lax.rem(c + 1, m), lax.rem(c + m - 1, m), lax.rem(c + 2, m)


def along_fsdp():
    f, n = lax.axis_index("fsdp"), lax.axis_size("fsdp")
    core = f + 1 - 2 * lax.rem(f, 2)
    far = f + 2 - 4 * lax.rem(lax.div(f, 2), 2)
    return f, core, far, lax.rem(f + 4, n), lax.rem(f + n - 4, n)


class RowSum:
    def __init__(self, wire, part, from_prv, from_nxt, mine, other, chunks):
        self.wire, self.part, self.chunks = wire, part, chunks
        self.from_prv, self.from_nxt, self.mine, self.other = from_prv, from_nxt, mine, other
        self.half = mine.shape[1]
        self.size = self.half // chunks
        self.c, self.nxt, self.prv, self.cf = along_context()
        self.relays, self.plains, self.mores, self.swaps = {}, {}, {}, {}

    def rows(self, k):
        return pl.ds(k * self.size, self.size)

    def win(self, owner, second, k):
        at = pl.multiple_of((owner * 2 + second) * self.half + k * self.size, 16)
        return pl.ds(at, self.size), slice(None)

    def start(self):
        up, down = {"context": self.nxt}, {"context": self.prv}
        part, push = self.part, self.wire.push
        for k in range(self.chunks):
            at = self.rows(k)
            self.relays[k] = (
                push(part.at[self.win(self.cf, 0, k)], self.from_prv.at[0, at, :], up),
                push(part.at[self.win(self.cf, 1, k)], self.from_nxt.at[0, at, :], down),
            )

    def relay(self, k):
        at, part, push = self.rows(k), self.part, self.wire.push
        up, down = {"context": self.nxt}, {"context": self.prv}
        self.relays[k][0].wait_recv()
        self.from_prv[0, at, :] = (
            self.from_prv[0, at, :].astype(f32) + part[self.win(self.nxt, 0, k)].astype(f32)
        ).astype(bf16)
        one = push(self.from_prv.at[0, at, :], self.from_prv.at[2, at, :], up)
        self.relays[k][1].wait_recv()
        self.from_nxt[0, at, :] = (
            self.from_nxt[0, at, :].astype(f32) + part[self.win(self.prv, 1, k)].astype(f32)
        ).astype(bf16)
        two = push(self.from_nxt.at[0, at, :], self.from_nxt.at[2, at, :], down)
        self.mores[k] = (one, two)
        self.plains[k] = (
            push(part.at[self.win(self.nxt, 1, k)], self.from_prv.at[1, at, :], up),
            push(part.at[self.win(self.prv, 0, k)], self.from_nxt.at[1, at, :], down),
        )

    def exchange(self, k):
        at = self.rows(k)
        self.mores[k][0].wait_recv()
        self.plains[k][1].wait_recv()
        self.mine[0, at, :] = (
            self.part[self.win(self.c, 0, k)].astype(f32)
            + self.from_nxt[1, at, :].astype(f32)
            + self.from_prv[2, at, :].astype(f32)
        ).astype(bf16)
        self.mores[k][1].wait_recv()
        self.plains[k][0].wait_recv()
        self.mine[1, at, :] = (
            self.part[self.win(self.c, 1, k)].astype(f32)
            + self.from_prv[1, at, :].astype(f32)
            + self.from_nxt[2, at, :].astype(f32)
        ).astype(bf16)
        to = {"tensor": 1 - lax.axis_index("tensor")}
        self.swaps[k] = self.wire.push(self.mine.at[:, at, :], self.other.at[:, at, :], to)

    def totals(self, k):
        self.swaps[k].wait_recv()
        at = self.rows(k)
        return [
            (
                pl.ds(second * self.half + k * self.size, self.size),
                self.mine[second, at, :].astype(f32) + self.other[second, at, :].astype(f32),
            )
            for second in range(2)
        ]


class ShardSum:
    def __init__(self, wire, both, came, from_down, from_up, pair, last, ranges):
        self.wire, self.both, self.came = wire, both, came
        self.from_down, self.from_up = from_down, from_up
        self.pair, self.last, self.ranges = pair, last, ranges
        self.shard = both.shape[2]
        self.half = self.shard // 2
        self.f, self.core, self.far, self.up, self.down = along_fsdp()
        self.side = lax.rem(lax.div(self.f, 2), 2)
        self.mine = lax.rem(self.f, 2)
        self.z = lax.div(self.f, 4)
        self.cores, self.plain, self.relay, self.more, self.cross = {}, {}, {}, {}, {}

    def cols(self, k):
        return pl.ds(*self.ranges[k])

    def block_cols(self, rel):
        size = 4 * self.shard
        return pl.ds(pl.multiple_of(lax.rem(self.z + rel, 4) * size, 128), size)

    def multiply(self, k, rel, left, right):
        tile = lax.dot_general(
            left, right, (((0,), (0,)), ((), ())), preferred_element_type=f32
        ).astype(bf16)
        cols = self.cols(k)
        for side in range(2):
            for core in range(2):
                lo = (2 * side + core) * self.shard
                place = lax.rem(core + self.mine, 2)
                self.both[place, 2 * rel + side, :, cols] = tile[lo : lo + self.shard]
        self.cores[k, rel] = self.wire.push(
            self.both.at[1, pl.ds(2 * rel, 2), :, cols],
            self.came.at[pl.ds(2 * rel, 2), :, cols],
            {"fsdp": self.core},
        )

    def block(self, rel, second, k):
        return pl.ds(2 * rel, 2), pl.ds(second * self.half, self.half), self.cols(k)

    def add_core(self, k, rel):
        self.cores[k, rel].wait_recv()
        at = pl.ds(2 * rel, 2), slice(None), self.cols(k)
        mine = (0,) + at
        self.both[mine] = (self.both[mine].astype(f32) + self.came[at].astype(f32)).astype(bf16)

    def start(self, k):
        got, cols, push = self.both.at[0], self.cols(k), self.wire.push
        up, down = {"fsdp": self.up}, {"fsdp": self.down}
        self.add_core(k, 2)
        self.relay[k] = (
            push(got.at[self.block(2, 0, k)], self.from_down.at[0, :, :, cols], up),
            push(got.at[self.block(2, 1, k)], self.from_up.at[0, :, :, cols], down),
        )
        self.add_core(k, 1)
        self.add_core(k, 3)
        self.add_core(k, 0)

    def relays(self, k):
        got, cols, push = self.both.at[0], self.cols(k), self.wire.push
        self.relay[k][0].wait_recv()
        at = (0, slice(None), slice(None), cols)
        self.from_down[at] = (
            self.from_down[at].astype(f32) + got[self.block(1, 0, k)].astype(f32)
        ).astype(bf16)
        one = push(self.from_down.at[at], self.from_down.at[2, :, :, cols], {"fsdp": self.up})
        self.relay[k][1].wait_recv()
        self.from_up[at] = (
            self.from_up[at].astype(f32) + got[self.block(3, 1, k)].astype(f32)
        ).astype(bf16)
        two = push(self.from_up.at[at], self.from_up.at[2, :, :, cols], {"fsdp": self.down})
        self.more[k] = (one, two)
        self.plain[k] = (
            push(got.at[self.block(1, 1, k)], self.from_down.at[1, :, :, cols], {"fsdp": self.up}),
            push(got.at[self.block(3, 0, k)], self.from_up.at[1, :, :, cols], {"fsdp": self.down}),
        )

    def across(self, k):
        got, cols, half = self.both.at[0], self.cols(k), self.half
        self.more[k][0].wait_recv()
        self.plain[k][1].wait_recv()
        self.pair[:, pl.ds(0, half), cols] = (
            got[self.block(0, 0, k)].astype(f32)
            + self.from_down[2, :, :, cols].astype(f32)
            + self.from_up[1, :, :, cols].astype(f32)
        ).astype(bf16)
        self.more[k][1].wait_recv()
        self.plain[k][0].wait_recv()
        self.pair[:, pl.ds(half, half), cols] = (
            got[self.block(0, 1, k)].astype(f32)
            + self.from_down[1, :, :, cols].astype(f32)
            + self.from_up[2, :, :, cols].astype(f32)
        ).astype(bf16)
        self.cross[k] = self.wire.push(
            self.pair.at[1 - self.side, :, cols], self.last.at[:, cols], {"fsdp": self.far}
        )

    def total(self, k):
        cols = self.cols(k)
        self.cross[k].wait_recv()
        return self.pair[self.side, :, cols].astype(f32) + self.last[:, cols].astype(f32)


def row_scratch(rows, width):
    return [pltpu.VMEM((3, rows // 2, width), bf16)] * 2 + [pltpu.VMEM((2, rows // 2, width), bf16)] * 2


def everyone_near():
    _, core, far, up, down = along_fsdp()
    _, nxt, prv, _ = along_context()
    return [{"fsdp": i} for i in (core, far, up, down)] + [
        {"context": nxt}, {"context": prv}, {"tensor": 1 - lax.axis_index("tensor")}
    ]


def half_turn(x):
    return pltpu.roll(x, HD // 2, 1)


def signal(sem, to):
    pl.semaphore_signal(sem, inc=1, device_id=to, device_id_type=MESH)


ORDER = (2, 1, 3, 0)
SMALL = (8, 512)


def layer_back_kernel(
    normed_hbm, dy_hbm, both_hbm, hidden_hbm, first_hbm, second_hbm,
    out_hbm, lin_hbm, probs_hbm,
    middle_ref, dy_ref, gain_ref, mixed_ref, query_ref, kv_ref,
    normed_one_ref, tokens_ref, cos_ref, sin_ref,
    result_ref, gt_ref, small_ref, attn_ref, mlp_hbm,
    part, from_prv, from_nxt, mine, other,
    left, right, both, came, from_down, from_up, pair, last, shard_out,
    probs, d_probs, d_low, low, d_branch, d_mixed, acc_k, acc_v, kv_send, kv_came,
    d_lin, swap_mine, swap_other, attn_own, attn_came, small_own, small_came,
    send, recv, local, free,
):
    wire, loads = Wire(send, recv), Loads(local)
    rows, width = middle_ref.shape
    q_cols, kv_cols = mixed_ref.shape[1], kv_ref.shape[2]
    heads = q_cols // HD
    span = hidden_hbm.shape[1]
    scale = HD ** (-0.5)
    c, nxt, prv, cf = along_context()
    f, core, far, up, down = along_fsdp()
    opposite = lax.rem(f + 8, lax.axis_size("fsdp"))
    C = lambda i: {"context": i}
    F = lambda i: {"fsdp": i}
    T = {"tensor": 1 - lax.axis_index("tensor")}

    def keep_small(at, values):
        for k in range(values.shape[1] // SMALL[1]):
            small_own[pl.ds(at + k, 1), :] = values[:, k * SMALL[1] : (k + 1) * SMALL[1]]

    load_part = loads.start(first_hbm, part)
    load_left = loads.start(normed_hbm, left)
    load_r0 = loads.start(both_hbm.at[:, pl.ds(0, span)], right.at[0])
    load_r1 = loads.start(both_hbm.at[:, pl.ds(span, span)], right.at[1])
    meet(everyone_near() + [C(cf), F(opposite)])

    one = RowSum(wire, part, from_prv, from_nxt, mine, other, 4)
    two = RowSum(wire, part, from_prv, from_nxt, mine, other, 4)
    mlp = ShardSum(wire, both, came, from_down, from_up, pair, last, [(k * span, span) for k in range(3)])
    attn = ShardSum(
        wire, both, came, from_down, from_up, pair, last,
        [(0, q_cols), (q_cols, q_cols), (2 * q_cols, 2 * kv_cols)],
    )
    load_part.wait()
    one.start()

    def weights(k, rel, slot):
        mlp.multiply(k, rel, left[:, mlp.block_cols(rel)], right[slot])

    load_left.wait()
    load_r0.wait()
    for rel in ORDER:
        weights(0, rel, 0)
    load_r0 = loads.start(hidden_hbm, right.at[0])
    mlp.start(0)
    one.relay(0)
    load_r1.wait()
    weights(1, 2, 1)
    one.relay(1)
    weights(1, 1, 1)
    one.relay(2)
    weights(1, 3, 1)
    one.relay(3)
    weights(1, 0, 1)
    load_left = loads.start(dy_hbm, left)
    mlp.start(1)
    mlp.relays(0)
    load_r0.wait()
    load_left.wait()
    weights(2, 2, 0)
    one.exchange(0)
    weights(2, 1, 0)
    weights(2, 3, 0)
    weights(2, 0, 0)
    one.exchange(1)
    mlp.start(2)
    signal(free.at[0], F(core))
    deep = left.shape[0]
    rest = width - deep
    load_out = (
        loads.start(out_hbm.at[pl.ds(0, deep)], left.at[:, pl.ds(0, q_cols)]),
        loads.start(out_hbm.at[pl.ds(deep, rest)], left.at[pl.ds(0, rest), pl.ds(q_cols, q_cols)]),
    )
    lin_cols = lin_hbm.shape[1]
    load_lin = (
        loads.start(lin_hbm.at[pl.ds(0, deep)], right.at[0, :, pl.ds(0, lin_cols)]),
        loads.start(lin_hbm.at[pl.ds(deep, rest)], right.at[1, pl.ds(0, rest), pl.ds(0, lin_cols)]),
    )
    load_probs = {h: loads.start(probs_hbm.at[h], probs.at[h % 2]) for h in range(2)}
    mlp.relays(1)
    one.exchange(2)

    gain_two = gain_ref[pl.ds(1, 1), :]
    gain_grad = jnp.zeros((1, width), f32)
    for k in range(4):
        if k == 1:
            one.exchange(3)
            mlp.relays(2)
            for j in range(4):
                wire.sent(*one.relays[j], *one.plains[j], *one.mores[j])
            signal(free.at[1], C(nxt))
            signal(free.at[2], C(prv))
            load_part = loads.start(second_hbm, part)
        if k == 3:
            load_part.wait()
            pl.semaphore_wait(free.at[1], 1)
            pl.semaphore_wait(free.at[2], 1)
            two.start()
            mlp.across(0)
        for at, grad in one.totals(k):
            mid = middle_ref[at, :]
            r = lax.rsqrt(jnp.mean(mid * mid, axis=-1, keepdims=True) + EPSILON)
            gain_grad += jnp.sum(grad * mid * r, axis=0, keepdims=True)
            scaled = grad * gain_two
            back = jnp.mean(scaled * mid, axis=-1, keepdims=True)
            value = dy_ref[at, :].astype(f32) + r * scaled - mid * (r * r * r * back)
            gt_ref[at, :] = value
            d_branch[at, :] = value.astype(bf16)
    wire.sent(*one.swaps.values())
    signal(free.at[3], T)
    keep_small(3, gain_grad)

    for copy in load_out:
        copy.wait()
    d_mixed[...] = (
        jnp.dot(d_branch[:, pl.ds(0, deep)], left[:, pl.ds(0, q_cols)], preferred_element_type=f32)
        + jnp.dot(
            d_branch[:, pl.ds(deep, rest)], left[pl.ds(0, rest), pl.ds(q_cols, q_cols)],
            preferred_element_type=f32,
        )
    ).astype(bf16)
    lane = lax.broadcasted_iota(jnp.int32, (1, HD), 1)
    sign = jnp.where(lane < HD // 2, 1.0, -1.0).astype(f32)

    def turn_back(w):
        return w * cos_ref[...] + half_turn(w * sin_ref[...]) * sign

    nt = (((1,), (1,)), ((), ()))
    tn = (((0,), (0,)), ((), ()))

    def head(h):
        cols = pl.ds(h * HD, HD)
        load_probs[h].wait()
        dm = d_mixed[:, cols]
        d_probs[...] = lax.dot_general(dm, kv_ref[1], nt, preferred_element_type=f32)
        for at in range(0, rows, 32):
            at = pl.ds(at, 32)
            p, dp = probs[h % 2, at, :], d_probs[at, :]
            inner = jnp.sum(p * dp, axis=-1, keepdims=True)
            d_low[at, :] = (p * (dp - inner)).astype(bf16)
            low[at, :] = p.astype(bf16)
        ds = d_low[...]
        dq = jnp.dot(ds, kv_ref[0], preferred_element_type=f32) * scale
        d_lin[:, cols] = turn_back(dq).astype(bf16)
        dk = lax.dot_general(ds, query_ref[:, cols], tn, preferred_element_type=f32)
        dv = lax.dot_general(low[...], dm, tn, preferred_element_type=f32)
        if h == 0:
            acc_k[...] = dk
            acc_v[...] = dv
        else:
            acc_k[...] += dk
            acc_v[...] += dv
        if h + 2 < heads:
            load_probs[h + 2] = loads.start(probs_hbm.at[h + 2], probs.at[h % 2])

    def leave(k):
        wire.sent(*[mlp.cores[k, rel] for rel in ORDER], *mlp.relay[k], *mlp.plain[k], *mlp.more[k])

    head(0)
    two.relay(0)
    leave(0)
    signal(free.at[4], F(up))
    signal(free.at[5], F(down))
    head(1)
    two.relay(1)
    two.relay(2)
    mlp.across(1)
    leave(1)
    signal(free.at[7], F(up))
    signal(free.at[8], F(down))
    pl.semaphore_wait(free.at[0], 1)
    for rel in ORDER:
        attn.multiply(0, rel, d_branch[:, attn.block_cols(rel)], mixed_ref[...])
    head(2)
    pl.semaphore_wait(free.at[4], 1)
    pl.semaphore_wait(free.at[5], 1)
    attn.start(0)
    head(3)
    pl.semaphore_wait(free.at[3], 1)
    two.exchange(0)
    mlp.across(2)
    leave(2)
    head(4)
    two.exchange(1)
    head(5)

    for k in range(4):
        kv_send[k, 0] = acc_k[pl.ds(k * rows, rows), :].astype(bf16)
        kv_send[k, 1] = acc_v[pl.ds(k * rows, rows), :].astype(bf16)
    kv = [
        wire.push(kv_send.at[nxt], kv_came.at[0], C(nxt)),
        wire.push(kv_send.at[prv], kv_came.at[1], C(prv)),
        wire.push(kv_send.at[cf], kv_came.at[2], C(cf)),
    ]
    two.relay(3)
    for rel in ORDER:
        attn.multiply(1, rel, normed_one_ref[:, attn.block_cols(rel)], d_lin[:, pl.ds(0, q_cols)])
    attn.relays(0)
    for k in range(3):
        shard_out[:, mlp.cols(k)] = mlp.total(k).astype(bf16)
    signal(free.at[6], F(far))
    for k in range(3):
        wire.sent(mlp.cross[k])
    pl.semaphore_wait(free.at[7], 1)
    pl.semaphore_wait(free.at[8], 1)
    attn.start(1)
    for copy in kv:
        copy.wait_recv()
    d_key = acc_k[pl.ds(pl.multiple_of(c * rows, 8), rows), :]
    d_value = acc_v[pl.ds(pl.multiple_of(c * rows, 8), rows), :]
    for k in range(3):
        d_key += kv_came[k, 0].astype(f32)
        d_value += kv_came[k, 1].astype(f32)
    d_lin[:, pl.ds(q_cols, kv_cols)] = turn_back(d_key * scale).astype(bf16)
    d_lin[:, pl.ds(q_cols + kv_cols, kv_cols)] = d_value.astype(bf16)
    for copy in load_lin:
        copy.wait()
    swap_mine[:, pl.ds(0, deep)] = lax.dot_general(
        d_lin[...], right[0, :, pl.ds(0, lin_cols)], nt, preferred_element_type=f32
    ).astype(bf16)
    swap_mine[:, pl.ds(deep, rest)] = lax.dot_general(
        d_lin[...], right[1, pl.ds(0, rest), pl.ds(0, lin_cols)], nt, preferred_element_type=f32
    ).astype(bf16)
    spread = [
        wire.push(shard_out, mlp_hbm.at[c], C(nxt)),
        wire.push(shard_out, mlp_hbm.at[c], C(prv)),
    ]
    keep = loads.start(shard_out, mlp_hbm.at[c])
    sizes = 64
    gain_grad = jnp.zeros((1, width), f32)
    for k in range(rows // sizes):
        at = pl.ds(k * sizes, sizes)
        mid = tokens_ref[at, :].astype(f32)
        r = lax.rsqrt(jnp.mean(mid * mid, axis=-1, keepdims=True) + EPSILON)
        gain_grad += jnp.sum(swap_mine[at, :].astype(f32) * mid * r, axis=0, keepdims=True)
    keep_small(0, gain_grad)
    keep_small(6, jnp.sum(d_lin[...].astype(f32), axis=0, keepdims=True))
    small_step = wire.push(small_own, small_came.at[0], T)
    swaps = []

    def swap(k):
        at = pl.ds(k * sizes, sizes)
        swaps.append(wire.push(swap_mine.at[at, :], swap_other.at[at, :], T))

    for k in range(3):
        swap(k)
    for rel in ORDER:
        attn.multiply(
            2, rel, normed_one_ref[:, attn.block_cols(rel)], d_lin[:, pl.ds(q_cols, 2 * kv_cols)]
        )
    small_step.wait_recv()
    gain_rows = lax.broadcasted_iota(jnp.int32, SMALL, 0) < 3
    small_came[1] = small_own[...] + jnp.where(gain_rows, small_came[0], 0.0)
    small_step = wire.push(small_came.at[1], small_came.at[2], F(core))
    attn.start(2)
    pl.semaphore_wait(free.at[6], 1)
    attn.across(0)
    swap(3)
    small_step.wait_recv()
    small_came[3] = small_came[1] + small_came[2]
    small_steps = [
        wire.push(small_came.at[3], small_came.at[4 + k], F(to)) for k, to in enumerate((up, down, opposite))
    ]
    attn.relays(1)
    attn.relays(2)
    for step in small_steps:
        step.wait_recv()
    small_came[7] = (small_came[3] + small_came[6]) + (small_came[4] + small_came[5])
    small_step = wire.push(small_came.at[7], small_came.at[8], F(far))

    half = shard_out.shape[0] // 2
    near, rest_of = {}, {}

    def to_ranks(k):
        cols = attn.cols(k)
        attn_own[:, cols] = attn.total(k).astype(bf16)
        w = attn_own.at[:, cols]
        near[k] = (
            wire.push(w, attn_came.at[0, :, cols], C(nxt)),
            wire.push(w, attn_came.at[1, :, cols], C(prv)),
        )

    def onward(k):
        cols, first, second = attn.cols(k), pl.ds(0, half), pl.ds(half, half)
        near[k][0].wait_recv()
        near[k][1].wait_recv()
        rest_of[k] = (
            wire.push(attn_came.at[0, first, cols], attn_came.at[2, first, cols], C(nxt)),
            wire.push(attn_came.at[1, second, cols], attn_came.at[2, second, cols], C(prv)),
        )

    attn.across(1)
    attn.across(2)
    two.exchange(2)
    two.exchange(3)

    gain_one = gain_ref[pl.ds(0, 1), :]
    for k in range(rows // sizes):
        swaps[k].wait_recv()
        at = pl.ds(k * sizes, sizes)
        grad = swap_mine[at, :].astype(f32) + swap_other[at, :].astype(f32)
        mid = tokens_ref[at, :].astype(f32)
        r = lax.rsqrt(jnp.mean(mid * mid, axis=-1, keepdims=True) + EPSILON)
        scaled = grad * gain_one
        back = jnp.mean(scaled * mid, axis=-1, keepdims=True)
        gt_ref[at, :] = gt_ref[at, :] + r * scaled - mid * (r * r * r * back)
    to_ranks(0)
    small_step.wait_recv()
    small_came[9] = small_came[7] + small_came[8]
    spread[0].wait_recv()
    w = mlp_hbm.at[prv, pl.ds(0, half)]
    spread.append(wire.push(w, w, C(nxt)))
    spread[1].wait_recv()
    w = mlp_hbm.at[nxt, pl.ds(half, half)]
    spread.append(wire.push(w, w, C(prv)))
    to_ranks(1)
    to_ranks(2)
    small_steps = [
        wire.push(small_came.at[9], small_came.at[10 + k], C(to)) for k, to in enumerate((nxt, prv, cf))
    ]
    onward(0)
    for k in range(4):
        for at, total in two.totals(k):
            result_ref[at, :] = (middle_ref[at, :] + total).astype(bf16)
    onward(1)
    onward(2)
    for k in range(3):
        cols = attn.cols(k)
        rest_of[k][0].wait_recv()
        rest_of[k][1].wait_recv()
        attn_ref[:, cols] = (attn_own[:, cols].astype(f32) + attn_came[2, :, cols].astype(f32)) + (
            attn_came[0, :, cols].astype(f32) + attn_came[1, :, cols].astype(f32)
        )
    for step in small_steps:
        step.wait_recv()
    small_ref[...] = (small_came[9] + small_came[12]) + (small_came[10] + small_came[11])
    spread[2].wait_recv()
    spread[3].wait_recv()
    keep.wait()
    wire.drain()


def layer_back(hbm, near, cid=4):
    normed, dy, both, hidden, first, second, out, lin, probs = hbm
    group, width = normed.shape
    rows = group // 4
    shard, span = width // 16, hidden.shape[1]
    lin_cols = lin.shape[1]
    q_cols = out.shape[1]
    sems = 2 * 28 + 2 * (12 + 3 * 7) + 3 + 4 + 4 + 12 + 9
    return pl.pallas_call(
        layer_back_kernel,
        out_shape=(
            jax.ShapeDtypeStruct((rows, width), bf16),
            jax.ShapeDtypeStruct((rows, width), f32),
            jax.ShapeDtypeStruct(SMALL, f32),
            jax.ShapeDtypeStruct((shard, lin_cols + q_cols), f32),
            jax.ShapeDtypeStruct((4, shard, 3 * span), bf16),
        ),
        in_specs=[ANY] * len(hbm) + [VM] * len(near),
        out_specs=(VM, VM, VM, VM, ANY),
        scratch_shapes=[pltpu.VMEM((group, width), bf16)]
        + row_scratch(rows, width)
        + [
            pltpu.VMEM((group, width), bf16),
            pltpu.VMEM((2, group, span), bf16),
            pltpu.VMEM((2, 8, shard, 3 * span), bf16),
            pltpu.VMEM((8, shard, 3 * span), bf16),
            pltpu.VMEM((3, 2, shard // 2, 3 * span), bf16),
            pltpu.VMEM((3, 2, shard // 2, 3 * span), bf16),
            pltpu.VMEM((2, shard, 3 * span), bf16),
            pltpu.VMEM((shard, 3 * span), bf16),
            pltpu.VMEM((shard, 3 * span), bf16),
            pltpu.VMEM((2, rows, group), f32),
            pltpu.VMEM((rows, group), f32),
            pltpu.VMEM((rows, group), bf16),
            pltpu.VMEM((rows, group), bf16),
            pltpu.VMEM((rows, width), bf16),
            pltpu.VMEM((rows, q_cols), bf16),
            pltpu.VMEM((group, HD), f32),
            pltpu.VMEM((group, HD), f32),
            pltpu.VMEM((4, 2, rows, HD), bf16),
            pltpu.VMEM((3, 2, rows, HD), bf16),
            pltpu.VMEM((rows, lin_cols), bf16),
            pltpu.VMEM((rows, width), bf16),
            pltpu.VMEM((rows, width), bf16),
            pltpu.VMEM((shard, lin_cols + q_cols), bf16),
            pltpu.VMEM((3, shard, lin_cols + q_cols), bf16),
            pltpu.VMEM(SMALL, f32),
            pltpu.VMEM((13,) + SMALL, f32),
            pltpu.SemaphoreType.DMA((sems,)),
            pltpu.SemaphoreType.DMA((sems,)),
            pltpu.SemaphoreType.DMA((18,)),
            pltpu.SemaphoreType.REGULAR((9,)),
        ],
        compiler_params=pltpu.CompilerParams(
            collective_id=cid, has_side_effects=True, vmem_limit_bytes=63 << 20
        ),
        name="layer_back",
    )(*hbm, *near)


class Blocks:
    def __init__(self, wire, ref, shard, cols=None):
        self.wire, self.ref, self.shard, self.half = wire, ref, shard, shard // 2
        self.cols = slice(None) if cols is None else cols
        self.f, self.core, self.far, self.up, self.down = along_fsdp()
        n = lax.axis_size("fsdp")
        self.opposite = lax.rem(self.f + 8, n)
        self.sibling = []

    def pair(self, i):
        return i + 2 - 4 * lax.rem(lax.div(i, 2), 2)

    def win(self, owner, lo=0, size=None):
        at = pl.multiple_of(owner * self.shard + lo, 16)
        return self.ref.at[pl.ds(at, size or self.shard), self.cols]

    def push(self, w, to):
        return self.wire.push(w, w, {"fsdp": to})

    def to_core(self, w):
        self.sibling.append(self.push(w, self.core))

    def ex(self):
        w = self.win(self.f)
        self.from_far = self.push(w, self.far)
        self.to_core(w)

    def ez(self):
        w = self.win(self.f)
        self.from_down = self.push(w, self.up)
        self.from_up = self.push(w, self.down)

    def e0(self):
        self.ex()
        self.ez()

    def e1(self):
        self.from_far.wait_recv()
        w = self.win(self.far)
        self.far_down = self.push(w, self.up)
        self.far_up = self.push(w, self.down)
        self.to_core(w)

    def relay(self, below, above, one, two):
        one.wait_recv()
        first = self.push(self.win(below, 0, self.half), self.up)
        self.to_core(self.win(below))
        two.wait_recv()
        second = self.push(self.win(above, self.half, self.half), self.down)
        self.to_core(self.win(above))
        return first, second

    def e2(self):
        self.last = self.relay(self.down, self.up, self.from_down, self.from_up)

    def e3(self):
        self.last += self.relay(self.pair(self.down), self.pair(self.up), self.far_down, self.far_up)

    def e4(self):
        for k, copy in enumerate(self.last):
            copy.wait_recv()
            owner = self.opposite if k < 2 else self.pair(self.opposite)
            self.to_core(self.win(owner, self.half * (k % 2), self.half))

    def end(self):
        for copy in self.sibling:
            copy.wait_recv()


def layer_front_kernel(
    query_hbm, key_hbm, value_hbm, out_hbm, gate_hbm, lift_hbm, down_hbm, dy_hbm,
    gains_ref, tokens_ref, cos_ref, sin_ref, seg_q_ref, seg_k_ref, bias_ref,
    middle_ref, normed_one_ref, mixed_ref, q_ref, kv_ref, gain_ref,
    normed_hbm, dyg_hbm, lin_hbm, outf_hbm, probs_hbm,
    both_hbm, hidden_hbm, first_hbm, second_hbm,
    gains, wl, wo, wm, dyg, normed, mask, probs, part, other, d_hidden,
    low, pair, d_both, hidden, first, second,
    send, recv, local,
):
    wire, loads = Wire(send, recv), Loads(local)
    rows, width = tokens_ref.shape
    group = dyg.shape[0]
    shard, q_cols = query_hbm.shape
    kv_cols = key_hbm.shape[1]
    heads = q_cols // HD
    hidden_cols = gate_hbm.shape[1]
    span = hidden.shape[1]
    overlap = 4 * span - hidden_cols
    scale = HD ** (-0.5)
    c, nxt, prv, cf = along_context()
    f, core, far, up, down = along_fsdp()
    C = lambda i: {"context": i}
    T = {"tensor": 1 - lax.axis_index("tensor")}
    mine = pl.ds(pl.multiple_of(f * shard, 16), shard)
    group_rows = lambda owner, lo=0, size=rows: pl.ds(pl.multiple_of(owner * rows + lo, 16), size)
    start = pl.multiple_of(c * span - lax.div(c, 3) * overlap, 128)

    own = [
        loads.start(query_hbm, wl.at[mine, pl.ds(0, q_cols)]),
        loads.start(key_hbm, wl.at[mine, pl.ds(q_cols, kv_cols)]),
        loads.start(value_hbm, wl.at[mine, pl.ds(q_cols + kv_cols, kv_cols)]),
        loads.start(out_hbm, wo.at[mine, :]),
        loads.start(dy_hbm, dyg.at[group_rows(c), :]),
    ]
    sizes_of = (512, 384, span - 896)
    offsets = (0, 512, 896)
    big = [
        [
            loads.start(
                w.at[:, pl.ds(start + off, n)], wm.at[mine, pl.ds(3 * off + k * n, n)]
            )
            for k, w in enumerate((down_hbm, gate_hbm, lift_hbm))
        ]
        for off, n in zip(offsets, sizes_of)
    ]
    tile = gains_ref.shape[0]
    gains[pl.ds(pl.multiple_of(f * tile, 16), tile), :] = gains_ref[...]
    meet(everyone_near() + [C(cf)])
    G = Blocks(wire, gains, tile)
    Q = Blocks(wire, wl, shard)
    O = Blocks(wire, wo, shard)
    A, B, D = (Blocks(wire, wm, shard, pl.ds(3 * off, 3 * n)) for off, n in zip(offsets, sizes_of))

    G.e0()
    for copy in own:
        copy.wait()
    Q.e0()
    w = dyg.at[group_rows(c), :]
    dy_copies = [wire.push(w, w, C(nxt)), wire.push(w, w, C(prv))]
    G.e1()
    O.e0()
    for copy in big[0]:
        copy.wait()
    A.ex()
    here = c * rows + lax.broadcasted_iota(jnp.int32, (rows, group), 0)
    there = lax.broadcasted_iota(jnp.int32, (rows, group), 1)
    allowed = (seg_q_ref[...] == seg_k_ref[...]) & (there <= here)
    mask[...] = jnp.where(allowed, 0.0, -1e30).astype(f32)
    G.e2()
    G.e3()
    Q.e1()
    G.e4()
    G.end()
    for k in range(2):
        gain_ref[pl.ds(k, 1), :] = jnp.concatenate(
            [gains[pl.ds(i * tile + k, 1), :].astype(f32)[:, :shard] for i in range(width // shard)], axis=1
        )
    sizes = 64
    for at in range(0, rows, sizes):
        at = pl.ds(at, sizes)
        x = tokens_ref[at, :].astype(f32)
        r = lax.rsqrt(jnp.mean(x * x, axis=-1, keepdims=True) + EPSILON)
        normed_one_ref[at, :] = (x * r * gain_ref[pl.ds(0, 1), :]).astype(bf16)
    Q.e2()
    Q.e3()
    O.e1()
    A.ez()
    Q.e4()
    for copy in big[1] + big[2]:
        copy.wait()
    B.ex()
    D.ex()
    Q.end()

    sign = jnp.where(lax.broadcasted_iota(jnp.int32, (1, HD), 1) < HD // 2, -1.0, 1.0).astype(f32)

    def turned(v):
        return v * cos_ref[...] + half_turn(v) * sign * sin_ref[...]

    def linear(at, size):
        cols = pl.ds(at, size)
        return jnp.dot(normed_one_ref[...], wl[:, cols], preferred_element_type=f32) + bias_ref[:, cols]

    lin = linear(q_cols, 2 * kv_cols)
    kv_ref[0, group_rows(c), :] = turned(lin[:, :kv_cols]).astype(bf16)
    kv_ref[1, group_rows(c), :] = lin[:, kv_cols:].astype(bf16)
    kv = []
    for k in range(2):
        w = kv_ref.at[k, group_rows(c), :]
        kv.append([wire.push(w, w, C(i)) for i in (cf, nxt, prv)])
    for h in range(0, heads, 2):
        lin = linear(h * HD, 2 * HD)
        q_ref[:, pl.ds(h * HD, HD)] = turned(lin[:, :HD]).astype(bf16)
        q_ref[:, pl.ds((h + 1) * HD, HD)] = turned(lin[:, HD:]).astype(bf16)
    O.e2()
    O.e3()
    A.e1()
    keep = [loads.start(wl, lin_hbm)]
    half = rows // 2
    dy_copies[0].wait_recv()
    w = dyg.at[group_rows(prv, 0, half), :]
    dy_copies.append(wire.push(w, w, C(nxt)))
    dy_copies[1].wait_recv()
    w = dyg.at[group_rows(nxt, half, half), :]
    dy_copies.append(wire.push(w, w, C(prv)))
    O.e4()
    for copy in kv[0]:
        copy.wait_recv()

    nt = (((1,), (1,)), ((), ()))
    probs_out = {}

    def head(h):
        cols = pl.ds(h * HD, HD)
        if h >= 2:
            probs_out[h - 2].wait()
        probs[h % 2] = lax.dot_general(q_ref[:, cols], kv_ref[0], nt, preferred_element_type=f32)
        for at in range(0, rows, 32):
            at = pl.ds(at, 32)
            s = probs[h % 2, at, :] * scale + mask[at, :]
            e = jnp.exp(s - jnp.max(s, axis=-1, keepdims=True))
            p = e * (1.0 / jnp.sum(e, axis=-1, keepdims=True))
            probs[h % 2, at, :] = p
            low[at, :] = p.astype(bf16)
        probs_out[h] = loads.start(probs.at[h % 2], probs_hbm.at[h])
        if h == 0:
            for copy in kv[1]:
                copy.wait_recv()
        mixed_ref[:, cols] = jnp.dot(low[...], kv_ref[1], preferred_element_type=f32).astype(bf16)

    for h in range(heads):
        head(h)
        if h == 3:
            A.e2()
    probs_out[heads - 2].wait()
    probs_out[heads - 1].wait()
    O.end()
    sizes = 32
    chunks = rows // sizes
    swaps = []
    for k in range(chunks // 2):
        at = pl.ds(2 * k * sizes, 2 * sizes)
        part[at, :] = lax.dot_general(mixed_ref[at, :], wo[...], nt, preferred_element_type=f32).astype(bf16)
        for j in range(2):
            at = pl.ds((2 * k + j) * sizes, sizes)
            swaps.append(wire.push(part.at[at, :], other.at[at, :], T))
    keep.append(loads.start(wo, outf_hbm))
    B.ez()
    A.e3()
    for copy in dy_copies[2:]:
        copy.wait_recv()
    keep.append(loads.start(dyg, dyg_hbm))

    from_prv, from_nxt, last = {}, {}, []
    cut = sizes // 2

    def forward(k):
        from_prv[k].wait_recv()
        w = normed.at[group_rows(prv, k * sizes, cut), :]
        last.append(wire.push(w, w, C(nxt)))
        from_nxt[k].wait_recv()
        w = normed.at[group_rows(nxt, k * sizes + cut, cut), :]
        last.append(wire.push(w, w, C(prv)))

    for k in range(chunks):
        at = pl.ds(k * sizes, sizes)
        swaps[k].wait_recv()
        mid = tokens_ref[at, :].astype(f32) + (part[at, :].astype(f32) + other[at, :].astype(f32))
        middle_ref[at, :] = mid
        r = lax.rsqrt(jnp.mean(mid * mid, axis=-1, keepdims=True) + EPSILON)
        normed[group_rows(c, k * sizes, sizes), :] = (mid * r * gain_ref[pl.ds(1, 1), :]).astype(bf16)
        w = normed.at[group_rows(c, k * sizes, sizes), :]
        from_prv[k] = wire.push(w, w, C(nxt))
        from_nxt[k] = wire.push(w, w, C(prv))
        if k == 1:
            B.e1()
        if k == 2:
            A.e4()
        if k == 3:
            D.ez()
        if k == 5:
            B.e2()
    A.end()
    for k in range(3):
        forward(k)

    skip = lax.div(c, 3) * overlap

    def feed(owner, piece):
        at = group_rows(owner)
        off, n = offsets[piece], sizes_of[piece]
        down_at, wide = pl.ds(3 * off, n), pl.ds(3 * off + n, 2 * n)
        hidden_at, both_at = pl.ds(off, n), pl.ds(2 * off, 2 * n)
        pair[:, pl.ds(0, 2 * n)] = jnp.dot(normed[at, :], wm[:, wide], preferred_element_type=f32)
        d_hidden[:, pl.ds(0, n)] = jnp.dot(dyg[at, :], wm[:, down_at], preferred_element_type=f32)
        step = 32
        for k in range(0, rows, step):
            here, rows_here = pl.ds(k, step), group_rows(owner, k, step)
            gate, lift = pair[here, pl.ds(0, n)], pair[here, pl.ds(n, n)]
            dh = d_hidden[here, pl.ds(0, n)]
            sig = 1.0 / (1.0 + jnp.exp(-gate))
            swish = gate * sig
            up_part = swish * lift
            if piece == 0:
                live = lax.broadcasted_iota(jnp.int32, (1, n), 1) >= skip
                dh = jnp.where(live, dh, 0.0)
                up_part = jnp.where(live, up_part, 0.0)
            hidden[rows_here, hidden_at] = up_part.astype(bf16)
            d_both[rows_here, pl.ds(2 * off, n)] = (
                dh * lift * sig * (1.0 + gate * (1.0 - sig))
            ).astype(bf16)
            d_both[rows_here, pl.ds(2 * off + n, n)] = (dh * swish).astype(bf16)
        one = lax.dot_general(d_both[at, both_at], wm[:, wide], nt, preferred_element_type=f32)
        two = lax.dot_general(hidden[at, hidden_at], wm[:, down_at], nt, preferred_element_type=f32)
        if piece:
            one += first[at, :].astype(f32)
            two += second[at, :].astype(f32)
        first[at, :] = one.astype(bf16)
        second[at, :] = two.astype(bf16)
        keep.append(loads.start(hidden.at[at, hidden_at], hidden_hbm.at[at, hidden_at]))
        for k in range(2):
            keep.append(
                loads.start(
                    d_both.at[at, pl.ds(2 * off + k * n, n)], both_hbm.at[at, pl.ds(k * span + off, n)]
                )
            )
        if piece == 2:
            for src, dst in ((first, first_hbm), (second, second_hbm)):
                keep.append(loads.start(src.at[at, :], dst.at[at, :]))

    feed(c, 0)
    for k in range(3, 6):
        forward(k)
    B.e3()
    D.e1()
    for k in range(6, chunks):
        forward(k)
    feed(prv, 0)
    D.e2()
    B.e4()
    feed(nxt, 0)
    B.end()
    feed(c, 1)
    D.e3()
    feed(prv, 1)
    feed(nxt, 1)
    for copy in last:
        copy.wait_recv()
    keep.append(loads.start(normed, normed_hbm))
    feed(cf, 0)
    D.e4()
    feed(cf, 1)
    D.end()
    for owner in (c, prv, nxt, cf):
        feed(owner, 2)
    for copy in keep:
        copy.wait()
    wire.drain()


def layer_front(hbm, near, span, cid=1):
    query, key, value, out, gate, lift, down, dy = hbm
    rows, width = dy.shape
    group = 4 * rows
    shard, q_cols = query.shape
    lin_cols = q_cols + 2 * key.shape[1]
    heads = q_cols // HD
    sems = 6 * 19 + 4 + 6 + 8 + 32
    S = jax.ShapeDtypeStruct
    return pl.pallas_call(
        layer_front_kernel,
        out_shape=(
            S((rows, width), f32),
            S((rows, width), bf16),
            S((rows, q_cols), bf16),
            S((rows, q_cols), bf16),
            S((2, group, HD), bf16),
            S((2, width), f32),
            S((group, width), bf16),
            S((group, width), bf16),
            S((width, lin_cols), bf16),
            S((width, q_cols), bf16),
            S((heads, rows, group), f32),
        )
        + (S((group, 2 * span), bf16), S((group, span), bf16))
        + (S((group, width), bf16),) * 2,
        in_specs=[ANY] * len(hbm) + [VM] * len(near),
        out_specs=(VM,) * 6 + (ANY,) * 9,
        scratch_shapes=[
            pltpu.VMEM((width // shard * near[0].shape[0], 128), bf16),
            pltpu.VMEM((width, lin_cols), bf16),
            pltpu.VMEM((width, q_cols), bf16),
            pltpu.VMEM((width, 3 * span), bf16),
            pltpu.VMEM((group, width), bf16),
            pltpu.VMEM((group, width), bf16),
            pltpu.VMEM((rows, group), f32),
            pltpu.VMEM((2, rows, group), f32),
            pltpu.VMEM((rows, width), bf16),
            pltpu.VMEM((rows, width), bf16),
            pltpu.VMEM((rows, 512), f32),
            pltpu.VMEM((rows, group), bf16),
            pltpu.VMEM((rows, 1024), f32),
            pltpu.VMEM((group, 2 * span), bf16),
            pltpu.VMEM((group, span), bf16),
            pltpu.VMEM((group, width), bf16),
            pltpu.VMEM((group, width), bf16),
            pltpu.SemaphoreType.DMA((sems,)),
            pltpu.SemaphoreType.DMA((sems,)),
            pltpu.SemaphoreType.DMA((14 + heads + 4 + 44,)),
        ],
        compiler_params=pltpu.CompilerParams(
            collective_id=cid, has_side_effects=True, vmem_limit_bytes=63 << 20
        ),
        name="layer_front",
    )(*hbm, *near)


def rope_tables(positions, head_width):
    half_width = head_width // 2
    freq_index = jnp.arange(half_width).astype(jnp.float32)
    inverse = ROPE_BASE ** (-(freq_index * 2.0 / head_width))
    angles = positions.astype(jnp.float32)[:, None] * inverse[None, :]
    cosine = jnp.cos(angles)
    sine_table = jnp.sin(angles)
    return (jnp.concatenate([cosine, cosine], -1), jnp.concatenate([sine_table, sine_table], -1))


def segment_info(seq_lengths, total_rows):
    ends_at = jnp.cumsum(seq_lengths)
    places = jnp.arange(total_rows, dtype=jnp.int32)
    passed = places[:, None] >= ends_at[None, :]
    segment = jnp.sum(passed.astype(jnp.int32), axis=1)
    starts = jnp.sum(jnp.where(passed, seq_lengths[None, :], 0), axis=1)
    return (segment, places - starts)


def on_device(
    tokens,
    cotangent,
    lengths,
    gain_attn,
    w_query,
    b_query,
    w_key,
    b_key,
    w_value,
    b_value,
    w_out,
    gain_mlp,
    w_gate,
    w_up,
    w_down,
):
    row_count, width = tokens.shape
    context_size = lax.axis_size("context")
    context_rank = lax.axis_index("context")
    fsdp_rank = lax.axis_index("fsdp")
    shard = w_query.shape[0]
    query_cols, kv_cols, hidden_cols = w_query.shape[1], w_key.shape[1], w_gate.shape[1]
    group_rows = row_count * context_size
    segment_all, position_all = segment_info(lengths[0], group_rows)
    first_row = context_rank * row_count
    segment_mine = lax.dynamic_slice_in_dim(segment_all, first_row, row_count)
    position_mine = lax.dynamic_slice_in_dim(position_all, first_row, row_count)
    cosine, sine_table = rope_tables(position_mine, HD)

    span = -(-(hidden_cols // 128) // context_size) * 128
    overlap = context_size * span - hidden_cols
    gains = jnp.pad(jnp.stack([gain_attn, gain_mlp]), ((0, 30), (0, 128 - shard)))
    bias = jnp.concatenate([b_query, b_key, b_value]).astype(f32)[None]
    (
        middle, normed_one, mixed, query_heads, kv_group, gain_full,
        normed_group, dy_group, lin_full, out_turned, probs,
        d_both, hidden, d_normed_part, mlp_part,
    ) = layer_front(
        (w_query, w_key, w_value, w_out.T, w_gate, w_up, w_down.T, cotangent),
        (
            gains, tokens, cosine, sine_table, segment_mine[:, None], segment_all[None], bias,
        ),
        span,
    )
    result, grad_tokens, small, attn_shard, mlp_all = layer_back(
        (
            normed_group, dy_group, d_both, hidden, d_normed_part, mlp_part,
            out_turned, lin_full, probs,
        ),
        (
            middle, cotangent, gain_full, mixed, query_heads, kv_group, normed_one, tokens, cosine, sine_table,
        ),
    )

    def whole(k):
        parts = [mlp_all[i, :, k * span : (k + 1) * span] for i in range(context_size)]
        parts[-1] = parts[-1][:, overlap:]
        return jnp.concatenate(parts, axis=1).astype(f32)

    small = small.reshape(-1)
    own = lambda at: lax.dynamic_slice_in_dim(small, at + fsdp_rank * shard, shard)
    bias_total = small[2 * width :]
    at_query = query_cols
    at_key = at_query + query_cols
    at_value = at_key + kv_cols
    return (
        result,
        grad_tokens,
        own(0),
        attn_shard[:, at_query:at_key],
        bias_total[:query_cols],
        attn_shard[:, at_key:at_value],
        bias_total[query_cols : query_cols + kv_cols],
        attn_shard[:, at_value:],
        bias_total[query_cols + kv_cols :],
        attn_shard[:, :query_cols].T,
        own(width),
        whole(0),
        whole(1),
        whole(2).T,
    )


def solution(mesh):
    return jax.shard_map(
        on_device,
        mesh=mesh,
        in_specs=(
            P(("fsdp", "context"), None),
            P(("fsdp", "context"), None),
            P("fsdp", None),
            P("fsdp"),
            P("fsdp", "tensor"),
            P("tensor"),
            P("fsdp", "tensor"),
            P("tensor"),
            P("fsdp", "tensor"),
            P("tensor"),
            P("tensor", "fsdp"),
            P("fsdp"),
            P("fsdp", "tensor"),
            P("fsdp", "tensor"),
            P("tensor", "fsdp"),
        ),
        out_specs=(
            P(("fsdp", "context"), None),
            P(("fsdp", "context"), None),
            P("fsdp"),
            P("fsdp", "tensor"),
            P("tensor"),
            P("fsdp", "tensor"),
            P("tensor"),
            P("fsdp", "tensor"),
            P("tensor"),
            P("tensor", "fsdp"),
            P("fsdp"),
            P("fsdp", "tensor"),
            P("fsdp", "tensor"),
            P("tensor", "fsdp"),
        ),
        check_vma=False,
    )
```

```python
import math

import jax
import jax.numpy as jnp
import numpy as np
from jax import lax
from jax.experimental import pallas as pl
from jax.experimental.pallas import tpu as pltpu
from jax.sharding import PartitionSpec as P

HD = 128
MESH = pl.DeviceIdType.MESH
ANY = pl.BlockSpec(memory_space=pl.ANY)
VM = pl.BlockSpec(memory_space=pltpu.VMEM)
f32, bf16 = jnp.float32, jnp.bfloat16

ROPE_BASE = 1000000.0
EPSILON = 1e-06
INVERSE = np.tile(ROPE_BASE ** (-(np.arange(HD // 2) * 2.0 / HD)), 2).astype(np.float32)[None]

def meet(targets):
    barrier = pltpu.get_barrier_semaphore()
    for t in targets:
        pl.semaphore_signal(barrier, inc=1, device_id=t, device_id_type=MESH)
    pl.semaphore_wait(barrier, len(targets))


class Wire:
    def __init__(self, send, recv):
        self.send, self.recv, self.used, self.started = send, recv, 0, []

    def push(self, src, dst, to):
        k = self.used
        self.used += 1
        copy = pltpu.make_async_remote_copy(
            src, dst, self.send.at[k], self.recv.at[k], device_id=to, device_id_type=MESH
        )
        copy.start()
        self.started.append(copy)
        return copy

    def sent(self, *copies):
        for copy in copies:
            copy.wait_send()
            self.started = [other for other in self.started if other is not copy]

    def drain(self):
        self.sent(*list(self.started))


class Loads:
    def __init__(self, sems):
        self.sems, self.used = sems, 0

    def start(self, src, dst):
        copy = pltpu.make_async_copy(src, dst, self.sems.at[self.used])
        self.used += 1
        copy.start()
        return copy


def along_context():
    c, m = lax.axis_index("context"), lax.axis_size("context")
    return c, lax.rem(c + 1, m), lax.rem(c + m - 1, m), lax.rem(c + 2, m)


def along_fsdp():
    f, n = lax.axis_index("fsdp"), lax.axis_size("fsdp")
    core = f + 1 - 2 * lax.rem(f, 2)
    far = f + 2 - 4 * lax.rem(lax.div(f, 2), 2)
    return f, core, far, lax.rem(f + 4, n), lax.rem(f + n - 4, n)


class RowSum:
    def __init__(self, wire, part, source, early, from_prv, from_nxt, mine, other, chunks):
        self.wire, self.part, self.source, self.chunks = wire, part, source, chunks
        self.early_prv, self.early_nxt = early
        self.from_prv, self.from_nxt, self.mine, self.other = from_prv, from_nxt, mine, other
        self.half = mine.shape[1]
        self.size = self.half // chunks
        self.c, self.nxt, self.prv, self.cf = along_context()
        self.relays, self.plains, self.mores, self.swaps = {}, {}, {}, {}

    def rows(self, k):
        return pl.ds(k * self.size, self.size)

    def win(self, owner, second, k):
        at = pl.multiple_of((owner * 2 + second) * self.half + k * self.size, 16)
        return pl.ds(at, self.size), slice(None)

    def start(self):
        up, down = {"context": self.nxt}, {"context": self.prv}
        source, push = self.source, self.wire.push
        for k in range(self.chunks):
            at = self.rows(k)
            self.relays[k] = (
                push(source.at[self.win(self.cf, 0, k)], self.early_prv.at[at, :], up),
                push(source.at[self.win(self.cf, 1, k)], self.early_nxt.at[at, :], down),
            )

    def relay(self, k):
        at, part, source, push = self.rows(k), self.part, self.source, self.wire.push
        up, down = {"context": self.nxt}, {"context": self.prv}
        self.relays[k][0].wait_recv()
        self.early_prv[at, :] = (
            self.early_prv[at, :].astype(f32) + part[self.win(self.nxt, 0, k)].astype(f32)
        ).astype(bf16)
        one = push(self.early_prv.at[at, :], self.from_prv.at[1, at, :], up)
        self.relays[k][1].wait_recv()
        self.early_nxt[at, :] = (
            self.early_nxt[at, :].astype(f32) + part[self.win(self.prv, 1, k)].astype(f32)
        ).astype(bf16)
        two = push(self.early_nxt.at[at, :], self.from_nxt.at[1, at, :], down)
        self.mores[k] = (one, two)
        self.plains[k] = (
            push(source.at[self.win(self.nxt, 1, k)], self.from_prv.at[0, at, :], up),
            push(source.at[self.win(self.prv, 0, k)], self.from_nxt.at[0, at, :], down),
        )

    def exchange(self, k):
        at = self.rows(k)
        self.mores[k][0].wait_recv()
        self.plains[k][1].wait_recv()
        self.mine[0, at, :] = (
            self.part[self.win(self.c, 0, k)].astype(f32)
            + self.from_nxt[0, at, :].astype(f32)
            + self.from_prv[1, at, :].astype(f32)
        ).astype(bf16)
        self.mores[k][1].wait_recv()
        self.plains[k][0].wait_recv()
        self.mine[1, at, :] = (
            self.part[self.win(self.c, 1, k)].astype(f32)
            + self.from_prv[0, at, :].astype(f32)
            + self.from_nxt[1, at, :].astype(f32)
        ).astype(bf16)
        to = {"tensor": 1 - lax.axis_index("tensor")}
        self.swaps[k] = self.wire.push(self.mine.at[:, at, :], self.other.at[:, at, :], to)

    def totals(self, k):
        self.swaps[k].wait_recv()
        at = self.rows(k)
        return [
            (
                pl.ds(second * self.half + k * self.size, self.size),
                self.mine[second, at, :].astype(f32) + self.other[second, at, :].astype(f32),
            )
            for second in range(2)
        ]


class ShardSum:
    def __init__(self, wire, both, came, from_down, from_up, pair, last, ranges):
        self.wire, self.both, self.came = wire, both, came
        self.from_down, self.from_up = from_down, from_up
        self.pair, self.last, self.ranges = pair, last, ranges
        self.shard = both.shape[2]
        self.half = self.shard // 2
        self.f, self.core, self.far, self.up, self.down = along_fsdp()
        self.side = lax.rem(lax.div(self.f, 2), 2)
        self.mine = lax.rem(self.f, 2)
        self.z = lax.div(self.f, 4)
        self.cores, self.plain, self.relay, self.more, self.cross = {}, {}, {}, {}, {}

    def cols(self, k):
        return pl.ds(*self.ranges[k])

    def block_cols(self, rel):
        size = 4 * self.shard
        return pl.ds(pl.multiple_of(lax.rem(self.z + rel, 4) * size, 128), size)

    def multiply(self, k, rel, left, right):
        tile = lax.dot_general(
            left, right, (((0,), (0,)), ((), ())), preferred_element_type=f32
        ).astype(bf16)
        cols = self.cols(k)
        for side in range(2):
            for core in range(2):
                lo = (2 * side + core) * self.shard
                place = lax.rem(core + self.mine, 2)
                self.both[place, 2 * rel + side, :, cols] = tile[lo : lo + self.shard]
        self.cores[k, rel] = self.wire.push(
            self.both.at[1, pl.ds(2 * rel, 2), :, cols],
            self.came.at[pl.ds(2 * rel, 2), :, cols],
            {"fsdp": self.core},
        )

    def block(self, rel, second, k):
        return pl.ds(2 * rel, 2), pl.ds(second * self.half, self.half), self.cols(k)

    def add_core(self, k, rel):
        self.cores[k, rel].wait_recv()
        at = pl.ds(2 * rel, 2), slice(None), self.cols(k)
        mine = (0,) + at
        self.both[mine] = (self.both[mine].astype(f32) + self.came[at].astype(f32)).astype(bf16)

    def start(self, k):
        got, cols, push = self.both.at[0], self.cols(k), self.wire.push
        up, down = {"fsdp": self.up}, {"fsdp": self.down}
        self.add_core(k, 2)
        self.relay[k] = (
            push(got.at[self.block(2, 0, k)], self.from_down.at[0, :, :, cols], up),
            push(got.at[self.block(2, 1, k)], self.from_up.at[0, :, :, cols], down),
        )
        self.add_core(k, 1)
        self.add_core(k, 3)
        self.add_core(k, 0)

    def relays(self, k):
        got, cols, push = self.both.at[0], self.cols(k), self.wire.push
        self.relay[k][0].wait_recv()
        at = (0, slice(None), slice(None), cols)
        self.from_down[at] = (
            self.from_down[at].astype(f32) + got[self.block(1, 0, k)].astype(f32)
        ).astype(bf16)
        one = push(self.from_down.at[at], self.from_down.at[2, :, :, cols], {"fsdp": self.up})
        self.relay[k][1].wait_recv()
        self.from_up[at] = (
            self.from_up[at].astype(f32) + got[self.block(3, 1, k)].astype(f32)
        ).astype(bf16)
        two = push(self.from_up.at[at], self.from_up.at[2, :, :, cols], {"fsdp": self.down})
        self.more[k] = (one, two)
        self.plain[k] = (
            push(got.at[self.block(1, 1, k)], self.from_down.at[1, :, :, cols], {"fsdp": self.up}),
            push(got.at[self.block(3, 0, k)], self.from_up.at[1, :, :, cols], {"fsdp": self.down}),
        )

    def across(self, k):
        got, cols, half = self.both.at[0], self.cols(k), self.half
        self.more[k][0].wait_recv()
        self.plain[k][1].wait_recv()
        self.pair[:, pl.ds(0, half), cols] = (
            got[self.block(0, 0, k)].astype(f32)
            + self.from_down[2, :, :, cols].astype(f32)
            + self.from_up[1, :, :, cols].astype(f32)
        ).astype(bf16)
        self.more[k][1].wait_recv()
        self.plain[k][0].wait_recv()
        self.pair[:, pl.ds(half, half), cols] = (
            got[self.block(0, 1, k)].astype(f32)
            + self.from_down[1, :, :, cols].astype(f32)
            + self.from_up[2, :, :, cols].astype(f32)
        ).astype(bf16)
        self.cross[k] = self.wire.push(
            self.pair.at[1 - self.side, :, cols], self.last.at[:, cols], {"fsdp": self.far}
        )

    def total(self, k):
        cols = self.cols(k)
        self.cross[k].wait_recv()
        return self.pair[self.side, :, cols].astype(f32) + self.last[:, cols].astype(f32)


def row_scratch(rows, width):
    return [pltpu.VMEM((2, rows // 2, width), bf16)] * 6


def everyone_near():
    _, core, far, up, down = along_fsdp()
    _, nxt, prv, _ = along_context()
    return [{"fsdp": i} for i in (core, far, up, down)] + [
        {"context": nxt}, {"context": prv}, {"tensor": 1 - lax.axis_index("tensor")}
    ]


def half_turn(x):
    return pltpu.roll(x, HD // 2, 1)


def signal(sem, to):
    pl.semaphore_signal(sem, inc=1, device_id=to, device_id_type=MESH)


ORDER = (2, 1, 3, 0)
SMALL = (8, 512)


def layer_back_kernel(
    normed_hbm, dy_hbm, both_hbm, hidden_hbm, first_hbm, second_hbm,
    out_hbm, lin_hbm, probs_hbm,
    middle_ref, dy_ref, gain_ref, mixed_ref, query_ref, kv_ref,
    normed_one_ref, tokens_ref, cos_ref, sin_ref,
    result_ref, gt_ref, small_ref, attn_ref, mlp_hbm,
    part, early_one, early_two, from_prv, from_nxt, mine, other,
    left, right, both, came, from_down, from_up, pair, last, shard_out,
    probs, d_probs, d_low, low, d_branch, d_mixed, acc_k, acc_v, kv_send, kv_came,
    d_lin, swap_mine, swap_other, attn_own, attn_came, small_own, small_came,
    send, recv, local, free,
):
    wire, loads = Wire(send, recv), Loads(local)
    rows, width = middle_ref.shape
    q_cols, kv_cols = mixed_ref.shape[1], kv_ref.shape[2]
    heads = q_cols // HD
    span = hidden_hbm.shape[1]
    scale = HD ** (-0.5)
    c, nxt, prv, cf = along_context()
    f, core, far, up, down = along_fsdp()
    opposite = lax.rem(f + 8, lax.axis_size("fsdp"))
    C = lambda i: {"context": i}
    F = lambda i: {"fsdp": i}
    T = {"tensor": 1 - lax.axis_index("tensor")}

    def keep_small(at, values):
        for k in range(values.shape[1] // SMALL[1]):
            small_own[pl.ds(at + k, 1), :] = values[:, k * SMALL[1] : (k + 1) * SMALL[1]]

    load_part = loads.start(first_hbm, part)
    load_left = loads.start(normed_hbm, left)
    load_r0 = loads.start(both_hbm.at[:, pl.ds(0, span)], right.at[0])
    load_r1 = loads.start(both_hbm.at[:, pl.ds(span, span)], right.at[1])
    meet(everyone_near() + [C(cf), F(opposite)])

    one, two = (
        RowSum(wire, part, source, (early.at[0], early.at[1]), from_prv, from_nxt, mine, other, 4)
        for source, early in ((first_hbm, early_one), (second_hbm, early_two))
    )
    mlp = ShardSum(wire, both, came, from_down, from_up, pair, last, [(k * span, span) for k in range(3)])
    attn = ShardSum(
        wire, both, came, from_down, from_up, pair, last,
        [(0, q_cols), (q_cols, q_cols), (2 * q_cols, 2 * kv_cols)],
    )
    one.start()

    def weights(k, rel, slot):
        mlp.multiply(k, rel, left[:, mlp.block_cols(rel)], right[slot])

    load_left.wait()
    load_r0.wait()
    for rel in ORDER:
        weights(0, rel, 0)
    load_r0 = loads.start(hidden_hbm, right.at[0])
    mlp.start(0)
    load_part.wait()
    one.relay(0)
    load_r1.wait()
    weights(1, 2, 1)
    one.relay(1)
    weights(1, 1, 1)
    one.relay(2)
    weights(1, 3, 1)
    one.relay(3)
    two.start()
    weights(1, 0, 1)
    load_left = loads.start(dy_hbm, left)
    mlp.start(1)
    mlp.relays(0)
    load_r0.wait()
    load_left.wait()
    weights(2, 2, 0)
    one.exchange(0)
    weights(2, 1, 0)
    weights(2, 3, 0)
    weights(2, 0, 0)
    one.exchange(1)
    mlp.start(2)
    signal(free.at[0], F(core))
    deep = left.shape[0]
    rest = width - deep
    load_out = (
        loads.start(out_hbm.at[pl.ds(0, deep)], left.at[:, pl.ds(0, q_cols)]),
        loads.start(out_hbm.at[pl.ds(deep, rest)], left.at[pl.ds(0, rest), pl.ds(q_cols, q_cols)]),
    )
    lin_cols = lin_hbm.shape[1]
    load_lin = (
        loads.start(lin_hbm.at[pl.ds(0, deep)], right.at[0, :, pl.ds(0, lin_cols)]),
        loads.start(lin_hbm.at[pl.ds(deep, rest)], right.at[1, pl.ds(0, rest), pl.ds(0, lin_cols)]),
    )
    load_probs = {h: loads.start(probs_hbm.at[h], probs.at[h % 2]) for h in range(2)}
    mlp.relays(1)
    one.exchange(2)

    gain_two = gain_ref[pl.ds(1, 1), :]
    gain_grad = jnp.zeros((1, width), f32)
    for k in range(4):
        if k == 1:
            one.exchange(3)
            mlp.relays(2)
            for j in range(4):
                wire.sent(*one.relays[j], *one.plains[j], *one.mores[j])
            signal(free.at[1], C(nxt))
            signal(free.at[2], C(prv))
            load_part = loads.start(second_hbm, part)
        if k == 3:
            load_part.wait()
            pl.semaphore_wait(free.at[1], 1)
            pl.semaphore_wait(free.at[2], 1)
            mlp.across(0)
        for at, grad in one.totals(k):
            mid = middle_ref[at, :]
            r = lax.rsqrt(jnp.mean(mid * mid, axis=-1, keepdims=True) + EPSILON)
            gain_grad += jnp.sum(grad * mid * r, axis=0, keepdims=True)
            scaled = grad * gain_two
            back = jnp.mean(scaled * mid, axis=-1, keepdims=True)
            value = dy_ref[at, :].astype(f32) + r * scaled - mid * (r * r * r * back)
            gt_ref[at, :] = value
            d_branch[at, :] = value.astype(bf16)
    wire.sent(*one.swaps.values())
    signal(free.at[3], T)
    keep_small(3, gain_grad)

    for copy in load_out:
        copy.wait()
    d_mixed[...] = (
        jnp.dot(d_branch[:, pl.ds(0, deep)], left[:, pl.ds(0, q_cols)], preferred_element_type=f32)
        + jnp.dot(
            d_branch[:, pl.ds(deep, rest)], left[pl.ds(0, rest), pl.ds(q_cols, q_cols)],
            preferred_element_type=f32,
        )
    ).astype(bf16)
    lane = lax.broadcasted_iota(jnp.int32, (1, HD), 1)
    sign = jnp.where(lane < HD // 2, 1.0, -1.0).astype(f32)

    def turn_back(w):
        return w * cos_ref[...] + half_turn(w * sin_ref[...]) * sign

    nt = (((1,), (1,)), ((), ()))
    tn = (((0,), (0,)), ((), ()))

    def head(h):
        cols = pl.ds(h * HD, HD)
        load_probs[h].wait()
        dm = d_mixed[:, cols]
        d_probs[...] = lax.dot_general(dm, kv_ref[1], nt, preferred_element_type=f32)
        for at in range(0, rows, 32):
            at = pl.ds(at, 32)
            p, dp = probs[h % 2, at, :], d_probs[at, :]
            inner = jnp.sum(p * dp, axis=-1, keepdims=True)
            d_low[at, :] = (p * (dp - inner)).astype(bf16)
            low[at, :] = p.astype(bf16)
        ds = d_low[...]
        dq = jnp.dot(ds, kv_ref[0], preferred_element_type=f32) * scale
        d_lin[:, cols] = turn_back(dq).astype(bf16)
        dk = lax.dot_general(ds, query_ref[:, cols], tn, preferred_element_type=f32)
        dv = lax.dot_general(low[...], dm, tn, preferred_element_type=f32)
        if h == 0:
            acc_k[...] = dk
            acc_v[...] = dv
        else:
            acc_k[...] += dk
            acc_v[...] += dv
        if h + 2 < heads:
            load_probs[h + 2] = loads.start(probs_hbm.at[h + 2], probs.at[h % 2])

    def leave(k):
        wire.sent(*[mlp.cores[k, rel] for rel in ORDER], *mlp.relay[k], *mlp.plain[k], *mlp.more[k])

    head(0)
    two.relay(0)
    leave(0)
    signal(free.at[4], F(up))
    signal(free.at[5], F(down))
    head(1)
    two.relay(1)
    two.relay(2)
    mlp.across(1)
    leave(1)
    signal(free.at[7], F(up))
    signal(free.at[8], F(down))
    pl.semaphore_wait(free.at[0], 1)
    for rel in ORDER:
        attn.multiply(0, rel, d_branch[:, attn.block_cols(rel)], mixed_ref[...])
    head(2)
    pl.semaphore_wait(free.at[4], 1)
    pl.semaphore_wait(free.at[5], 1)
    attn.start(0)
    head(3)
    pl.semaphore_wait(free.at[3], 1)
    two.exchange(0)
    mlp.across(2)
    leave(2)
    head(4)
    two.exchange(1)
    head(5)

    for k in range(4):
        kv_send[k, 0] = acc_k[pl.ds(k * rows, rows), :].astype(bf16)
        kv_send[k, 1] = acc_v[pl.ds(k * rows, rows), :].astype(bf16)
    kv = [
        wire.push(kv_send.at[nxt], kv_came.at[0], C(nxt)),
        wire.push(kv_send.at[prv], kv_came.at[1], C(prv)),
        wire.push(kv_send.at[cf], kv_came.at[2], C(cf)),
    ]
    two.relay(3)
    for rel in ORDER:
        attn.multiply(1, rel, normed_one_ref[:, attn.block_cols(rel)], d_lin[:, pl.ds(0, q_cols)])
    attn.relays(0)
    for k in range(3):
        shard_out[:, mlp.cols(k)] = mlp.total(k).astype(bf16)
    signal(free.at[6], F(far))
    for k in range(3):
        wire.sent(mlp.cross[k])
    pl.semaphore_wait(free.at[7], 1)
    pl.semaphore_wait(free.at[8], 1)
    attn.start(1)
    for copy in kv:
        copy.wait_recv()
    d_key = acc_k[pl.ds(pl.multiple_of(c * rows, 8), rows), :]
    d_value = acc_v[pl.ds(pl.multiple_of(c * rows, 8), rows), :]
    for k in range(3):
        d_key += kv_came[k, 0].astype(f32)
        d_value += kv_came[k, 1].astype(f32)
    d_lin[:, pl.ds(q_cols, kv_cols)] = turn_back(d_key * scale).astype(bf16)
    d_lin[:, pl.ds(q_cols + kv_cols, kv_cols)] = d_value.astype(bf16)
    for copy in load_lin:
        copy.wait()
    swap_mine[:, pl.ds(0, deep)] = lax.dot_general(
        d_lin[...], right[0, :, pl.ds(0, lin_cols)], nt, preferred_element_type=f32
    ).astype(bf16)
    swap_mine[:, pl.ds(deep, rest)] = lax.dot_general(
        d_lin[...], right[1, pl.ds(0, rest), pl.ds(0, lin_cols)], nt, preferred_element_type=f32
    ).astype(bf16)
    spread = [
        wire.push(shard_out, mlp_hbm.at[c], C(nxt)),
        wire.push(shard_out, mlp_hbm.at[c], C(prv)),
    ]
    keep = loads.start(shard_out, mlp_hbm.at[c])
    sizes = 64
    gain_grad = jnp.zeros((1, width), f32)
    for k in range(rows // sizes):
        at = pl.ds(k * sizes, sizes)
        mid = tokens_ref[at, :].astype(f32)
        r = lax.rsqrt(jnp.mean(mid * mid, axis=-1, keepdims=True) + EPSILON)
        gain_grad += jnp.sum(swap_mine[at, :].astype(f32) * mid * r, axis=0, keepdims=True)
    keep_small(0, gain_grad)
    keep_small(6, jnp.sum(d_lin[...].astype(f32), axis=0, keepdims=True))
    small_step = wire.push(small_own, small_came.at[0], T)
    swaps = []

    def swap(k):
        at = pl.ds(k * sizes, sizes)
        swaps.append(wire.push(swap_mine.at[at, :], swap_other.at[at, :], T))

    for k in range(3):
        swap(k)
    for rel in ORDER:
        attn.multiply(
            2, rel, normed_one_ref[:, attn.block_cols(rel)], d_lin[:, pl.ds(q_cols, 2 * kv_cols)]
        )
    small_step.wait_recv()
    gain_rows = lax.broadcasted_iota(jnp.int32, SMALL, 0) < 3
    small_came[1] = small_own[...] + jnp.where(gain_rows, small_came[0], 0.0)
    small_step = wire.push(small_came.at[1], small_came.at[2], F(core))
    attn.start(2)
    pl.semaphore_wait(free.at[6], 1)
    attn.across(0)
    swap(3)
    small_step.wait_recv()
    small_came[3] = small_came[1] + small_came[2]
    small_steps = [
        wire.push(small_came.at[3], small_came.at[4 + k], F(to)) for k, to in enumerate((up, down, opposite))
    ]
    attn.relays(1)
    attn.relays(2)
    for step in small_steps:
        step.wait_recv()
    small_came[7] = (small_came[3] + small_came[6]) + (small_came[4] + small_came[5])
    small_step = wire.push(small_came.at[7], small_came.at[8], F(far))

    half = shard_out.shape[0] // 2
    near, rest_of = {}, {}

    def to_ranks(k):
        cols = attn.cols(k)
        attn_own[:, cols] = attn.total(k).astype(bf16)
        w = attn_own.at[:, cols]
        near[k] = (
            wire.push(w, attn_came.at[0, :, cols], C(nxt)),
            wire.push(w, attn_came.at[1, :, cols], C(prv)),
        )

    def onward(k):
        cols, first, second = attn.cols(k), pl.ds(0, half), pl.ds(half, half)
        near[k][0].wait_recv()
        near[k][1].wait_recv()
        rest_of[k] = (
            wire.push(attn_came.at[0, first, cols], attn_came.at[2, first, cols], C(nxt)),
            wire.push(attn_came.at[1, second, cols], attn_came.at[2, second, cols], C(prv)),
        )

    attn.across(1)
    attn.across(2)
    two.exchange(2)
    two.exchange(3)

    gain_one = gain_ref[pl.ds(0, 1), :]
    for k in range(rows // sizes):
        swaps[k].wait_recv()
        at = pl.ds(k * sizes, sizes)
        grad = swap_mine[at, :].astype(f32) + swap_other[at, :].astype(f32)
        mid = tokens_ref[at, :].astype(f32)
        r = lax.rsqrt(jnp.mean(mid * mid, axis=-1, keepdims=True) + EPSILON)
        scaled = grad * gain_one
        back = jnp.mean(scaled * mid, axis=-1, keepdims=True)
        gt_ref[at, :] = gt_ref[at, :] + r * scaled - mid * (r * r * r * back)
    to_ranks(0)
    small_step.wait_recv()
    small_came[9] = small_came[7] + small_came[8]
    spread[0].wait_recv()
    w = mlp_hbm.at[prv, pl.ds(0, half)]
    spread.append(wire.push(w, w, C(nxt)))
    spread[1].wait_recv()
    w = mlp_hbm.at[nxt, pl.ds(half, half)]
    spread.append(wire.push(w, w, C(prv)))
    to_ranks(1)
    to_ranks(2)
    small_steps = [
        wire.push(small_came.at[9], small_came.at[10 + k], C(to)) for k, to in enumerate((nxt, prv, cf))
    ]
    onward(0)
    for k in range(4):
        for at, total in two.totals(k):
            result_ref[at, :] = (middle_ref[at, :] + total).astype(bf16)
    onward(1)
    onward(2)
    for k in range(3):
        cols = attn.cols(k)
        rest_of[k][0].wait_recv()
        rest_of[k][1].wait_recv()
        attn_ref[:, cols] = (attn_own[:, cols].astype(f32) + attn_came[2, :, cols].astype(f32)) + (
            attn_came[0, :, cols].astype(f32) + attn_came[1, :, cols].astype(f32)
        )
    for step in small_steps:
        step.wait_recv()
    small_ref[...] = (small_came[9] + small_came[12]) + (small_came[10] + small_came[11])
    spread[2].wait_recv()
    spread[3].wait_recv()
    keep.wait()
    wire.drain()


def layer_back(hbm, near, cid=4):
    normed, dy, both, hidden, first, second, out, lin, probs = hbm
    group, width = normed.shape
    rows = group // 4
    shard, span = width // 16, hidden.shape[1]
    lin_cols = lin.shape[1]
    q_cols = out.shape[1]
    sems = 2 * 28 + 2 * (12 + 3 * 7) + 3 + 4 + 4 + 12 + 9
    return pl.pallas_call(
        layer_back_kernel,
        out_shape=(
            jax.ShapeDtypeStruct((rows, width), bf16),
            jax.ShapeDtypeStruct((rows, width), f32),
            jax.ShapeDtypeStruct(SMALL, f32),
            jax.ShapeDtypeStruct((shard, lin_cols + q_cols), f32),
            jax.ShapeDtypeStruct((4, shard, 3 * span), bf16),
        ),
        in_specs=[ANY] * len(hbm) + [VM] * len(near),
        out_specs=(VM, VM, VM, VM, ANY),
        scratch_shapes=[pltpu.VMEM((group, width), bf16)]
        + row_scratch(rows, width)
        + [
            pltpu.VMEM((group, width), bf16),
            pltpu.VMEM((2, group, span), bf16),
            pltpu.VMEM((2, 8, shard, 3 * span), bf16),
            pltpu.VMEM((8, shard, 3 * span), bf16),
            pltpu.VMEM((3, 2, shard // 2, 3 * span), bf16),
            pltpu.VMEM((3, 2, shard // 2, 3 * span), bf16),
            pltpu.VMEM((2, shard, 3 * span), bf16),
            pltpu.VMEM((shard, 3 * span), bf16),
            pltpu.VMEM((shard, 3 * span), bf16),
            pltpu.VMEM((2, rows, group), f32),
            pltpu.VMEM((rows, group), f32),
            pltpu.VMEM((rows, group), bf16),
            pltpu.VMEM((rows, group), bf16),
            pltpu.VMEM((rows, width), bf16),
            pltpu.VMEM((rows, q_cols), bf16),
            pltpu.VMEM((group, HD), f32),
            pltpu.VMEM((group, HD), f32),
            pltpu.VMEM((4, 2, rows, HD), bf16),
            pltpu.VMEM((3, 2, rows, HD), bf16),
            pltpu.VMEM((rows, lin_cols), bf16),
            pltpu.VMEM((rows, width), bf16),
            pltpu.VMEM((rows, width), bf16),
            pltpu.VMEM((shard, lin_cols + q_cols), bf16),
            pltpu.VMEM((3, shard, lin_cols + q_cols), bf16),
            pltpu.VMEM(SMALL, f32),
            pltpu.VMEM((13,) + SMALL, f32),
            pltpu.SemaphoreType.DMA((sems,)),
            pltpu.SemaphoreType.DMA((sems,)),
            pltpu.SemaphoreType.DMA((18,)),
            pltpu.SemaphoreType.REGULAR((9,)),
        ],
        compiler_params=pltpu.CompilerParams(
            collective_id=cid, has_side_effects=True, vmem_limit_bytes=63 << 20
        ),
        name="layer_back",
    )(*hbm, *near)


class Blocks:
    def __init__(self, wire, ref, shard, cols=None):
        self.wire, self.ref, self.shard, self.half = wire, ref, shard, shard // 2
        self.cols = slice(None) if cols is None else cols
        self.f, self.core, self.far, self.up, self.down = along_fsdp()
        n = lax.axis_size("fsdp")
        self.opposite = lax.rem(self.f + 8, n)
        self.sibling = []

    def pair(self, i):
        return i + 2 - 4 * lax.rem(lax.div(i, 2), 2)

    def win(self, owner, lo=0, size=None):
        at = pl.multiple_of(owner * self.shard + lo, 16)
        return self.ref.at[pl.ds(at, size or self.shard), self.cols]

    def push(self, w, to):
        return self.wire.push(w, w, {"fsdp": to})

    def to_core(self, w):
        self.sibling.append(self.push(w, self.core))

    def ex(self):
        w = self.win(self.f)
        self.from_far = self.push(w, self.far)
        self.to_core(w)

    def ez(self):
        w = self.win(self.f)
        self.from_down = self.push(w, self.up)
        self.from_up = self.push(w, self.down)

    def e0(self):
        self.ex()
        self.ez()

    def e1(self):
        self.from_far.wait_recv()
        w = self.win(self.far)
        self.far_down = self.push(w, self.up)
        self.far_up = self.push(w, self.down)
        self.to_core(w)

    def relay(self, below, above, one, two):
        one.wait_recv()
        first = self.push(self.win(below, 0, self.half), self.up)
        self.to_core(self.win(below))
        two.wait_recv()
        second = self.push(self.win(above, self.half, self.half), self.down)
        self.to_core(self.win(above))
        return first, second

    def e2(self):
        self.last = self.relay(self.down, self.up, self.from_down, self.from_up)

    def e3(self):
        self.last += self.relay(self.pair(self.down), self.pair(self.up), self.far_down, self.far_up)

    def e4(self):
        for k, copy in enumerate(self.last):
            copy.wait_recv()
            owner = self.opposite if k < 2 else self.pair(self.opposite)
            self.to_core(self.win(owner, self.half * (k % 2), self.half))

    def end(self):
        for copy in self.sibling:
            copy.wait_recv()


def rotary(angle):
    turns = jnp.floor(angle * (0.5 / math.pi) + 0.5)
    x = (angle - turns * 6.28125) - turns * (2.0 * math.pi - 6.28125)
    square = x * x
    cosine, sine = jnp.zeros_like(x), jnp.zeros_like(x)
    for k in range(9, -1, -1):
        cosine = cosine * square + (-1.0) ** k / math.factorial(2 * k)
        sine = sine * square + (-1.0) ** k / math.factorial(2 * k + 1)
    return cosine, sine * x


def layer_front_kernel(
    query_hbm, key_hbm, value_hbm, out_hbm, gate_hbm, lift_hbm, down_hbm, dy_hbm,
    query_bias, key_bias, value_bias, first_gain, second_gain,
    tokens_ref, inverse_ref, lengths_ref,
    middle_ref, normed_one_ref, mixed_ref, q_ref, kv_ref, gain_ref, cos_ref, sin_ref,
    normed_hbm, dyg_hbm, lin_hbm, outf_hbm, probs_hbm,
    both_hbm, hidden_hbm, first_hbm, second_hbm,
    gains, wl, wo, wm, dyg, normed, mask, probs, part, other, d_hidden,
    low, pair, d_both, hidden, first, second,
    send, recv, local,
):
    wire, loads = Wire(send, recv), Loads(local)
    rows, width = tokens_ref.shape
    group = dyg.shape[0]
    shard, q_cols = query_hbm.shape
    kv_cols = key_hbm.shape[1]
    heads = q_cols // HD
    hidden_cols = gate_hbm.shape[1]
    span = hidden.shape[1]
    overlap = 4 * span - hidden_cols
    scale = HD ** (-0.5)
    c, nxt, prv, cf = along_context()
    f, core, far, up, down = along_fsdp()
    C = lambda i: {"context": i}
    T = {"tensor": 1 - lax.axis_index("tensor")}
    mine = pl.ds(pl.multiple_of(f * shard, 16), shard)
    group_rows = lambda owner, lo=0, size=rows: pl.ds(pl.multiple_of(owner * rows + lo, 16), size)
    start = pl.multiple_of(c * span - lax.div(c, 3) * overlap, 128)

    own = [
        loads.start(query_hbm, wl.at[mine, pl.ds(0, q_cols)]),
        loads.start(key_hbm, wl.at[mine, pl.ds(q_cols, kv_cols)]),
        loads.start(value_hbm, wl.at[mine, pl.ds(q_cols + kv_cols, kv_cols)]),
        loads.start(out_hbm, wo.at[mine, :]),
        loads.start(dy_hbm, dyg.at[group_rows(c), :]),
    ]
    sizes_of = (512, 384, span - 896)
    offsets = (0, 512, 896)
    big = [
        [
            loads.start(
                w.at[:, pl.ds(start + off, n)], wm.at[mine, pl.ds(3 * off + k * n, n)]
            )
            for k, w in enumerate((down_hbm, gate_hbm, lift_hbm))
        ]
        for off, n in zip(offsets, sizes_of)
    ]
    tile = gains.shape[0] * shard // width
    gains[pl.ds(pl.multiple_of(f * tile, 16), tile), :] = jnp.zeros((tile, HD), f32)
    gains[pl.ds(pl.multiple_of(f * tile, 16), 1), pl.ds(0, shard)] = first_gain[...].astype(f32)
    gains[pl.ds(pl.multiple_of(f * tile, 16) + 1, 1), pl.ds(0, shard)] = second_gain[...].astype(f32)
    meet(everyone_near() + [C(cf)])
    G = Blocks(wire, gains, tile)
    Q = Blocks(wire, wl, shard)
    O = Blocks(wire, wo, shard)
    A, B, D = (Blocks(wire, wm, shard, pl.ds(3 * off, 3 * n)) for off, n in zip(offsets, sizes_of))

    G.e0()
    for copy in own:
        copy.wait()
    Q.e0()
    w = dyg.at[group_rows(c), :]
    dy_copies = [wire.push(w, w, C(nxt)), wire.push(w, w, C(prv))]
    G.e1()
    O.e0()
    for copy in big[0]:
        copy.wait()
    A.ex()
    here = c * rows + lax.broadcasted_iota(jnp.int32, (rows, 1), 0)
    there = lax.broadcasted_iota(jnp.int32, (1, group), 1)
    end, position = jnp.zeros((1, 1), jnp.int32), here
    mine_of, its = jnp.zeros((rows, 1), jnp.int32), jnp.zeros((1, group), jnp.int32)
    for k in range(lengths_ref.shape[1]):
        end = end + lengths_ref[:, pl.ds(k, 1)]
        mine_of = mine_of + jnp.where(here >= end, 1, 0)
        position = jnp.where(here >= end, here - end, position)
        its = its + jnp.where(there >= end, 1, 0)
    cos_ref[...], sin_ref[...] = rotary(position.astype(f32) * inverse_ref[...])
    allowed = (mine_of == its) & (there <= here)
    mask[...] = jnp.where(allowed, 0.0, -1e30).astype(f32)
    G.e2()
    G.e3()
    Q.e1()
    G.e4()
    G.end()
    for k in range(2):
        gain_ref[pl.ds(k, 1), :] = jnp.concatenate(
            [gains[pl.ds(i * tile + k, 1), :][:, :shard] for i in range(width // shard)], axis=1
        )
    sizes = 64
    for at in range(0, rows, sizes):
        at = pl.ds(at, sizes)
        x = tokens_ref[at, :].astype(f32)
        r = lax.rsqrt(jnp.mean(x * x, axis=-1, keepdims=True) + EPSILON)
        normed_one_ref[at, :] = (x * r * gain_ref[pl.ds(0, 1), :]).astype(bf16)
    Q.e2()
    Q.e3()
    O.e1()
    A.ez()
    Q.e4()
    for copy in big[1] + big[2]:
        copy.wait()
    B.ex()
    D.ex()
    Q.end()

    sign = jnp.where(lax.broadcasted_iota(jnp.int32, (1, HD), 1) < HD // 2, -1.0, 1.0).astype(f32)

    def turned(v):
        return v * cos_ref[...] + half_turn(v) * sign * sin_ref[...]

    def linear(head, biases):
        both = jnp.dot(normed_one_ref[...], wl[:, pl.ds(head * HD, 2 * HD)], preferred_element_type=f32)
        return [both[:, k * HD : (k + 1) * HD] + bias.astype(f32) for k, bias in enumerate(biases)]

    key, value = linear(heads, (key_bias[...], value_bias[...]))
    kv_ref[0, group_rows(c), :] = turned(key).astype(bf16)
    kv_ref[1, group_rows(c), :] = value.astype(bf16)
    kv = []
    for k in range(2):
        w = kv_ref.at[k, group_rows(c), :]
        kv.append([wire.push(w, w, C(i)) for i in (cf, nxt, prv)])
    for h in range(0, heads, 2):
        biases = [query_bias[:, pl.ds((h + k) * HD, HD)] for k in range(2)]
        for k, lin in enumerate(linear(h, biases)):
            q_ref[:, pl.ds((h + k) * HD, HD)] = turned(lin).astype(bf16)
    O.e2()
    O.e3()
    A.e1()
    keep = [loads.start(wl, lin_hbm)]
    half = rows // 2
    dy_copies[0].wait_recv()
    w = dyg.at[group_rows(prv, 0, half), :]
    dy_copies.append(wire.push(w, w, C(nxt)))
    dy_copies[1].wait_recv()
    w = dyg.at[group_rows(nxt, half, half), :]
    dy_copies.append(wire.push(w, w, C(prv)))
    O.e4()
    for copy in kv[0]:
        copy.wait_recv()

    nt = (((1,), (1,)), ((), ()))
    probs_out = {}

    def head(h):
        cols = pl.ds(h * HD, HD)
        if h >= 2:
            probs_out[h - 2].wait()
        probs[h % 2] = lax.dot_general(q_ref[:, cols], kv_ref[0], nt, preferred_element_type=f32)
        for at in range(0, rows, 32):
            at = pl.ds(at, 32)
            s = probs[h % 2, at, :] * scale + mask[at, :]
            e = jnp.exp(s - jnp.max(s, axis=-1, keepdims=True))
            p = e * (1.0 / jnp.sum(e, axis=-1, keepdims=True))
            probs[h % 2, at, :] = p
            low[at, :] = p.astype(bf16)
        probs_out[h] = loads.start(probs.at[h % 2], probs_hbm.at[h])
        if h == 0:
            for copy in kv[1]:
                copy.wait_recv()
        mixed_ref[:, cols] = jnp.dot(low[...], kv_ref[1], preferred_element_type=f32).astype(bf16)

    for h in range(heads):
        head(h)
        if h == 3:
            A.e2()
    probs_out[heads - 2].wait()
    probs_out[heads - 1].wait()
    O.end()
    sizes = 32
    chunks = rows // sizes
    swaps = []
    for k in range(chunks // 2):
        at = pl.ds(2 * k * sizes, 2 * sizes)
        part[at, :] = lax.dot_general(mixed_ref[at, :], wo[...], nt, preferred_element_type=f32).astype(bf16)
        for j in range(2):
            at = pl.ds((2 * k + j) * sizes, sizes)
            swaps.append(wire.push(part.at[at, :], other.at[at, :], T))
    keep.append(loads.start(wo, outf_hbm))
    B.ez()
    A.e3()
    for copy in dy_copies[2:]:
        copy.wait_recv()
    keep.append(loads.start(dyg, dyg_hbm))

    from_prv, from_nxt, last = {}, {}, []
    cut = sizes // 2

    def forward(k):
        from_prv[k].wait_recv()
        w = normed.at[group_rows(prv, k * sizes, cut), :]
        last.append(wire.push(w, w, C(nxt)))
        from_nxt[k].wait_recv()
        w = normed.at[group_rows(nxt, k * sizes + cut, cut), :]
        last.append(wire.push(w, w, C(prv)))

    for k in range(chunks):
        at = pl.ds(k * sizes, sizes)
        swaps[k].wait_recv()
        mid = tokens_ref[at, :].astype(f32) + (part[at, :].astype(f32) + other[at, :].astype(f32))
        middle_ref[at, :] = mid
        r = lax.rsqrt(jnp.mean(mid * mid, axis=-1, keepdims=True) + EPSILON)
        normed[group_rows(c, k * sizes, sizes), :] = (mid * r * gain_ref[pl.ds(1, 1), :]).astype(bf16)
        w = normed.at[group_rows(c, k * sizes, sizes), :]
        from_prv[k] = wire.push(w, w, C(nxt))
        from_nxt[k] = wire.push(w, w, C(prv))
        if k == 1:
            B.e1()
        if k == 2:
            A.e4()
        if k == 3:
            D.ez()
        if k == 5:
            B.e2()
    A.end()
    for k in range(3):
        forward(k)

    skip = lax.div(c, 3) * overlap

    def feed(owner, piece):
        at = group_rows(owner)
        off, n = offsets[piece], sizes_of[piece]
        down_at, wide = pl.ds(3 * off, n), pl.ds(3 * off + n, 2 * n)
        hidden_at, both_at = pl.ds(off, n), pl.ds(2 * off, 2 * n)
        pair[:, pl.ds(0, 2 * n)] = jnp.dot(normed[at, :], wm[:, wide], preferred_element_type=f32)
        d_hidden[:, pl.ds(0, n)] = jnp.dot(dyg[at, :], wm[:, down_at], preferred_element_type=f32)
        step = 32
        for k in range(0, rows, step):
            here, rows_here = pl.ds(k, step), group_rows(owner, k, step)
            gate, lift = pair[here, pl.ds(0, n)], pair[here, pl.ds(n, n)]
            dh = d_hidden[here, pl.ds(0, n)]
            sig = 0.5 * jnp.tanh(0.5 * gate) + 0.5
            swish = gate * sig
            up_part = swish * lift
            if piece == 0:
                live = lax.broadcasted_iota(jnp.int32, (1, n), 1) >= skip
                dh = jnp.where(live, dh, 0.0)
                up_part = jnp.where(live, up_part, 0.0)
            hidden[rows_here, hidden_at] = up_part.astype(bf16)
            d_both[rows_here, pl.ds(2 * off, n)] = (
                dh * lift * (sig + swish * (1.0 - sig))
            ).astype(bf16)
            d_both[rows_here, pl.ds(2 * off + n, n)] = (dh * swish).astype(bf16)
        one = lax.dot_general(d_both[at, both_at], wm[:, wide], nt, preferred_element_type=f32)
        two = lax.dot_general(hidden[at, hidden_at], wm[:, down_at], nt, preferred_element_type=f32)
        if piece:
            one += first[at, :].astype(f32)
            two += second[at, :].astype(f32)
        first[at, :] = one.astype(bf16)
        second[at, :] = two.astype(bf16)
        keep.append(loads.start(hidden.at[at, hidden_at], hidden_hbm.at[at, hidden_at]))
        for k in range(2):
            keep.append(
                loads.start(
                    d_both.at[at, pl.ds(2 * off + k * n, n)], both_hbm.at[at, pl.ds(k * span + off, n)]
                )
            )
        if piece == 2:
            for src, dst in ((first, first_hbm), (second, second_hbm)):
                keep.append(loads.start(src.at[at, :], dst.at[at, :]))

    feed(c, 0)
    for k in range(3, 6):
        forward(k)
    B.e3()
    D.e1()
    for k in range(6, chunks):
        forward(k)
    feed(prv, 0)
    D.e2()
    B.e4()
    feed(nxt, 0)
    B.end()
    feed(c, 1)
    D.e3()
    feed(prv, 1)
    feed(nxt, 1)
    for copy in last:
        copy.wait_recv()
    keep.append(loads.start(normed, normed_hbm))
    feed(cf, 0)
    D.e4()
    feed(cf, 1)
    D.end()
    for owner in (c, prv, nxt, cf):
        feed(owner, 2)
    for copy in keep:
        copy.wait()
    wire.drain()


def layer_front(hbm, near, span, cid=1):
    query, key, value, out, gate, lift, down, dy = hbm
    rows, width = dy.shape
    group = 4 * rows
    shard, q_cols = query.shape
    lin_cols = q_cols + 2 * key.shape[1]
    heads = q_cols // HD
    sems = 6 * 19 + 4 + 6 + 8 + 32
    S = jax.ShapeDtypeStruct
    return pl.pallas_call(
        layer_front_kernel,
        out_shape=(
            S((rows, width), f32),
            S((rows, width), bf16),
            S((rows, q_cols), bf16),
            S((rows, q_cols), bf16),
            S((2, group, HD), bf16),
            S((2, width), f32),
            S((rows, HD), f32),
            S((rows, HD), f32),
            S((group, width), bf16),
            S((group, width), bf16),
            S((width, lin_cols), bf16),
            S((width, q_cols), bf16),
            S((heads, rows, group), f32),
        )
        + (S((group, 2 * span), bf16), S((group, span), bf16))
        + (S((group, width), bf16),) * 2,
        in_specs=[ANY] * len(hbm) + [VM] * len(near),
        out_specs=(VM,) * 8 + (ANY,) * 9,
        scratch_shapes=[
            pltpu.VMEM((width // shard * 32, HD), f32),
            pltpu.VMEM((width, lin_cols), bf16),
            pltpu.VMEM((width, q_cols), bf16),
            pltpu.VMEM((width, 3 * span), bf16),
            pltpu.VMEM((group, width), bf16),
            pltpu.VMEM((group, width), bf16),
            pltpu.VMEM((rows, group), f32),
            pltpu.VMEM((2, rows, group), f32),
            pltpu.VMEM((rows, width), bf16),
            pltpu.VMEM((rows, width), bf16),
            pltpu.VMEM((rows, 512), f32),
            pltpu.VMEM((rows, group), bf16),
            pltpu.VMEM((rows, 1024), f32),
            pltpu.VMEM((group, 2 * span), bf16),
            pltpu.VMEM((group, span), bf16),
            pltpu.VMEM((group, width), bf16),
            pltpu.VMEM((group, width), bf16),
            pltpu.SemaphoreType.DMA((sems,)),
            pltpu.SemaphoreType.DMA((sems,)),
            pltpu.SemaphoreType.DMA((14 + heads + 4 + 44,)),
        ],
        compiler_params=pltpu.CompilerParams(
            collective_id=cid, has_side_effects=True, vmem_limit_bytes=63 << 20
        ),
        name="layer_front",
    )(*hbm, *near)


def on_device(
    tokens,
    cotangent,
    lengths,
    gain_attn,
    w_query,
    b_query,
    w_key,
    b_key,
    w_value,
    b_value,
    w_out,
    gain_mlp,
    w_gate,
    w_up,
    w_down,
):
    row_count, width = tokens.shape
    context_size = lax.axis_size("context")
    context_rank = lax.axis_index("context")
    fsdp_rank = lax.axis_index("fsdp")
    shard = w_query.shape[0]
    query_cols, kv_cols, hidden_cols = w_query.shape[1], w_key.shape[1], w_gate.shape[1]
    span = -(-(hidden_cols // 128) // context_size) * 128
    overlap = context_size * span - hidden_cols
    (
        middle, normed_one, mixed, query_heads, kv_group, gain_full, cosine, sine_table,
        normed_group, dy_group, lin_full, out_turned, probs,
        d_both, hidden, d_normed_part, mlp_part,
    ) = layer_front(
        (w_query, w_key, w_value, w_out.T, w_gate, w_up, w_down.T, cotangent),
        (
            b_query[None], b_key[None], b_value[None], gain_attn[None], gain_mlp[None],
            tokens, jnp.asarray(INVERSE), lengths,
        ),
        span,
    )
    result, grad_tokens, small, attn_shard, mlp_all = layer_back(
        (
            normed_group, dy_group, d_both, hidden, d_normed_part, mlp_part,
            out_turned, lin_full, probs,
        ),
        (
            middle, cotangent, gain_full, mixed, query_heads, kv_group, normed_one, tokens, cosine, sine_table,
        ),
    )

    def whole(k):
        parts = [mlp_all[i, :, k * span : (k + 1) * span] for i in range(context_size)]
        parts[-1] = parts[-1][:, overlap:]
        return jnp.concatenate(parts, axis=1).astype(f32)

    small = small.reshape(-1)
    own = lambda at: lax.dynamic_slice_in_dim(small, at + fsdp_rank * shard, shard)
    bias_total = small[2 * width :]
    at_query = query_cols
    at_key = at_query + query_cols
    at_value = at_key + kv_cols
    return (
        result,
        grad_tokens,
        own(0),
        attn_shard[:, at_query:at_key],
        bias_total[:query_cols],
        attn_shard[:, at_key:at_value],
        bias_total[query_cols : query_cols + kv_cols],
        attn_shard[:, at_value:],
        bias_total[query_cols + kv_cols :],
        attn_shard[:, :query_cols].T,
        own(width),
        whole(0),
        whole(1),
        whole(2).T,
    )


def solution(mesh):
    return jax.shard_map(
        on_device,
        mesh=mesh,
        in_specs=(
            P(("fsdp", "context"), None),
            P(("fsdp", "context"), None),
            P("fsdp", None),
            P("fsdp"),
            P("fsdp", "tensor"),
            P("tensor"),
            P("fsdp", "tensor"),
            P("tensor"),
            P("fsdp", "tensor"),
            P("tensor"),
            P("tensor", "fsdp"),
            P("fsdp"),
            P("fsdp", "tensor"),
            P("fsdp", "tensor"),
            P("tensor", "fsdp"),
        ),
        out_specs=(
            P(("fsdp", "context"), None),
            P(("fsdp", "context"), None),
            P("fsdp"),
            P("fsdp", "tensor"),
            P("tensor"),
            P("fsdp", "tensor"),
            P("tensor"),
            P("fsdp", "tensor"),
            P("tensor"),
            P("tensor", "fsdp"),
            P("fsdp"),
            P("fsdp", "tensor"),
            P("fsdp", "tensor"),
            P("tensor", "fsdp"),
        ),
        check_vma=False,
    )
```

```python
import math

import jax
import jax.numpy as jnp
import numpy as np
from jax import lax
from jax.experimental import pallas as pl
from jax.experimental.pallas import tpu as pltpu
from jax.sharding import PartitionSpec as P

HD = 128
MESH = pl.DeviceIdType.MESH
ANY = pl.BlockSpec(memory_space=pl.ANY)
VM = pl.BlockSpec(memory_space=pltpu.VMEM)
f32, bf16 = jnp.float32, jnp.bfloat16

ROPE_BASE = 1000000.0
EPSILON = 1e-06
INVERSE = np.tile(ROPE_BASE ** (-(np.arange(HD // 2) * 2.0 / HD)), 2).astype(np.float32)[None]

def meet(targets):
    barrier = pltpu.get_barrier_semaphore()
    for t in targets:
        pl.semaphore_signal(barrier, inc=1, device_id=t, device_id_type=MESH)
    pl.semaphore_wait(barrier, len(targets))


class Wire:
    def __init__(self, send, recv):
        self.send, self.recv, self.used, self.started = send, recv, 0, []

    def push(self, src, dst, to):
        k = self.used
        self.used += 1
        copy = pltpu.make_async_remote_copy(
            src, dst, self.send.at[k], self.recv.at[k], device_id=to, device_id_type=MESH
        )
        copy.start()
        self.started.append(copy)
        return copy

    def sent(self, *copies):
        for copy in copies:
            copy.wait_send()
            self.started = [other for other in self.started if other is not copy]

    def drain(self):
        self.sent(*list(self.started))


class Loads:
    def __init__(self, sems):
        self.sems, self.used = sems, 0

    def start(self, src, dst):
        copy = pltpu.make_async_copy(src, dst, self.sems.at[self.used])
        self.used += 1
        copy.start()
        return copy


def along_context():
    c, m = lax.axis_index("context"), lax.axis_size("context")
    return c, lax.rem(c + 1, m), lax.rem(c + m - 1, m), lax.rem(c + 2, m)


def along_fsdp():
    f, n = lax.axis_index("fsdp"), lax.axis_size("fsdp")
    core = f + 1 - 2 * lax.rem(f, 2)
    far = f + 2 - 4 * lax.rem(lax.div(f, 2), 2)
    return f, core, far, lax.rem(f + 4, n), lax.rem(f + n - 4, n)


class RowSum:
    def __init__(self, wire, part, source, early, from_prv, from_nxt, mine, other, chunks):
        self.wire, self.part, self.source, self.chunks = wire, part, source, chunks
        self.early_prv, self.early_nxt = early
        self.from_prv, self.from_nxt, self.mine, self.other = from_prv, from_nxt, mine, other
        self.half = mine.shape[1]
        self.size = self.half // chunks
        self.c, self.nxt, self.prv, self.cf = along_context()
        self.relays, self.plains, self.mores, self.swaps = {}, {}, {}, {}

    def rows(self, k):
        return pl.ds(k * self.size, self.size)

    def win(self, owner, second, k):
        at = pl.multiple_of((owner * 2 + second) * self.half + k * self.size, 16)
        return pl.ds(at, self.size), slice(None)

    def start(self):
        up, down = {"context": self.nxt}, {"context": self.prv}
        source, push = self.source, self.wire.push
        for k in range(self.chunks):
            at = self.rows(k)
            self.relays[k] = (
                push(source.at[self.win(self.cf, 0, k)], self.early_prv.at[at, :], up),
                push(source.at[self.win(self.cf, 1, k)], self.early_nxt.at[at, :], down),
            )

    def relay(self, k):
        at, part, source, push = self.rows(k), self.part, self.source, self.wire.push
        up, down = {"context": self.nxt}, {"context": self.prv}
        self.relays[k][0].wait_recv()
        self.early_prv[at, :] = (
            self.early_prv[at, :].astype(f32) + part[self.win(self.nxt, 0, k)].astype(f32)
        ).astype(bf16)
        one = push(self.early_prv.at[at, :], self.from_prv.at[1, at, :], up)
        self.relays[k][1].wait_recv()
        self.early_nxt[at, :] = (
            self.early_nxt[at, :].astype(f32) + part[self.win(self.prv, 1, k)].astype(f32)
        ).astype(bf16)
        two = push(self.early_nxt.at[at, :], self.from_nxt.at[1, at, :], down)
        self.mores[k] = (one, two)
        self.plains[k] = (
            push(source.at[self.win(self.nxt, 1, k)], self.from_prv.at[0, at, :], up),
            push(source.at[self.win(self.prv, 0, k)], self.from_nxt.at[0, at, :], down),
        )

    def exchange(self, k):
        at = self.rows(k)
        self.mores[k][0].wait_recv()
        self.plains[k][1].wait_recv()
        self.mine[0, at, :] = (
            self.part[self.win(self.c, 0, k)].astype(f32)
            + self.from_nxt[0, at, :].astype(f32)
            + self.from_prv[1, at, :].astype(f32)
        ).astype(bf16)
        self.mores[k][1].wait_recv()
        self.plains[k][0].wait_recv()
        self.mine[1, at, :] = (
            self.part[self.win(self.c, 1, k)].astype(f32)
            + self.from_prv[0, at, :].astype(f32)
            + self.from_nxt[1, at, :].astype(f32)
        ).astype(bf16)
        to = {"tensor": 1 - lax.axis_index("tensor")}
        self.swaps[k] = self.wire.push(self.mine.at[:, at, :], self.other.at[:, at, :], to)

    def totals(self, k):
        self.swaps[k].wait_recv()
        at = self.rows(k)
        return [
            (
                pl.ds(second * self.half + k * self.size, self.size),
                self.mine[second, at, :].astype(f32) + self.other[second, at, :].astype(f32),
            )
            for second in range(2)
        ]


class ShardSum:
    def __init__(self, wire, both, came, from_down, from_up, pair, last, ranges):
        self.wire, self.both, self.came = wire, both, came
        self.from_down, self.from_up = from_down, from_up
        self.pair, self.last, self.ranges = pair, last, ranges
        self.shard = both.shape[2]
        self.half = self.shard // 2
        self.f, self.core, self.far, self.up, self.down = along_fsdp()
        self.side = lax.rem(lax.div(self.f, 2), 2)
        self.mine = lax.rem(self.f, 2)
        self.z = lax.div(self.f, 4)
        self.cores, self.plain, self.relay, self.more, self.cross = {}, {}, {}, {}, {}

    def cols(self, k):
        return pl.ds(*self.ranges[k])

    def block_cols(self, rel):
        size = 4 * self.shard
        return pl.ds(pl.multiple_of(lax.rem(self.z + rel, 4) * size, 128), size)

    def multiply(self, k, rel, left, right):
        tile = lax.dot_general(
            left, right, (((0,), (0,)), ((), ())), preferred_element_type=f32
        ).astype(bf16)
        cols = self.cols(k)
        for side in range(2):
            for core in range(2):
                lo = (2 * side + core) * self.shard
                place = lax.rem(core + self.mine, 2)
                self.both[place, 2 * rel + side, :, cols] = tile[lo : lo + self.shard]
        self.cores[k, rel] = self.wire.push(
            self.both.at[1, pl.ds(2 * rel, 2), :, cols],
            self.came.at[pl.ds(2 * rel, 2), :, cols],
            {"fsdp": self.core},
        )

    def block(self, rel, second, k):
        return pl.ds(2 * rel, 2), pl.ds(second * self.half, self.half), self.cols(k)

    def add_core(self, k, rel):
        self.cores[k, rel].wait_recv()
        at = pl.ds(2 * rel, 2), slice(None), self.cols(k)
        mine = (0,) + at
        self.both[mine] = (self.both[mine].astype(f32) + self.came[at].astype(f32)).astype(bf16)

    def start(self, k):
        got, cols, push = self.both.at[0], self.cols(k), self.wire.push
        up, down = {"fsdp": self.up}, {"fsdp": self.down}
        self.add_core(k, 2)
        self.relay[k] = (
            push(got.at[self.block(2, 0, k)], self.from_down.at[0, :, :, cols], up),
            push(got.at[self.block(2, 1, k)], self.from_up.at[0, :, :, cols], down),
        )
        self.add_core(k, 1)
        self.add_core(k, 3)
        self.add_core(k, 0)

    def relays(self, k):
        got, cols, push = self.both.at[0], self.cols(k), self.wire.push
        self.relay[k][0].wait_recv()
        at = (0, slice(None), slice(None), cols)
        self.from_down[at] = (
            self.from_down[at].astype(f32) + got[self.block(1, 0, k)].astype(f32)
        ).astype(bf16)
        one = push(self.from_down.at[at], self.from_down.at[2, :, :, cols], {"fsdp": self.up})
        self.relay[k][1].wait_recv()
        self.from_up[at] = (
            self.from_up[at].astype(f32) + got[self.block(3, 1, k)].astype(f32)
        ).astype(bf16)
        two = push(self.from_up.at[at], self.from_up.at[2, :, :, cols], {"fsdp": self.down})
        self.more[k] = (one, two)
        self.plain[k] = (
            push(got.at[self.block(1, 1, k)], self.from_down.at[1, :, :, cols], {"fsdp": self.up}),
            push(got.at[self.block(3, 0, k)], self.from_up.at[1, :, :, cols], {"fsdp": self.down}),
        )

    def across(self, k):
        got, cols, half = self.both.at[0], self.cols(k), self.half
        self.more[k][0].wait_recv()
        self.plain[k][1].wait_recv()
        self.pair[:, pl.ds(0, half), cols] = (
            got[self.block(0, 0, k)].astype(f32)
            + self.from_down[2, :, :, cols].astype(f32)
            + self.from_up[1, :, :, cols].astype(f32)
        ).astype(bf16)
        self.more[k][1].wait_recv()
        self.plain[k][0].wait_recv()
        self.pair[:, pl.ds(half, half), cols] = (
            got[self.block(0, 1, k)].astype(f32)
            + self.from_down[1, :, :, cols].astype(f32)
            + self.from_up[2, :, :, cols].astype(f32)
        ).astype(bf16)
        self.cross[k] = self.wire.push(
            self.pair.at[1 - self.side, :, cols], self.last.at[:, cols], {"fsdp": self.far}
        )

    def total(self, k):
        cols = self.cols(k)
        self.cross[k].wait_recv()
        return self.pair[self.side, :, cols].astype(f32) + self.last[:, cols].astype(f32)


def row_scratch(rows, width):
    return [pltpu.VMEM((2, rows // 2, width), bf16)] * 6


def everyone_near():
    _, core, far, up, down = along_fsdp()
    _, nxt, prv, _ = along_context()
    return [{"fsdp": i} for i in (core, far, up, down)] + [
        {"context": nxt}, {"context": prv}, {"tensor": 1 - lax.axis_index("tensor")}
    ]


def half_turn(x):
    return pltpu.roll(x, HD // 2, 1)


def signal(sem, to):
    pl.semaphore_signal(sem, inc=1, device_id=to, device_id_type=MESH)


ORDER = (2, 1, 3, 0)
SMALL = (8, 512)


def layer_back_kernel(
    normed_hbm, dy_hbm, both_hbm, hidden_hbm, first_hbm, second_hbm,
    out_hbm, lin_hbm, probs_hbm,
    middle_ref, dy_ref, gain_ref, mixed_ref, query_ref, kv_ref,
    normed_one_ref, tokens_ref, cos_ref, sin_ref,
    result_ref, gt_ref, small_ref, attn_ref, mlp_hbm,
    part, early_one, early_two, from_prv, from_nxt, mine, other,
    left, right, both, came, from_down, from_up, pair, last, shard_out,
    probs, d_probs, d_low, low, d_branch, d_mixed, acc_k, acc_v, kv_send, kv_came,
    d_lin, swap_mine, swap_other, attn_own, attn_came, small_own, small_came,
    send, recv, local, free,
):
    wire, loads = Wire(send, recv), Loads(local)
    rows, width = middle_ref.shape
    q_cols, kv_cols = mixed_ref.shape[1], kv_ref.shape[2]
    heads = q_cols // HD
    span = hidden_hbm.shape[1]
    scale = HD ** (-0.5)
    c, nxt, prv, cf = along_context()
    f, core, far, up, down = along_fsdp()
    opposite = lax.rem(f + 8, lax.axis_size("fsdp"))
    C = lambda i: {"context": i}
    F = lambda i: {"fsdp": i}
    T = {"tensor": 1 - lax.axis_index("tensor")}

    def keep_small(at, values):
        for k in range(values.shape[1] // SMALL[1]):
            small_own[pl.ds(at + k, 1), :] = values[:, k * SMALL[1] : (k + 1) * SMALL[1]]

    load_part = loads.start(first_hbm, part)
    load_left = loads.start(normed_hbm, left)
    load_r0 = loads.start(both_hbm.at[:, pl.ds(0, span)], right.at[0])
    load_r1 = loads.start(both_hbm.at[:, pl.ds(span, span)], right.at[1])
    meet(everyone_near() + [C(cf), F(opposite)])

    one, two = (
        RowSum(wire, part, source, (early.at[0], early.at[1]), from_prv, from_nxt, mine, other, 4)
        for source, early in ((first_hbm, early_one), (second_hbm, early_two))
    )
    mlp = ShardSum(wire, both, came, from_down, from_up, pair, last, [(k * span, span) for k in range(3)])
    attn = ShardSum(
        wire, both, came, from_down, from_up, pair, last,
        [(0, q_cols), (q_cols, q_cols), (2 * q_cols, 2 * kv_cols)],
    )
    one.start()

    def weights(k, rel, slot):
        mlp.multiply(k, rel, left[:, mlp.block_cols(rel)], right[slot])

    load_left.wait()
    load_r0.wait()
    for rel in ORDER:
        weights(0, rel, 0)
    load_r0 = loads.start(hidden_hbm, right.at[0])
    mlp.start(0)
    load_part.wait()
    one.relay(0)
    load_r1.wait()
    weights(1, 2, 1)
    one.relay(1)
    weights(1, 1, 1)
    one.relay(2)
    weights(1, 3, 1)
    one.relay(3)
    two.start()
    weights(1, 0, 1)
    load_left = loads.start(dy_hbm, left)
    mlp.start(1)
    mlp.relays(0)
    load_r0.wait()
    load_left.wait()
    weights(2, 2, 0)
    one.exchange(0)
    weights(2, 1, 0)
    weights(2, 3, 0)
    weights(2, 0, 0)
    one.exchange(1)
    mlp.start(2)
    signal(free.at[0], F(core))
    deep = left.shape[0]
    rest = width - deep
    load_out = (
        loads.start(out_hbm.at[pl.ds(0, deep)], left.at[:, pl.ds(0, q_cols)]),
        loads.start(out_hbm.at[pl.ds(deep, rest)], left.at[pl.ds(0, rest), pl.ds(q_cols, q_cols)]),
    )
    lin_cols = lin_hbm.shape[1]
    load_lin = (
        loads.start(lin_hbm.at[pl.ds(0, deep)], right.at[0, :, pl.ds(0, lin_cols)]),
        loads.start(lin_hbm.at[pl.ds(deep, rest)], right.at[1, pl.ds(0, rest), pl.ds(0, lin_cols)]),
    )
    load_probs = {h: loads.start(probs_hbm.at[h], probs.at[h % 2]) for h in range(2)}
    mlp.relays(1)
    one.exchange(2)

    gain_two = gain_ref[pl.ds(1, 1), :]
    gain_grad = jnp.zeros((1, width), f32)
    for k in range(4):
        if k == 1:
            one.exchange(3)
            for j in range(4):
                wire.sent(*one.relays[j], *one.plains[j], *one.mores[j])
            signal(free.at[1], C(nxt))
            signal(free.at[2], C(prv))
            load_part = loads.start(second_hbm, part)
        if k == 3:
            load_part.wait()
            pl.semaphore_wait(free.at[1], 1)
            pl.semaphore_wait(free.at[2], 1)
            mlp.across(0)
        for at, grad in one.totals(k):
            mid = middle_ref[at, :]
            r = lax.rsqrt(jnp.mean(mid * mid, axis=-1, keepdims=True) + EPSILON)
            gain_grad += jnp.sum(grad * mid * r, axis=0, keepdims=True)
            scaled = grad * gain_two
            back = jnp.mean(scaled * mid, axis=-1, keepdims=True)
            value = dy_ref[at, :].astype(f32) + r * scaled - mid * (r * r * r * back)
            gt_ref[at, :] = value
            d_branch[at, :] = value.astype(bf16)
    wire.sent(*one.swaps.values())
    signal(free.at[3], T)
    keep_small(3, gain_grad)

    for copy in load_out:
        copy.wait()
    d_mixed[...] = (
        jnp.dot(d_branch[:, pl.ds(0, deep)], left[:, pl.ds(0, q_cols)], preferred_element_type=f32)
        + jnp.dot(
            d_branch[:, pl.ds(deep, rest)], left[pl.ds(0, rest), pl.ds(q_cols, q_cols)],
            preferred_element_type=f32,
        )
    ).astype(bf16)
    lane = lax.broadcasted_iota(jnp.int32, (1, HD), 1)
    sign = jnp.where(lane < HD // 2, 1.0, -1.0).astype(f32)

    def turn_back(w):
        return w * cos_ref[...] + half_turn(w * sin_ref[...]) * sign

    nt = (((1,), (1,)), ((), ()))
    tn = (((0,), (0,)), ((), ()))

    def head(h):
        cols = pl.ds(h * HD, HD)
        load_probs[h].wait()
        dm = d_mixed[:, cols]
        d_probs[...] = lax.dot_general(dm, kv_ref[1], nt, preferred_element_type=f32)
        for at in range(0, rows, 32):
            at = pl.ds(at, 32)
            p, dp = probs[h % 2, at, :], d_probs[at, :]
            inner = jnp.sum(p * dp, axis=-1, keepdims=True)
            d_low[at, :] = (p * (dp - inner)).astype(bf16)
            low[at, :] = p.astype(bf16)
        ds = d_low[...]
        dq = jnp.dot(ds, kv_ref[0], preferred_element_type=f32) * scale
        d_lin[:, cols] = turn_back(dq).astype(bf16)
        dk = lax.dot_general(ds, query_ref[:, cols], tn, preferred_element_type=f32)
        dv = lax.dot_general(low[...], dm, tn, preferred_element_type=f32)
        if h == 0:
            acc_k[...] = dk
            acc_v[...] = dv
        else:
            acc_k[...] += dk
            acc_v[...] += dv
        if h + 2 < heads:
            load_probs[h + 2] = loads.start(probs_hbm.at[h + 2], probs.at[h % 2])

    def leave(k):
        wire.sent(*[mlp.cores[k, rel] for rel in ORDER], *mlp.relay[k], *mlp.plain[k], *mlp.more[k])

    mlp.relays(2)
    head(0)
    two.relay(0)
    leave(0)
    signal(free.at[4], F(up))
    signal(free.at[5], F(down))
    head(1)
    two.relay(1)
    head(2)
    two.relay(2)
    head(3)
    head(4)
    pl.semaphore_wait(free.at[3], 1)
    two.exchange(0)
    head(5)

    for k in range(4):
        kv_send[k, 0] = acc_k[pl.ds(k * rows, rows), :].astype(bf16)
        kv_send[k, 1] = acc_v[pl.ds(k * rows, rows), :].astype(bf16)
    kv = [
        wire.push(kv_send.at[nxt], kv_came.at[0], C(nxt)),
        wire.push(kv_send.at[prv], kv_came.at[1], C(prv)),
        wire.push(kv_send.at[cf], kv_came.at[2], C(cf)),
    ]
    two.relay(3)
    mlp.across(1)
    leave(1)
    signal(free.at[7], F(up))
    signal(free.at[8], F(down))
    pl.semaphore_wait(free.at[0], 1)
    for rel in ORDER:
        attn.multiply(0, rel, d_branch[:, attn.block_cols(rel)], mixed_ref[...])
    pl.semaphore_wait(free.at[4], 1)
    pl.semaphore_wait(free.at[5], 1)
    attn.start(0)
    for rel in ORDER:
        attn.multiply(1, rel, normed_one_ref[:, attn.block_cols(rel)], d_lin[:, pl.ds(0, q_cols)])
    two.exchange(1)
    mlp.across(2)
    leave(2)
    pl.semaphore_wait(free.at[7], 1)
    pl.semaphore_wait(free.at[8], 1)
    attn.start(1)
    for copy in kv:
        copy.wait_recv()
    d_key = acc_k[pl.ds(pl.multiple_of(c * rows, 8), rows), :]
    d_value = acc_v[pl.ds(pl.multiple_of(c * rows, 8), rows), :]
    for k in range(3):
        d_key += kv_came[k, 0].astype(f32)
        d_value += kv_came[k, 1].astype(f32)
    d_lin[:, pl.ds(q_cols, kv_cols)] = turn_back(d_key * scale).astype(bf16)
    d_lin[:, pl.ds(q_cols + kv_cols, kv_cols)] = d_value.astype(bf16)
    for copy in load_lin:
        copy.wait()
    swap_mine[:, pl.ds(0, deep)] = lax.dot_general(
        d_lin[...], right[0, :, pl.ds(0, lin_cols)], nt, preferred_element_type=f32
    ).astype(bf16)
    swap_mine[:, pl.ds(deep, rest)] = lax.dot_general(
        d_lin[...], right[1, pl.ds(0, rest), pl.ds(0, lin_cols)], nt, preferred_element_type=f32
    ).astype(bf16)
    sizes = 64
    gain_grad = jnp.zeros((1, width), f32)
    for k in range(rows // sizes):
        at = pl.ds(k * sizes, sizes)
        mid = tokens_ref[at, :].astype(f32)
        r = lax.rsqrt(jnp.mean(mid * mid, axis=-1, keepdims=True) + EPSILON)
        gain_grad += jnp.sum(swap_mine[at, :].astype(f32) * mid * r, axis=0, keepdims=True)
    keep_small(0, gain_grad)
    keep_small(6, jnp.sum(d_lin[...].astype(f32), axis=0, keepdims=True))
    small_step = wire.push(small_own, small_came.at[0], T)
    swaps = []

    def swap(k):
        at = pl.ds(k * sizes, sizes)
        swaps.append(wire.push(swap_mine.at[at, :], swap_other.at[at, :], T))

    for k in range(3):
        swap(k)
    attn.relays(0)
    for k in range(3):
        shard_out[:, mlp.cols(k)] = mlp.total(k).astype(bf16)
    signal(free.at[6], F(far))
    for k in range(3):
        wire.sent(mlp.cross[k])
    spread = [
        wire.push(shard_out, mlp_hbm.at[c], C(nxt)),
        wire.push(shard_out, mlp_hbm.at[c], C(prv)),
    ]
    keep = loads.start(shard_out, mlp_hbm.at[c])
    for rel in ORDER:
        attn.multiply(
            2, rel, normed_one_ref[:, attn.block_cols(rel)], d_lin[:, pl.ds(q_cols, 2 * kv_cols)]
        )
    small_step.wait_recv()
    gain_rows = lax.broadcasted_iota(jnp.int32, SMALL, 0) < 3
    small_came[1] = small_own[...] + jnp.where(gain_rows, small_came[0], 0.0)
    small_step = wire.push(small_came.at[1], small_came.at[2], F(core))
    attn.start(2)
    pl.semaphore_wait(free.at[6], 1)
    attn.across(0)
    swap(3)
    small_step.wait_recv()
    small_came[3] = small_came[1] + small_came[2]
    small_steps = [
        wire.push(small_came.at[3], small_came.at[4 + k], F(to)) for k, to in enumerate((up, down, opposite))
    ]
    attn.relays(1)
    attn.relays(2)
    for step in small_steps:
        step.wait_recv()
    small_came[7] = (small_came[3] + small_came[6]) + (small_came[4] + small_came[5])
    small_step = wire.push(small_came.at[7], small_came.at[8], F(far))

    half = shard_out.shape[0] // 2
    near, rest_of = {}, {}

    def to_ranks(k):
        cols = attn.cols(k)
        attn_own[:, cols] = attn.total(k).astype(bf16)
        w = attn_own.at[:, cols]
        near[k] = (
            wire.push(w, attn_came.at[0, :, cols], C(nxt)),
            wire.push(w, attn_came.at[1, :, cols], C(prv)),
        )

    def onward(k):
        cols, first, second = attn.cols(k), pl.ds(0, half), pl.ds(half, half)
        near[k][0].wait_recv()
        near[k][1].wait_recv()
        rest_of[k] = (
            wire.push(attn_came.at[0, first, cols], attn_came.at[2, first, cols], C(nxt)),
            wire.push(attn_came.at[1, second, cols], attn_came.at[2, second, cols], C(prv)),
        )

    attn.across(1)
    attn.across(2)
    two.exchange(2)
    two.exchange(3)

    gain_one = gain_ref[pl.ds(0, 1), :]
    for k in range(rows // sizes):
        swaps[k].wait_recv()
        at = pl.ds(k * sizes, sizes)
        grad = swap_mine[at, :].astype(f32) + swap_other[at, :].astype(f32)
        mid = tokens_ref[at, :].astype(f32)
        r = lax.rsqrt(jnp.mean(mid * mid, axis=-1, keepdims=True) + EPSILON)
        scaled = grad * gain_one
        back = jnp.mean(scaled * mid, axis=-1, keepdims=True)
        gt_ref[at, :] = gt_ref[at, :] + r * scaled - mid * (r * r * r * back)
    to_ranks(0)
    small_step.wait_recv()
    small_came[9] = small_came[7] + small_came[8]
    spread[0].wait_recv()
    w = mlp_hbm.at[prv, pl.ds(0, half)]
    spread.append(wire.push(w, w, C(nxt)))
    spread[1].wait_recv()
    w = mlp_hbm.at[nxt, pl.ds(half, half)]
    spread.append(wire.push(w, w, C(prv)))
    to_ranks(1)
    to_ranks(2)
    small_steps = [
        wire.push(small_came.at[9], small_came.at[10 + k], C(to)) for k, to in enumerate((nxt, prv, cf))
    ]
    onward(0)
    for k in range(4):
        for at, total in two.totals(k):
            result_ref[at, :] = (middle_ref[at, :] + total).astype(bf16)
    onward(1)
    onward(2)
    for k in range(3):
        cols = attn.cols(k)
        rest_of[k][0].wait_recv()
        rest_of[k][1].wait_recv()
        attn_ref[:, cols] = (attn_own[:, cols].astype(f32) + attn_came[2, :, cols].astype(f32)) + (
            attn_came[0, :, cols].astype(f32) + attn_came[1, :, cols].astype(f32)
        )
    for step in small_steps:
        step.wait_recv()
    small_ref[...] = (small_came[9] + small_came[12]) + (small_came[10] + small_came[11])
    spread[2].wait_recv()
    spread[3].wait_recv()
    keep.wait()
    wire.drain()


def layer_back(hbm, near, cid=4):
    normed, dy, both, hidden, first, second, out, lin, probs = hbm
    group, width = normed.shape
    rows = group // 4
    shard, span = width // 16, hidden.shape[1]
    lin_cols = lin.shape[1]
    q_cols = out.shape[1]
    sems = 2 * 28 + 2 * (12 + 3 * 7) + 3 + 4 + 4 + 12 + 9
    return pl.pallas_call(
        layer_back_kernel,
        out_shape=(
            jax.ShapeDtypeStruct((rows, width), bf16),
            jax.ShapeDtypeStruct((rows, width), f32),
            jax.ShapeDtypeStruct(SMALL, f32),
            jax.ShapeDtypeStruct((shard, lin_cols + q_cols), f32),
            jax.ShapeDtypeStruct((4, shard, 3 * span), bf16),
        ),
        in_specs=[ANY] * len(hbm) + [VM] * len(near),
        out_specs=(VM, VM, VM, VM, ANY),
        scratch_shapes=[pltpu.VMEM((group, width), bf16)]
        + row_scratch(rows, width)
        + [
            pltpu.VMEM((group, width), bf16),
            pltpu.VMEM((2, group, span), bf16),
            pltpu.VMEM((2, 8, shard, 3 * span), bf16),
            pltpu.VMEM((8, shard, 3 * span), bf16),
            pltpu.VMEM((3, 2, shard // 2, 3 * span), bf16),
            pltpu.VMEM((3, 2, shard // 2, 3 * span), bf16),
            pltpu.VMEM((2, shard, 3 * span), bf16),
            pltpu.VMEM((shard, 3 * span), bf16),
            pltpu.VMEM((shard, 3 * span), bf16),
            pltpu.VMEM((2, rows, group), f32),
            pltpu.VMEM((rows, group), f32),
            pltpu.VMEM((rows, group), bf16),
            pltpu.VMEM((rows, group), bf16),
            pltpu.VMEM((rows, width), bf16),
            pltpu.VMEM((rows, q_cols), bf16),
            pltpu.VMEM((group, HD), f32),
            pltpu.VMEM((group, HD), f32),
            pltpu.VMEM((4, 2, rows, HD), bf16),
            pltpu.VMEM((3, 2, rows, HD), bf16),
            pltpu.VMEM((rows, lin_cols), bf16),
            pltpu.VMEM((rows, width), bf16),
            pltpu.VMEM((rows, width), bf16),
            pltpu.VMEM((shard, lin_cols + q_cols), bf16),
            pltpu.VMEM((3, shard, lin_cols + q_cols), bf16),
            pltpu.VMEM(SMALL, f32),
            pltpu.VMEM((13,) + SMALL, f32),
            pltpu.SemaphoreType.DMA((sems,)),
            pltpu.SemaphoreType.DMA((sems,)),
            pltpu.SemaphoreType.DMA((18,)),
            pltpu.SemaphoreType.REGULAR((9,)),
        ],
        compiler_params=pltpu.CompilerParams(
            collective_id=cid, has_side_effects=True, vmem_limit_bytes=63 << 20
        ),
        name="layer_back",
    )(*hbm, *near)


class Blocks:
    def __init__(self, wire, ref, shard, cols=None):
        self.wire, self.ref, self.shard, self.half = wire, ref, shard, shard // 2
        self.cols = slice(None) if cols is None else cols
        self.f, self.core, self.far, self.up, self.down = along_fsdp()
        n = lax.axis_size("fsdp")
        self.opposite = lax.rem(self.f + 8, n)
        self.sibling = []

    def pair(self, i):
        return i + 2 - 4 * lax.rem(lax.div(i, 2), 2)

    def win(self, owner, lo=0, size=None):
        at = pl.multiple_of(owner * self.shard + lo, 16)
        return self.ref.at[pl.ds(at, size or self.shard), self.cols]

    def push(self, w, to):
        return self.wire.push(w, w, {"fsdp": to})

    def to_core(self, w):
        self.sibling.append(self.push(w, self.core))

    def ex(self):
        w = self.win(self.f)
        self.from_far = self.push(w, self.far)
        self.to_core(w)

    def ez(self):
        w = self.win(self.f)
        self.from_down = self.push(w, self.up)
        self.from_up = self.push(w, self.down)

    def e0(self):
        self.ex()
        self.ez()

    def e1(self):
        self.from_far.wait_recv()
        w = self.win(self.far)
        self.far_down = self.push(w, self.up)
        self.far_up = self.push(w, self.down)
        self.to_core(w)

    def relay(self, below, above, one, two):
        one.wait_recv()
        first = self.push(self.win(below, 0, self.half), self.up)
        self.to_core(self.win(below))
        two.wait_recv()
        second = self.push(self.win(above, self.half, self.half), self.down)
        self.to_core(self.win(above))
        return first, second

    def e2(self):
        self.last = self.relay(self.down, self.up, self.from_down, self.from_up)

    def e3(self):
        self.last += self.relay(self.pair(self.down), self.pair(self.up), self.far_down, self.far_up)

    def e4(self):
        for k, copy in enumerate(self.last):
            copy.wait_recv()
            owner = self.opposite if k < 2 else self.pair(self.opposite)
            self.to_core(self.win(owner, self.half * (k % 2), self.half))

    def end(self):
        for copy in self.sibling:
            copy.wait_recv()


def rotary(angle):
    turns = jnp.floor(angle * (0.5 / math.pi) + 0.5)
    x = (angle - turns * 6.28125) - turns * (2.0 * math.pi - 6.28125)
    square = x * x
    cosine, sine = jnp.zeros_like(x), jnp.zeros_like(x)
    for k in range(9, -1, -1):
        cosine = cosine * square + (-1.0) ** k / math.factorial(2 * k)
        sine = sine * square + (-1.0) ** k / math.factorial(2 * k + 1)
    return cosine, sine * x


def layer_front_kernel(
    query_hbm, key_hbm, value_hbm, out_hbm, gate_hbm, lift_hbm, down_hbm, dy_hbm,
    query_bias, key_bias, value_bias, first_gain, second_gain,
    tokens_ref, inverse_ref, lengths_ref,
    middle_ref, normed_one_ref, mixed_ref, q_ref, kv_ref, gain_ref, cos_ref, sin_ref,
    normed_hbm, dyg_hbm, lin_hbm, outf_hbm, probs_hbm,
    both_hbm, hidden_hbm, first_hbm, second_hbm,
    gains, wl, wo, wm, dyg, normed, mask, probs, part, other, d_hidden,
    low, pair, d_both, hidden, first, second,
    send, recv, local,
):
    wire, loads = Wire(send, recv), Loads(local)
    rows, width = tokens_ref.shape
    group = dyg.shape[0]
    shard, q_cols = query_hbm.shape
    kv_cols = key_hbm.shape[1]
    heads = q_cols // HD
    hidden_cols = gate_hbm.shape[1]
    span = hidden.shape[1]
    overlap = 4 * span - hidden_cols
    scale = HD ** (-0.5)
    c, nxt, prv, cf = along_context()
    f, core, far, up, down = along_fsdp()
    C = lambda i: {"context": i}
    T = {"tensor": 1 - lax.axis_index("tensor")}
    mine = pl.ds(pl.multiple_of(f * shard, 16), shard)
    group_rows = lambda owner, lo=0, size=rows: pl.ds(pl.multiple_of(owner * rows + lo, 16), size)
    start = pl.multiple_of(c * span - lax.div(c, 3) * overlap, 128)

    own = [
        loads.start(query_hbm, wl.at[mine, pl.ds(0, q_cols)]),
        loads.start(key_hbm, wl.at[mine, pl.ds(q_cols, kv_cols)]),
        loads.start(value_hbm, wl.at[mine, pl.ds(q_cols + kv_cols, kv_cols)]),
        loads.start(out_hbm, wo.at[mine, :]),
        loads.start(dy_hbm, dyg.at[group_rows(c), :]),
    ]
    sizes_of = (640, span - 640)
    offsets = (0, 640)
    big = [
        [
            loads.start(
                w.at[:, pl.ds(start + off, n)], wm.at[mine, pl.ds(3 * off + k * n, n)]
            )
            for k, w in enumerate((down_hbm, gate_hbm, lift_hbm))
        ]
        for off, n in zip(offsets, sizes_of)
    ]
    tile = gains.shape[0] * shard // width
    gains[pl.ds(pl.multiple_of(f * tile, 16), tile), :] = jnp.zeros((tile, HD), f32)
    gains[pl.ds(pl.multiple_of(f * tile, 16), 1), pl.ds(0, shard)] = first_gain[...].astype(f32)
    gains[pl.ds(pl.multiple_of(f * tile, 16) + 1, 1), pl.ds(0, shard)] = second_gain[...].astype(f32)
    meet(everyone_near() + [C(cf)])
    G = Blocks(wire, gains, tile)
    Q = Blocks(wire, wl, shard)
    O = Blocks(wire, wo, shard)
    A, B = (Blocks(wire, wm, shard, pl.ds(3 * off, 3 * n)) for off, n in zip(offsets, sizes_of))

    G.e0()
    for copy in own:
        copy.wait()
    Q.e0()
    w = dyg.at[group_rows(c), :]
    dy_copies = [wire.push(w, w, C(nxt)), wire.push(w, w, C(prv))]
    G.e1()
    O.e0()
    for copy in big[0]:
        copy.wait()
    A.ex()
    here = c * rows + lax.broadcasted_iota(jnp.int32, (rows, 1), 0)
    there = lax.broadcasted_iota(jnp.int32, (1, group), 1)
    end, position = jnp.zeros((1, 1), jnp.int32), here
    mine_of, its = jnp.zeros((rows, 1), jnp.int32), jnp.zeros((1, group), jnp.int32)
    for k in range(lengths_ref.shape[1]):
        end = end + lengths_ref[:, pl.ds(k, 1)]
        mine_of = mine_of + jnp.where(here >= end, 1, 0)
        position = jnp.where(here >= end, here - end, position)
        its = its + jnp.where(there >= end, 1, 0)
    cos_ref[...], sin_ref[...] = rotary(position.astype(f32) * inverse_ref[...])
    allowed = (mine_of == its) & (there <= here)
    mask[...] = jnp.where(allowed, 0.0, -1e30).astype(f32)
    G.e2()
    G.e3()
    Q.e1()
    G.e4()
    G.end()
    for k in range(2):
        gain_ref[pl.ds(k, 1), :] = jnp.concatenate(
            [gains[pl.ds(i * tile + k, 1), :][:, :shard] for i in range(width // shard)], axis=1
        )
    sizes = 64
    for at in range(0, rows, sizes):
        at = pl.ds(at, sizes)
        x = tokens_ref[at, :].astype(f32)
        r = lax.rsqrt(jnp.mean(x * x, axis=-1, keepdims=True) + EPSILON)
        normed_one_ref[at, :] = (x * r * gain_ref[pl.ds(0, 1), :]).astype(bf16)
    Q.e2()
    Q.e3()
    O.e1()
    A.ez()
    Q.e4()
    for copy in big[1]:
        copy.wait()
    B.ex()
    Q.end()

    sign = jnp.where(lax.broadcasted_iota(jnp.int32, (1, HD), 1) < HD // 2, -1.0, 1.0).astype(f32)

    def turned(v):
        return v * cos_ref[...] + half_turn(v) * sign * sin_ref[...]

    def linear(head, biases):
        both = jnp.dot(normed_one_ref[...], wl[:, pl.ds(head * HD, 2 * HD)], preferred_element_type=f32)
        return [both[:, k * HD : (k + 1) * HD] + bias.astype(f32) for k, bias in enumerate(biases)]

    key, value = linear(heads, (key_bias[...], value_bias[...]))
    kv_ref[0, group_rows(c), :] = turned(key).astype(bf16)
    kv_ref[1, group_rows(c), :] = value.astype(bf16)
    kv = []
    for k in range(2):
        w = kv_ref.at[k, group_rows(c), :]
        kv.append([wire.push(w, w, C(i)) for i in (cf, nxt, prv)])
    for h in range(0, heads, 2):
        biases = [query_bias[:, pl.ds((h + k) * HD, HD)] for k in range(2)]
        for k, lin in enumerate(linear(h, biases)):
            q_ref[:, pl.ds((h + k) * HD, HD)] = turned(lin).astype(bf16)
    O.e2()
    O.e3()
    A.e1()
    keep = [loads.start(wl, lin_hbm)]
    half = rows // 2
    dy_copies[0].wait_recv()
    w = dyg.at[group_rows(prv, 0, half), :]
    dy_copies.append(wire.push(w, w, C(nxt)))
    dy_copies[1].wait_recv()
    w = dyg.at[group_rows(nxt, half, half), :]
    dy_copies.append(wire.push(w, w, C(prv)))
    for copy in kv[0]:
        copy.wait_recv()

    nt = (((1,), (1,)), ((), ()))
    probs_out = {}

    def head(h):
        cols = pl.ds(h * HD, HD)
        if h >= 2:
            probs_out[h - 2].wait()
        probs[h % 2] = lax.dot_general(q_ref[:, cols], kv_ref[0], nt, preferred_element_type=f32)
        for at in range(0, rows, 32):
            at = pl.ds(at, 32)
            s = probs[h % 2, at, :] * scale + mask[at, :]
            e = jnp.exp(s - jnp.max(s, axis=-1, keepdims=True))
            p = e * (1.0 / jnp.sum(e, axis=-1, keepdims=True))
            probs[h % 2, at, :] = p
            low[at, :] = p.astype(bf16)
        probs_out[h] = loads.start(probs.at[h % 2], probs_hbm.at[h])
        if h == 0:
            for copy in kv[1]:
                copy.wait_recv()
        mixed_ref[:, cols] = jnp.dot(low[...], kv_ref[1], preferred_element_type=f32).astype(bf16)

    for h in range(heads):
        head(h)
    A.e2()
    O.e4()
    probs_out[heads - 2].wait()
    probs_out[heads - 1].wait()
    O.end()
    sizes = 32
    chunks = rows // sizes
    swaps = []
    for k in range(chunks // 2):
        at = pl.ds(2 * k * sizes, 2 * sizes)
        part[at, :] = lax.dot_general(mixed_ref[at, :], wo[...], nt, preferred_element_type=f32).astype(bf16)
        for j in range(2):
            at = pl.ds((2 * k + j) * sizes, sizes)
            swaps.append(wire.push(part.at[at, :], other.at[at, :], T))
    keep.append(loads.start(wo, outf_hbm))
    B.ez()
    for copy in dy_copies[2:]:
        copy.wait_recv()
    keep.append(loads.start(dyg, dyg_hbm))

    from_prv, from_nxt, last = {}, {}, []
    cut = sizes // 2

    def forward(k):
        from_prv[k].wait_recv()
        w = normed.at[group_rows(prv, k * sizes, cut), :]
        last.append(wire.push(w, w, C(nxt)))
        from_nxt[k].wait_recv()
        w = normed.at[group_rows(nxt, k * sizes + cut, cut), :]
        last.append(wire.push(w, w, C(prv)))

    for k in range(chunks):
        at = pl.ds(k * sizes, sizes)
        swaps[k].wait_recv()
        mid = tokens_ref[at, :].astype(f32) + (part[at, :].astype(f32) + other[at, :].astype(f32))
        middle_ref[at, :] = mid
        r = lax.rsqrt(jnp.mean(mid * mid, axis=-1, keepdims=True) + EPSILON)
        normed[group_rows(c, k * sizes, sizes), :] = (mid * r * gain_ref[pl.ds(1, 1), :]).astype(bf16)
        w = normed.at[group_rows(c, k * sizes, sizes), :]
        from_prv[k] = wire.push(w, w, C(nxt))
        from_nxt[k] = wire.push(w, w, C(prv))
        if k == 1:
            A.e3()
            B.e1()
    forward(0)
    A.e4()
    B.e2()
    forward(1)
    forward(2)
    A.end()

    skip = lax.div(c, 3) * overlap

    def feed(owner, piece):
        at = group_rows(owner)
        off, n = offsets[piece], sizes_of[piece]
        down_at, wide = pl.ds(3 * off, n), pl.ds(3 * off + n, 2 * n)
        hidden_at, both_at = pl.ds(off, n), pl.ds(2 * off, 2 * n)
        pair[:, pl.ds(0, 2 * n)] = jnp.dot(normed[at, :], wm[:, wide], preferred_element_type=f32)
        d_hidden[:, pl.ds(0, n)] = jnp.dot(dyg[at, :], wm[:, down_at], preferred_element_type=f32)
        step = 32
        for k in range(0, rows, step):
            here, rows_here = pl.ds(k, step), group_rows(owner, k, step)
            gate, lift = pair[here, pl.ds(0, n)], pair[here, pl.ds(n, n)]
            dh = d_hidden[here, pl.ds(0, n)]
            sig = 0.5 * jnp.tanh(0.5 * gate) + 0.5
            swish = gate * sig
            up_part = swish * lift
            if piece == 0:
                live = lax.broadcasted_iota(jnp.int32, (1, n), 1) >= skip
                dh = jnp.where(live, dh, 0.0)
                up_part = jnp.where(live, up_part, 0.0)
            hidden[rows_here, hidden_at] = up_part.astype(bf16)
            d_both[rows_here, pl.ds(2 * off, n)] = (
                dh * lift * (sig + swish * (1.0 - sig))
            ).astype(bf16)
            d_both[rows_here, pl.ds(2 * off + n, n)] = (dh * swish).astype(bf16)
        one = lax.dot_general(d_both[at, both_at], wm[:, wide], nt, preferred_element_type=f32)
        two = lax.dot_general(hidden[at, hidden_at], wm[:, down_at], nt, preferred_element_type=f32)
        if piece:
            one += first[at, :].astype(f32)
            two += second[at, :].astype(f32)
        first[at, :] = one.astype(bf16)
        second[at, :] = two.astype(bf16)
        keep.append(loads.start(hidden.at[at, hidden_at], hidden_hbm.at[at, hidden_at]))
        for k in range(2):
            keep.append(
                loads.start(
                    d_both.at[at, pl.ds(2 * off + k * n, n)], both_hbm.at[at, pl.ds(k * span + off, n)]
                )
            )
        if piece == 1:
            for src, dst in ((first, first_hbm), (second, second_hbm)):
                keep.append(loads.start(src.at[at, :], dst.at[at, :]))

    feed(c, 0)
    for k in range(3, 6):
        forward(k)
    B.e3()
    for k in range(6, chunks):
        forward(k)
    feed(prv, 0)
    feed(nxt, 0)
    for copy in last:
        copy.wait_recv()
    keep.append(loads.start(normed, normed_hbm))
    B.e4()
    feed(cf, 0)
    B.end()
    for owner in (c, prv, nxt, cf):
        feed(owner, 1)
    for copy in keep:
        copy.wait()
    wire.drain()


def layer_front(hbm, near, span, cid=1):
    query, key, value, out, gate, lift, down, dy = hbm
    rows, width = dy.shape
    group = 4 * rows
    shard, q_cols = query.shape
    lin_cols = q_cols + 2 * key.shape[1]
    heads = q_cols // HD
    sems = 6 * 19 + 4 + 6 + 8 + 32
    S = jax.ShapeDtypeStruct
    return pl.pallas_call(
        layer_front_kernel,
        out_shape=(
            S((rows, width), f32),
            S((rows, width), bf16),
            S((rows, q_cols), bf16),
            S((rows, q_cols), bf16),
            S((2, group, HD), bf16),
            S((2, width), f32),
            S((rows, HD), f32),
            S((rows, HD), f32),
            S((group, width), bf16),
            S((group, width), bf16),
            S((width, lin_cols), bf16),
            S((width, q_cols), bf16),
            S((heads, rows, group), f32),
        )
        + (S((group, 2 * span), bf16), S((group, span), bf16))
        + (S((group, width), bf16),) * 2,
        in_specs=[ANY] * len(hbm) + [VM] * len(near),
        out_specs=(VM,) * 8 + (ANY,) * 9,
        scratch_shapes=[
            pltpu.VMEM((width // shard * 32, HD), f32),
            pltpu.VMEM((width, lin_cols), bf16),
            pltpu.VMEM((width, q_cols), bf16),
            pltpu.VMEM((width, 3 * span), bf16),
            pltpu.VMEM((group, width), bf16),
            pltpu.VMEM((group, width), bf16),
            pltpu.VMEM((rows, group), f32),
            pltpu.VMEM((2, rows, group), f32),
            pltpu.VMEM((rows, width), bf16),
            pltpu.VMEM((rows, width), bf16),
            pltpu.VMEM((rows, 640), f32),
            pltpu.VMEM((rows, group), bf16),
            pltpu.VMEM((rows, 1280), f32),
            pltpu.VMEM((group, 2 * span), bf16),
            pltpu.VMEM((group, span), bf16),
            pltpu.VMEM((group, width), bf16),
            pltpu.VMEM((group, width), bf16),
            pltpu.SemaphoreType.DMA((sems,)),
            pltpu.SemaphoreType.DMA((sems,)),
            pltpu.SemaphoreType.DMA((14 + heads + 4 + 44,)),
        ],
        compiler_params=pltpu.CompilerParams(
            collective_id=cid, has_side_effects=True, vmem_limit_bytes=63 << 20
        ),
        name="layer_front",
    )(*hbm, *near)


def on_device(
    tokens,
    cotangent,
    lengths,
    gain_attn,
    w_query,
    b_query,
    w_key,
    b_key,
    w_value,
    b_value,
    w_out,
    gain_mlp,
    w_gate,
    w_up,
    w_down,
):
    row_count, width = tokens.shape
    context_size = lax.axis_size("context")
    context_rank = lax.axis_index("context")
    fsdp_rank = lax.axis_index("fsdp")
    shard = w_query.shape[0]
    query_cols, kv_cols, hidden_cols = w_query.shape[1], w_key.shape[1], w_gate.shape[1]
    span = -(-(hidden_cols // 128) // context_size) * 128
    overlap = context_size * span - hidden_cols
    (
        middle, normed_one, mixed, query_heads, kv_group, gain_full, cosine, sine_table,
        normed_group, dy_group, lin_full, out_turned, probs,
        d_both, hidden, d_normed_part, mlp_part,
    ) = layer_front(
        (w_query, w_key, w_value, w_out.T, w_gate, w_up, w_down.T, cotangent),
        (
            b_query[None], b_key[None], b_value[None], gain_attn[None], gain_mlp[None],
            tokens, jnp.asarray(INVERSE), lengths,
        ),
        span,
    )
    result, grad_tokens, small, attn_shard, mlp_all = layer_back(
        (
            normed_group, dy_group, d_both, hidden, d_normed_part, mlp_part,
            out_turned, lin_full, probs,
        ),
        (
            middle, cotangent, gain_full, mixed, query_heads, kv_group, normed_one, tokens, cosine, sine_table,
        ),
    )

    def whole(k):
        parts = [mlp_all[i, :, k * span : (k + 1) * span] for i in range(context_size)]
        parts[-1] = parts[-1][:, overlap:]
        return jnp.concatenate(parts, axis=1).astype(f32)

    small = small.reshape(-1)
    own = lambda at: lax.dynamic_slice_in_dim(small, at + fsdp_rank * shard, shard)
    bias_total = small[2 * width :]
    at_query = query_cols
    at_key = at_query + query_cols
    at_value = at_key + kv_cols
    return (
        result,
        grad_tokens,
        own(0),
        attn_shard[:, at_query:at_key],
        bias_total[:query_cols],
        attn_shard[:, at_key:at_value],
        bias_total[query_cols : query_cols + kv_cols],
        attn_shard[:, at_value:],
        bias_total[query_cols + kv_cols :],
        attn_shard[:, :query_cols].T,
        own(width),
        whole(0),
        whole(1),
        whole(2).T,
    )


def solution(mesh):
    return jax.shard_map(
        on_device,
        mesh=mesh,
        in_specs=(
            P(("fsdp", "context"), None),
            P(("fsdp", "context"), None),
            P("fsdp", None),
            P("fsdp"),
            P("fsdp", "tensor"),
            P("tensor"),
            P("fsdp", "tensor"),
            P("tensor"),
            P("fsdp", "tensor"),
            P("tensor"),
            P("tensor", "fsdp"),
            P("fsdp"),
            P("fsdp", "tensor"),
            P("fsdp", "tensor"),
            P("tensor", "fsdp"),
        ),
        out_specs=(
            P(("fsdp", "context"), None),
            P(("fsdp", "context"), None),
            P("fsdp"),
            P("fsdp", "tensor"),
            P("tensor"),
            P("fsdp", "tensor"),
            P("tensor"),
            P("fsdp", "tensor"),
            P("tensor"),
            P("tensor", "fsdp"),
            P("fsdp"),
            P("fsdp", "tensor"),
            P("fsdp", "tensor"),
            P("tensor", "fsdp"),
        ),
        check_vma=False,
    )
```
